32 devices in a mesh: cell: 8 (over y, x, core), tm: 4 (over z).
Axes of the slice: x: 2, y: 2, z: 4, core: 2. Of those that a mesh axis runs over, the one named last changes fastest.
Arguments:
- window: float32 [8192, 8192], P('cell', 'tm'), may hold values from -0.1875 to 0.1875
- range_test: float32 [8192, 256], P('tm'), may hold values from -0.0625 to 0.0625
- co_test: float32 [256, 8192], P(None, 'cell'), may hold values from -0.0625 to 0.0625
- core_left: float32 [512, 8192], P(None, 'cell'), may hold values from -0.0625 to 0.0625
- core_right: float32 [512, 8192], P(None, 'tm'), may hold values from -0.0625 to 0.0625
Outputs:
- range_basis: float32 [8192, 256], P('cell')
- co_basis: float32 [256, 8192], P(None, 'tm')
- core: float32 [256, 256], replicated
The draws below stay inside these ranges and needn't reach their ends.
All inputs are finite; a program needn't handle non-finite values.
Results may differ from the reference program's by a relative error of at most 0.00023.
Values sent between devices are 32-bit elements; how exact they have to be, the bound alone decides.
No kernel may reach another device: no remote copies, remote signals or barrier semaphores. Data moves between devices by JAX's collectives and lax.ppermute only.
A program may use at most 128 MiB of HBM per device.

```python
import math
import jax
import jax.numpy as jnp
from jax import lax

K = 256
L = 256
S_CORE = 512
M = 8192
N = 8192


def steps_of(own_key, extent, split, least, high):
    level = 1.0
    for position, blocks in split:
        draws = jax.random.uniform(jax.random.fold_in(jax.random.fold_in(own_key, 6), position), (blocks,), jnp.float32, least / len(split), high / len(split))
        level = level * jnp.repeat(jnp.exp(draws), extent[position] // blocks).reshape((-1,) + (1,) * (len(extent) - 1 - position))
    return level


def bell_draw(own_key, dims, scale, bound, cuts=(), held_as=jnp.bfloat16):
    values = jax.random.normal(own_key, dims, jnp.float32) * scale
    if len(cuts) > 0:
        values = steps_of(own_key, dims, cuts, -0.22, 0.18) * values
    return jnp.clip(values, min=-bound, max=bound).astype(held_as)


def setup_inputs(seed: int = 0) -> dict:
    streams_of = jax.random.split(jax.random.key(seed), 6)
    window = bell_draw(streams_of[0], (M, N), (M * N // ((S_CORE - K) * (S_CORE - L))) ** -0.5, 0.1875, ((0, 8), (1, 4)), jnp.float32)
    range_test = bell_draw(streams_of[1], (N, K), N ** -0.5, 0.0625, ((0, 4),), jnp.float32)
    co_test = bell_draw(streams_of[2], (L, M), M ** -0.5, 0.0625, ((1, 8),), jnp.float32)
    core_left = bell_draw(streams_of[3], (S_CORE, M), M ** -0.5, 0.0625, ((1, 8),), jnp.float32)
    core_right = bell_draw(streams_of[4], (S_CORE, N), N ** -0.5, 0.0625, ((1, 4),), jnp.float32)
    return dict(window=window, range_test=range_test, co_test=co_test, core_left=core_left, core_right=core_right)


def reference(window, range_test, co_test, core_left, core_right):
    highest = lax.Precision.HIGHEST
    sketch_y = jnp.dot(window.astype(jnp.float32), range_test.astype(jnp.float32), precision=highest, preferred_element_type=jnp.float32)
    sketch_w = jnp.dot(co_test.astype(jnp.float32), window.astype(jnp.float32), precision=highest, preferred_element_type=jnp.float32)
    left_window = jnp.dot(core_left.astype(jnp.float32), window.astype(jnp.float32), precision=highest, preferred_element_type=jnp.float32)
    sketch_z = lax.dot_general(left_window, core_right, (((1,), (1,)), ((), ())), precision=highest)
    gram_y = lax.dot_general(sketch_y, sketch_y, (((0,), (0,)), ((), ())), precision=highest) / M
    gram_w = lax.dot_general(sketch_w, sketch_w, (((1,), (1,)), ((), ())), precision=highest) / N
    lower_y = jnp.linalg.cholesky(gram_y)
    lower_w = jnp.linalg.cholesky(gram_w)
    range_basis = jax.scipy.linalg.solve_triangular(lower_y, sketch_y.T, lower=True).T
    co_basis = jax.scipy.linalg.solve_triangular(lower_w, sketch_w, lower=True)
    left_image = jnp.dot(core_left, range_basis, precision=highest)
    right_image = lax.dot_general(core_right, co_basis, (((1,), (1,)), ((), ())), precision=highest)
    gram_left = jnp.dot(left_image.T, left_image, precision=highest)
    gram_right = jnp.dot(right_image.T, right_image, precision=highest)
    projected = jnp.dot(left_image.T, sketch_z, precision=highest)
    left_solved = jax.scipy.linalg.cho_solve((jnp.linalg.cholesky(gram_left), True), projected)
    middle = jnp.dot(left_solved, right_image, precision=highest)
    core = jax.scipy.linalg.cho_solve((jnp.linalg.cholesky(gram_right), True), middle.T).T
    core = core * math.sqrt(M * N)
    return (range_basis, co_basis, core)
```

```python
import math

import jax
import jax.numpy as jnp
from jax import lax
from jax.experimental import pallas as pl
from jax.experimental.pallas import tpu as pltpu
from jax.sharding import PartitionSpec as P

BASE = 64
LANES = 128
SUBLANES = 8


def contract(left, right, left_dim, right_dim, precision):
    dims = (((left_dim,), (right_dim,)), ((), ()))
    return lax.dot_general(left, right, dims, precision=precision, preferred_element_type=jnp.float32)


def high(left, right, left_dim=1, right_dim=0):
    return contract(left, right, left_dim, right_dim, lax.Precision.HIGH)


def highest(left, right, left_dim=1, right_dim=0):
    return contract(left, right, left_dim, right_dim, lax.Precision.HIGHEST)


def bits_of(axis):
    return int(math.log2(lax.axis_size(axis)))


def swap(values, axis, bit):
    return lax.ppermute(values, axis, [(i, i ^ (1 << bit)) for i in range(lax.axis_size(axis))])


def side_of(axis, bit):
    return (lax.axis_index(axis) >> bit) & 1


def halve(values, axis, bit, dim):
    extent = values.shape[dim] // 2
    side = side_of(axis, bit)
    kept = lax.dynamic_slice_in_dim(values, side * extent, extent, dim)
    sent = lax.dynamic_slice_in_dim(values, (1 - side) * extent, extent, dim)
    return kept + swap(sent, axis, bit)


def join(values, axis, bit, dim):
    other = swap(values, axis, bit)
    first = jnp.concatenate([values, other], axis=dim)
    second = jnp.concatenate([other, values], axis=dim)
    return jnp.where(side_of(axis, bit) == 0, first, second)


def reduce_pieces(values, steps, dim):
    for axis, bit in steps:
        values = halve(values, axis, bit, dim)
    return values


def gather_pieces(values, steps, dim):
    for axis, bit in reversed(steps):
        values = join(values, axis, bit, dim)
    return values


def spread_lane(values, lane):
    return jnp.broadcast_to(values[:, lane:lane + 1], values.shape)


def spread_row(values, row):
    return jnp.broadcast_to(values[row:row + 1, :], values.shape)


def factor_blocks(blocks):
    count = len(blocks)
    groups = BASE // SUBLANES
    rows = [[x[SUBLANES * g:SUBLANES * (g + 1)] for g in range(groups)] for x in blocks]
    sub = lax.broadcasted_iota(jnp.int32, (SUBLANES, LANES), 0)
    pivots = [[] for _ in blocks]
    for p in range(groups):
        cols = [{g: [spread_lane(rows[b][g], SUBLANES * p + k) for k in range(SUBLANES)] for g in range(p, groups)} for b in range(count)]
        found = [jnp.zeros((SUBLANES, LANES), jnp.float32)] * count
        for k in range(SUBLANES):
            for b in range(count):
                held = cols[b]
                pivot = spread_row(held[p][k], k)
                found[b] = jnp.where(sub == k, pivot, found[b])
                scale = 1.0 / pivot
                pivot_row = spread_row(rows[b][p], k)
                heads = [spread_row(held[p][j], k) for j in range(k + 1, SUBLANES)]
                for g in range(p, groups):
                    weight = held[g][k] * scale
                    if g == p:
                        weight = jnp.where(sub > k, weight, 0.0)
                    rows[b][g] = rows[b][g] - weight * pivot_row
                    for j in range(k + 1, SUBLANES):
                        held[g][j] = held[g][j] - weight * heads[j - k - 1]
        for b in range(count):
            pivots[b].append(found[b])
    return [jnp.concatenate([rows[b][g] * lax.rsqrt(pivots[b][g]) for g in range(groups)], axis=0) for b in range(count)]


def factor_kernel(gram_ref, inverse_ref, upper_ref):
    count, n = gram_ref.shape[0], gram_ref.shape[1]
    every = range(count)
    inverse_ref[...] = gram_ref[...]
    row_id = lax.broadcasted_iota(jnp.int32, (n, n), 0)
    col_id = lax.broadcasted_iota(jnp.int32, (n, n), 1)
    panel_col = lax.broadcasted_iota(jnp.int32, (BASE, n), 1)
    lane = lax.broadcasted_iota(jnp.int32, (BASE, LANES), 1)
    low = lax.broadcasted_iota(jnp.int32, (BASE, LANES), 0)

    def place(half, start):
        rest = [jnp.zeros((BASE, LANES), jnp.float32)] * (n // LANES - 1)
        return pltpu.roll(jnp.concatenate([jnp.where(lane < BASE, half, 0.0)] + rest, axis=1), start, 1)

    def step(t, carry):
        start = pl.multiple_of(t * BASE, BASE)
        back = jnp.where(t == 0, 0, n - start)
        panel = [inverse_ref[b, pl.ds(start, BASE), :] for b in every]
        whole = [inverse_ref[b] for b in every]
        block = [pltpu.roll(panel[b], back, 1)[:, :LANES] for b in every]
        block = [jnp.where(lane < BASE, block[b], jnp.where(lane - BASE == low, 1.0, 0.0)) for b in every]
        done = factor_blocks(block)
        inv = [pltpu.roll(done[b], LANES - BASE, 1) for b in every]
        inv_placed = [place(inv[b], start) for b in every]
        up_placed = [place(done[b], start) for b in every]
        inside = (panel_col >= start) & (panel_col < start + BASE)
        rows = [jnp.where(inside, inv_placed[b], highest(inv[b][:, :BASE], panel[b])) for b in every]
        below = [jnp.where(row_id[:, :BASE] >= start + BASE, highest(whole[b], inv_placed[b], 1, 1), 0.0) for b in every]
        spent = (row_id >= start + BASE) & (col_id >= start) & (col_id < start + BASE)
        left = [jnp.where(spent, 0.0, whole[b]) - highest(below[b], rows[b]) for b in every]
        for b in every:
            inverse_ref[b] = left[b]
        for b in every:
            inverse_ref[b, pl.ds(start, BASE), :] = rows[b]
            upper_ref[b, pl.ds(start, BASE), :] = jnp.where(inside, up_placed[b], jnp.where(panel_col >= start + BASE, rows[b], 0.0))
        return carry

    lax.fori_loop(0, n // BASE, step, 0)
    for b in every:
        inverse_ref[b] = jnp.where(row_id >= col_id, inverse_ref[b], 0.0)
        upper_ref[b] = jnp.where(row_id <= col_id, upper_ref[b], 0.0)


def factor_grams(grams):
    count, n, _ = grams.shape
    vmem = pl.BlockSpec(memory_space=pltpu.VMEM)
    return pl.pallas_call(
        factor_kernel,
        out_shape=(jax.ShapeDtypeStruct(grams.shape, jnp.float32),) * 2,
        in_specs=[vmem],
        out_specs=(vmem, vmem),
        compiler_params=pltpu.CompilerParams(vmem_limit_bytes=24 * 1024 * 1024),
        cost_estimate=pl.CostEstimate(flops=count * n * n * n * 200, bytes_accessed=count * n * n * 12, transcendentals=0),
    )(grams)


def per_device(window, range_test, co_test, core_left, core_right):
    rows_total = window.shape[0] * lax.axis_size("cell")
    cols_total = window.shape[1] * lax.axis_size("tm")
    k = range_test.shape[1]
    s_core = core_left.shape[0]
    cell_steps = [("cell", bit) for bit in range(bits_of("cell"))]
    tm_steps = [("tm", bit) for bit in range(bits_of("tm"))]
    core_steps = cell_steps[:1] + cell_steps[:0:-1] + tm_steps

    range_term = high(window, range_test)
    co_term = high(co_test, window)
    range_piece = reduce_pieces(range_term, tm_steps, 0)
    co_piece = reduce_pieces(co_term, cell_steps, 1)
    window_core = high(window, core_right, 1, 1)
    left_fold = high(core_left, range_term)
    core_term = high(core_left, window_core)
    right_fold = high(window_core, co_test, 0, 1)
    sketches = jnp.concatenate([core_term, left_fold, right_fold], axis=1)
    sketches = gather_pieces(reduce_pieces(sketches, core_steps, 0), core_steps, 0)
    sketch_z, left_total, right_total = sketches[:, :s_core], sketches[:, s_core:s_core + k], sketches[:, s_core + k:]

    grams = jnp.stack([highest(range_piece, range_piece, 0, 0) / rows_total, highest(co_piece, co_piece, 1, 1) / cols_total])
    grams = grams.reshape(-1, k)
    gram_steps = cell_steps + tm_steps
    grams = gather_pieces(reduce_pieces(grams, gram_steps, 0), gram_steps, 0).reshape(2, k, k)
    range_full = gather_pieces(range_piece, tm_steps, 0)
    co_full = gather_pieces(co_piece, cell_steps, 1)
    inverses, uppers = factor_grams(grams)
    range_basis = high(range_full, inverses[0], 1, 1)
    co_basis = high(inverses[1], co_full)

    image_grams = jnp.stack([highest(left_total, left_total, 0, 0), highest(right_total, right_total, 0, 0)])
    image_inverses, _ = factor_grams(image_grams)
    middle = highest(highest(left_total, sketch_z, 0, 0), right_total)
    middle = highest(highest(image_inverses[0], middle), image_inverses[1], 1, 1)
    left_side = highest(uppers[0], image_inverses[0], 1, 1)
    right_side = highest(image_inverses[1], uppers[1], 1, 1)
    core = highest(highest(left_side, middle), right_side) * math.sqrt(rows_total * cols_total)
    return (range_basis, co_basis, core)


def solution(mesh):
    return jax.shard_map(
        per_device,
        mesh=mesh,
        in_specs=(P("cell", "tm"), P("tm", None), P(None, "cell"), P(None, "cell"), P(None, "tm")),
        out_specs=(P("cell", None), P(None, "tm"), P()),
        check_vma=False,
    )
```

```python
import math

import jax
import jax.numpy as jnp
from jax import lax
from jax.experimental import pallas as pl
from jax.experimental.pallas import tpu as pltpu
from jax.sharding import PartitionSpec as P

BASE = 64
LANES = 128
SUBLANES = 8
VMEM_BYTES = 48 * 1024 * 1024


def contract(left, right, left_dim, right_dim, precision):
    dims = (((left_dim,), (right_dim,)), ((), ()))
    return lax.dot_general(left, right, dims, precision=precision, preferred_element_type=jnp.float32)


def high(left, right, left_dim=1, right_dim=0):
    return contract(left, right, left_dim, right_dim, lax.Precision.HIGH)


def highest(left, right, left_dim=1, right_dim=0):
    return contract(left, right, left_dim, right_dim, lax.Precision.HIGHEST)


def bits_of(axis):
    return int(math.log2(lax.axis_size(axis)))


def groups_of(axis, first, width):
    bits = list(range(first, bits_of(axis)))
    return [(axis, tuple(bits[i:i + width])) for i in range(0, len(bits), width)]


def swap(values, axis, mask):
    return lax.ppermute(values, axis, [(i, i ^ mask) for i in range(lax.axis_size(axis))])


def side_of(axis, bit):
    return (lax.axis_index(axis) >> bit) & 1


def place_of(axis, bits):
    return sum(side_of(axis, bit) << i for i, bit in enumerate(bits))


def masks_of(bits):
    return [sum(((peer >> i) & 1) << bit for i, bit in enumerate(bits)) for peer in range(1 << len(bits))]


def pair_sum(parts):
    while len(parts) > 1:
        parts = [parts[i] + parts[i + 1] for i in range(0, len(parts), 2)]
    return parts[0]


def scatter_sum(values, group, dim):
    axis, bits = group
    peers = 1 << len(bits)
    extent = values.shape[dim] // peers
    place = place_of(axis, bits)
    parts = [lax.dynamic_slice_in_dim(values, (place ^ peer) * extent, extent, dim) for peer in range(peers)]
    return pair_sum([parts[0]] + [swap(parts[peer], axis, masks_of(bits)[peer]) for peer in range(1, peers)])


def whole_sum(values, group):
    axis, bits = group
    return pair_sum([values] + [swap(values, axis, mask) for mask in masks_of(bits)[1:]])


def gather(values, group, dim):
    axis, bits = group
    peers = 1 << len(bits)
    place = place_of(axis, bits)
    parts = [values] + [swap(values, axis, mask) for mask in masks_of(bits)[1:]]
    ordered = []
    for slot in range(peers):
        chosen = parts[slot]
        for here in range(1, peers):
            chosen = jnp.where(place == here, parts[slot ^ here], chosen)
        ordered.append(chosen)
    return jnp.concatenate(ordered, axis=dim)


def total_over_chips(values):
    for group in groups_of("cell", 1, 2):
        values = scatter_sum(values, group, 0)
    for group in groups_of("tm", 0, 2):
        values = whole_sum(values, group)
    for group in reversed(groups_of("cell", 1, 2)):
        values = gather(values, group, 0)
    return values


def split(values):
    top = values.astype(jnp.bfloat16)
    return top, (values - top.astype(jnp.float32)).astype(jnp.bfloat16)


def parts_dot(left, right, left_dim=1, right_dim=0):
    dims = (((left_dim,), (right_dim,)), ((), ()))
    pairs = ((left[0], right[0]), (left[0], right[1]), (left[1], right[0]))
    return sum(lax.dot_general(a, b, dims, preferred_element_type=jnp.float32) for a, b in pairs)


def range_kernel(order_ref, window_ref, test_ref, first_ref, second_ref, top_ref, rest_ref):
    @pl.when(pl.program_id(0) == 0)
    def _():
        top_ref[...], rest_ref[...] = split(test_ref[...])

    tile = parts_dot(split(window_ref[...]), (top_ref[...], rest_ref[...]))

    @pl.when(pl.program_id(0) == 0)
    def _():
        first_ref[...] = tile

    @pl.when(pl.program_id(0) == 1)
    def _():
        second_ref[...] = tile


def range_terms(window, range_test, order):
    rows, depth = window.shape
    k = range_test.shape[1]
    tile = rows // 4
    out = jax.ShapeDtypeStruct((tile, k), jnp.float32)
    return pl.pallas_call(
        range_kernel,
        out_shape=(out, out),
        grid_spec=pltpu.PrefetchScalarGridSpec(
            num_scalar_prefetch=1,
            grid=(2,),
            in_specs=[
                pl.BlockSpec((tile, depth), lambda i, order_ref: (order_ref[i], 0)),
                pl.BlockSpec((depth, k), lambda i, order_ref: (0, 0)),
            ],
            out_specs=(pl.BlockSpec((tile, k), lambda i, order_ref: (0, 0)),) * 2,
            scratch_shapes=[pltpu.VMEM((depth, k), jnp.bfloat16)] * 2,
        ),
        compiler_params=pltpu.CompilerParams(vmem_limit_bytes=VMEM_BYTES),
        cost_estimate=pl.CostEstimate(flops=rows * depth * k * 3, bytes_accessed=rows * depth * 2, transcendentals=0),
    )(order, window, range_test)


def co_kernel(order_ref, window_ref, test_ref, sent_ref, kept_ref):
    tile = parts_dot(split(test_ref[...]), split(window_ref[...]))

    @pl.when(pl.program_id(0) < 2)
    def _():
        sent_ref[...] = tile

    @pl.when(pl.program_id(0) >= 2)
    def _():
        kept_ref[...] = tile


def co_terms(window, co_test, order):
    rows, cols = window.shape
    count = co_test.shape[0]
    tile = cols // 4
    out = jax.ShapeDtypeStruct((count, 2 * tile), jnp.float32)
    return pl.pallas_call(
        co_kernel,
        out_shape=(out, out),
        grid_spec=pltpu.PrefetchScalarGridSpec(
            num_scalar_prefetch=1,
            grid=(4,),
            in_specs=[
                pl.BlockSpec((rows, tile), lambda i, order_ref: (0, order_ref[i])),
                pl.BlockSpec((count, rows), lambda i, order_ref: (0, 0)),
            ],
            out_specs=(
                pl.BlockSpec((count, tile), lambda i, order_ref: (0, jnp.minimum(i, 1))),
                pl.BlockSpec((count, tile), lambda i, order_ref: (0, jnp.maximum(i - 2, 0))),
            ),
        ),
        compiler_params=pltpu.CompilerParams(vmem_limit_bytes=VMEM_BYTES),
        cost_estimate=pl.CostEstimate(flops=rows * cols * count * 6, bytes_accessed=rows * cols * 4, transcendentals=0),
    )(order, window, co_test)


def core_kernel(order_ref, window_ref, right_ref, left_ref, co_ref, r0_ref, r1_ref, r2_ref, r3_ref, z_ref, lt_ref, rt_ref, top_ref, rest_ref, fold_ref):
    step = pl.program_id(0)

    @pl.when(step == 0)
    def _():
        top_ref[...], rest_ref[...] = split(right_ref[...])
        z_ref[...] = jnp.zeros_like(z_ref)
        lt_ref[...] = jnp.zeros_like(lt_ref)
        fold_ref[...] = jnp.zeros_like(fold_ref)

    image = split(parts_dot(split(window_ref[...]), (top_ref[...], rest_ref[...]), 1, 1))
    left = split(left_ref[...])
    z_ref[...] += parts_dot(left, image)
    fold_ref[...] += parts_dot(split(co_ref[...]), image)
    for i, r_ref in enumerate((r0_ref, r1_ref, r2_ref, r3_ref)):
        @pl.when(step == i)
        def _():
            lt_ref[...] += parts_dot(left, split(r_ref[...]))

    @pl.when(step == 3)
    def _():
        rt_ref[...] = fold_ref[...].T


def core_terms(window, core_right, core_left, co_test, ranges, order):
    rows, cols = window.shape
    s_core, count, k = core_right.shape[0], co_test.shape[0], ranges[0].shape[1]
    tile = rows // 4
    return pl.pallas_call(
        core_kernel,
        out_shape=(
            jax.ShapeDtypeStruct((s_core, s_core), jnp.float32),
            jax.ShapeDtypeStruct((s_core, k), jnp.float32),
            jax.ShapeDtypeStruct((s_core, count), jnp.float32),
        ),
        grid_spec=pltpu.PrefetchScalarGridSpec(
            num_scalar_prefetch=1,
            grid=(4,),
            in_specs=[
                pl.BlockSpec((tile, cols), lambda i, order_ref: (order_ref[i], 0)),
                pl.BlockSpec((s_core, cols), lambda i, order_ref: (0, 0)),
                pl.BlockSpec((s_core, tile), lambda i, order_ref: (0, order_ref[i])),
                pl.BlockSpec((count, tile), lambda i, order_ref: (0, order_ref[i])),
            ] + [pl.BlockSpec((tile, k), lambda i, order_ref: (0, 0))] * 4,
            out_specs=(
                pl.BlockSpec((s_core, s_core), lambda i, order_ref: (0, 0)),
                pl.BlockSpec((s_core, k), lambda i, order_ref: (0, 0)),
                pl.BlockSpec((s_core, count), lambda i, order_ref: (0, 0)),
            ),
            scratch_shapes=[pltpu.VMEM((s_core, cols), jnp.bfloat16)] * 2 + [pltpu.VMEM((count, s_core), jnp.float32)],
        ),
        compiler_params=pltpu.CompilerParams(vmem_limit_bytes=VMEM_BYTES),
        cost_estimate=pl.CostEstimate(flops=rows * cols * s_core * 9, bytes_accessed=rows * cols * 4, transcendentals=0),
    )(order, window, core_right, core_left, co_test, *ranges)


def spread_lane(values, lane):
    return jnp.broadcast_to(values[:, lane:lane + 1], values.shape)


def spread_row(values, row):
    return jnp.broadcast_to(values[row:row + 1, :], values.shape)


def factor_blocks(blocks):
    count = len(blocks)
    groups = BASE // SUBLANES
    rows = [[x[SUBLANES * g:SUBLANES * (g + 1)] for g in range(groups)] for x in blocks]
    sub = lax.broadcasted_iota(jnp.int32, (SUBLANES, LANES), 0)
    pivots = [[] for _ in blocks]
    for p in range(groups):
        cols = [{g: [spread_lane(rows[b][g], SUBLANES * p + k) for k in range(SUBLANES)] for g in range(p, groups)} for b in range(count)]
        found = [jnp.zeros((SUBLANES, LANES), jnp.float32)] * count
        for k in range(SUBLANES):
            for b in range(count):
                held = cols[b]
                pivot = spread_row(held[p][k], k)
                found[b] = jnp.where(sub == k, pivot, found[b])
                scale = 1.0 / pivot
                pivot_row = spread_row(rows[b][p], k)
                heads = [spread_row(held[p][j], k) for j in range(k + 1, SUBLANES)]
                for g in range(p, groups):
                    weight = held[g][k] * scale
                    if g == p:
                        weight = jnp.where(sub > k, weight, 0.0)
                    rows[b][g] = rows[b][g] - weight * pivot_row
                    for j in range(k + 1, SUBLANES):
                        held[g][j] = held[g][j] - weight * heads[j - k - 1]
        for b in range(count):
            pivots[b].append(found[b])
    return [jnp.concatenate([rows[b][g] * lax.rsqrt(pivots[b][g]) for g in range(groups)], axis=0) for b in range(count)]


def factor_kernel(gram_ref, inverse_ref, upper_ref):
    count, n = gram_ref.shape[0], gram_ref.shape[1]
    every = range(count)
    inverse_ref[...] = gram_ref[...]
    row_id = lax.broadcasted_iota(jnp.int32, (n, n), 0)
    col_id = lax.broadcasted_iota(jnp.int32, (n, n), 1)
    panel_col = lax.broadcasted_iota(jnp.int32, (BASE, n), 1)
    lane = lax.broadcasted_iota(jnp.int32, (BASE, LANES), 1)
    low = lax.broadcasted_iota(jnp.int32, (BASE, LANES), 0)

    def place(half, start):
        rest = [jnp.zeros((BASE, LANES), jnp.float32)] * (n // LANES - 1)
        return pltpu.roll(jnp.concatenate([jnp.where(lane < BASE, half, 0.0)] + rest, axis=1), start, 1)

    def step(t, carry):
        start = pl.multiple_of(t * BASE, BASE)
        back = jnp.where(t == 0, 0, n - start)
        panel = [inverse_ref[b, pl.ds(start, BASE), :] for b in every]
        whole = [inverse_ref[b] for b in every]
        block = [pltpu.roll(panel[b], back, 1)[:, :LANES] for b in every]
        block = [jnp.where(lane < BASE, block[b], jnp.where(lane - BASE == low, 1.0, 0.0)) for b in every]
        done = factor_blocks(block)
        inv = [pltpu.roll(done[b], LANES - BASE, 1) for b in every]
        inv_placed = [place(inv[b], start) for b in every]
        up_placed = [place(done[b], start) for b in every]
        inside = (panel_col >= start) & (panel_col < start + BASE)
        rows = [jnp.where(inside, inv_placed[b], highest(inv[b][:, :BASE], panel[b])) for b in every]
        below = [jnp.where(row_id[:, :BASE] >= start + BASE, highest(whole[b], inv_placed[b], 1, 1), 0.0) for b in every]
        spent = (row_id >= start + BASE) & (col_id >= start) & (col_id < start + BASE)
        left = [jnp.where(spent, 0.0, whole[b]) - highest(below[b], rows[b]) for b in every]
        for b in every:
            inverse_ref[b] = left[b]
        for b in every:
            inverse_ref[b, pl.ds(start, BASE), :] = rows[b]
            upper_ref[b, pl.ds(start, BASE), :] = jnp.where(inside, up_placed[b], jnp.where(panel_col >= start + BASE, rows[b], 0.0))
        return carry

    lax.fori_loop(0, n // BASE, step, 0)
    for b in every:
        inverse_ref[b] = jnp.where(row_id >= col_id, inverse_ref[b], 0.0)
        upper_ref[b] = jnp.where(row_id <= col_id, upper_ref[b], 0.0)


def factor_gram(gram):
    inverse, upper = factor_grams(gram[None])
    return inverse[0], upper[0]


def factor_grams(grams):
    count, n, _ = grams.shape
    vmem = pl.BlockSpec(memory_space=pltpu.VMEM)
    return pl.pallas_call(
        factor_kernel,
        out_shape=(jax.ShapeDtypeStruct(grams.shape, jnp.float32),) * 2,
        in_specs=[vmem],
        out_specs=(vmem, vmem),
        compiler_params=pltpu.CompilerParams(vmem_limit_bytes=24 * 1024 * 1024),
        cost_estimate=pl.CostEstimate(flops=count * n * n * n * 200, bytes_accessed=count * n * n * 12, transcendentals=0),
    )(grams)


def reduce_rows(first, second, third, fourth, axis):
    toward_far = swap(first, axis, 1)
    toward_near = swap(second, axis, 1)
    handed = swap(third + toward_far, axis, 2)
    piece = fourth + toward_near + handed
    for group in groups_of(axis, 2, 1):
        piece = scatter_sum(piece, group, 0)
    return piece


def gather_rows(piece, axis):
    for bit in reversed(range(bits_of(axis))):
        piece = gather(piece, (axis, (bit,)), 0)
    return piece


def per_device(window, range_test, co_test, core_left, core_right):
    rows_total = window.shape[0] * lax.axis_size("cell")
    cols_total = window.shape[1] * lax.axis_size("tm")
    core = side_of("cell", 0)
    near, far = side_of("tm", 0), side_of("tm", 1)
    cell_groups = groups_of("cell", 1, 2)

    order = jnp.stack([(1 - near) * 2 + 1 - far, (1 - near) * 2 + far, near * 2 + 1 - far, near * 2 + far]).astype(jnp.int32)
    first, second = range_terms(window, range_test, order[:2])
    third, fourth = range_terms(window, range_test, order[2:])
    halves = jnp.stack([(1 - core) * 2, (1 - core) * 2 + 1, core * 2, core * 2 + 1]).astype(jnp.int32)
    co_sent, co_kept = co_terms(window, co_test, halves)
    core_term, left_fold, right_fold = core_terms(window, core_right, core_left, co_test, (first, second, third, fourth), order)

    range_piece = reduce_rows(first, second, third, fourth, "tm")
    co_piece = co_kept + swap(co_sent, "cell", 1)
    for group in cell_groups:
        co_piece = scatter_sum(co_piece, group, 1)

    def own(left, right):
        return jnp.where(core == 0, left, right)

    fold = own(left_fold, right_fold) + swap(own(right_fold, left_fold), "cell", 1)
    fold = total_over_chips(fold)
    other_fold = swap(fold, "cell", 1)
    left_total, right_total = own(fold, other_fold), own(other_fold, fold)
    image_inverse, _ = factor_gram(highest(fold, fold, 0, 0))

    middle = high(high(left_total, core_term, 0, 0), right_total)
    middle = scatter_sum(middle, ("cell", (0,)), 0)
    middle = gather(total_over_chips(middle), ("cell", (0,)), 0)

    gram_y = highest(range_piece, range_piece, 0, 0) / rows_total
    gram_w = highest(co_piece, co_piece, 1, 1) / cols_total
    gram = own(gram_y, gram_w) + swap(own(gram_w, gram_y), "cell", 1)
    gram = total_over_chips(gram)
    inverse, upper = factor_gram(gram)
    other_inverse = swap(inverse, "cell", 1)

    range_full = gather_rows(range_piece, "tm")
    co_full = co_piece
    for group in reversed(cell_groups):
        co_full = gather(co_full, group, 1)
    co_full = gather(co_full, ("cell", (0,)), 1)
    range_basis = high(range_full, own(inverse, other_inverse), 1, 1)
    co_basis = high(own(other_inverse, inverse), co_full)

    flank = highest(highest(upper, image_inverse, 1, 1), image_inverse)
    other_flank = swap(flank, "cell", 1)
    core_out = highest(highest(own(flank, other_flank), middle), own(other_flank, flank), 1, 1)
    return (range_basis, co_basis, core_out * math.sqrt(rows_total * cols_total))


def solution(mesh):
    return jax.shard_map(
        per_device,
        mesh=mesh,
        in_specs=(P("cell", "tm"), P("tm", None), P(None, "cell"), P(None, "cell"), P(None, "tm")),
        out_specs=(P("cell", None), P(None, "tm"), P()),
        check_vma=False,
    )
```

```python
import functools
import math

import jax
import jax.numpy as jnp
from jax import lax
from jax.experimental import pallas as pl
from jax.experimental.pallas import tpu as pltpu
from jax.sharding import PartitionSpec as P

BASE = 64
LANES = 128
SUBLANES = 8


def contract(left, right, left_dim, right_dim, precision):
    dims = (((left_dim,), (right_dim,)), ((), ()))
    return lax.dot_general(left, right, dims, precision=precision, preferred_element_type=jnp.float32)


def highest(left, right, left_dim=1, right_dim=0):
    return contract(left, right, left_dim, right_dim, lax.Precision.HIGHEST)


def bits_of(axis):
    return int(math.log2(lax.axis_size(axis)))


def groups_of(axis, first, width):
    bits = list(range(first, bits_of(axis)))
    return [(axis, tuple(bits[i:i + width])) for i in range(0, len(bits), width)]


def swap(values, axis, mask):
    return lax.ppermute(values, axis, [(i, i ^ mask) for i in range(lax.axis_size(axis))])


def side_of(axis, bit):
    return (lax.axis_index(axis) >> bit) & 1


def place_of(axis, bits):
    return sum(side_of(axis, bit) << i for i, bit in enumerate(bits))


def masks_of(bits):
    return [sum(((peer >> i) & 1) << bit for i, bit in enumerate(bits)) for peer in range(1 << len(bits))]


def pair_sum(parts):
    while len(parts) > 1:
        parts = [parts[i] + parts[i + 1] for i in range(0, len(parts), 2)]
    return parts[0]


def scatter_sum(values, group, dim):
    axis, bits = group
    peers = 1 << len(bits)
    extent = values.shape[dim] // peers
    place = place_of(axis, bits)
    parts = [lax.dynamic_slice_in_dim(values, (place ^ peer) * extent, extent, dim) for peer in range(peers)]
    return pair_sum([parts[0]] + [swap(parts[peer], axis, masks_of(bits)[peer]) for peer in range(1, peers)])


def whole_sum(values, group):
    axis, bits = group
    return pair_sum([values] + [swap(values, axis, mask) for mask in masks_of(bits)[1:]])


def gather(values, group, dim):
    axis, bits = group
    peers = 1 << len(bits)
    place = place_of(axis, bits)
    parts = [values] + [swap(values, axis, mask) for mask in masks_of(bits)[1:]]
    ordered = []
    for slot in range(peers):
        chosen = parts[slot]
        for here in range(1, peers):
            chosen = jnp.where(place == here, parts[slot ^ here], chosen)
        ordered.append(chosen)
    return jnp.concatenate(ordered, axis=dim)


def total_over_chips(values):
    for group in groups_of("cell", 1, 2):
        values = scatter_sum(values, group, 0)
    for group in groups_of("tm", 0, 2):
        values = whole_sum(values, group)
    for group in reversed(groups_of("cell", 1, 2)):
        values = gather(values, group, 0)
    return values


def split(values):
    top = values.astype(jnp.bfloat16)
    return top, (values - top.astype(jnp.float32)).astype(jnp.bfloat16)


def parts_dot(left, right, left_dim=1, right_dim=0):
    dims = (((left_dim,), (right_dim,)), ((), ()))
    pairs = ((left[0], right[0]), (left[0], right[1]), (left[1], right[0]))
    return sum(lax.dot_general(a, b, dims, preferred_element_type=jnp.float32) for a, b in pairs)


def call(kernel, out_shape, in_specs, out_specs, scratch=(), flops=0, limit=24):
    return pl.pallas_call(
        kernel,
        out_shape=out_shape,
        in_specs=in_specs,
        out_specs=out_specs,
        scratch_shapes=list(scratch),
        compiler_params=pltpu.CompilerParams(vmem_limit_bytes=limit * 1024 * 1024),
        cost_estimate=pl.CostEstimate(flops=flops, bytes_accessed=4 * 1024 * 1024, transcendentals=0),
    )


WHOLE = pl.BlockSpec(memory_space=pltpu.VMEM)
SCALAR = pl.BlockSpec(memory_space=pltpu.SMEM)
OUTSIDE = pl.BlockSpec(memory_space=pl.ANY)
TILES = 4


def float_shape(*shape):
    return jax.ShapeDtypeStruct(shape, jnp.float32)


def range_kernel(window_ref, test_ref, out_ref, held_ref, test_held_ref, top_ref, rest_ref, window_sem, test_sem):
    tile = held_ref.shape[1]
    test_copy = pltpu.make_async_copy(test_ref, test_held_ref, test_sem)
    test_copy.start()
    for i in range(TILES):
        pltpu.make_async_copy(window_ref.at[pl.ds(i * tile, tile)], held_ref.at[i], window_sem.at[i]).start()
    test_copy.wait()
    top_ref[...], rest_ref[...] = split(test_held_ref[...])

    def step(i, carry):
        start = pl.multiple_of(i * tile, tile)
        pltpu.make_async_copy(window_ref.at[pl.ds(start, tile)], held_ref.at[i], window_sem.at[i]).wait()
        out_ref[pl.ds(start, tile), :] = parts_dot(split(held_ref[i]), (top_ref[...], rest_ref[...]))
        return carry

    lax.fori_loop(0, TILES, step, 0)


def range_terms(window, range_test):
    rows, depth = window.shape
    k = range_test.shape[1]
    return call(
        range_kernel, float_shape(rows, k), [OUTSIDE, OUTSIDE], WHOLE,
        [
            pltpu.VMEM((TILES, rows // TILES, depth), jnp.float32), pltpu.VMEM((depth, k), jnp.float32),
            pltpu.VMEM((depth, k), jnp.bfloat16), pltpu.VMEM((depth, k), jnp.bfloat16),
            pltpu.SemaphoreType.DMA((TILES,)), pltpu.SemaphoreType.DMA,
        ],
        flops=6 * rows * depth * k,
    )(window, range_test)


def co_kernel(core_ref, window_ref, test_ref, sent_ref, kept_ref, top_ref, rest_ref):
    half = sent_ref.shape[1]
    tile = half // 2
    top_ref[...], rest_ref[...] = split(test_ref[...])
    for out_ref, side in ((sent_ref, 1 - core_ref[0]), (kept_ref, core_ref[0])):
        for i in range(2):
            start = pl.multiple_of(side * half + i * tile, tile)
            out_ref[:, i * tile:(i + 1) * tile] = parts_dot((top_ref[...], rest_ref[...]), split(window_ref[:, pl.ds(start, tile)]))


def co_terms(core, window, co_test):
    rows, cols = window.shape
    count = co_test.shape[0]
    return call(
        co_kernel, (float_shape(count, cols // 2),) * 2, [SCALAR, WHOLE, WHOLE], (WHOLE, WHOLE),
        [pltpu.VMEM((count, rows), jnp.bfloat16)] * 2,
        flops=6 * rows * cols * count,
    )(core, window, co_test)


def core_kernel(core_ref, window_ref, right_ref, left_ref, co_ref, range_ref, sent_ref, kept_ref, top_ref, rest_ref, z_ref, lt_ref, rt_ref):
    rows = window_ref.shape[0]
    tile = rows // TILES
    s_core, k = lt_ref.shape
    half = s_core // 2
    top_ref[...], rest_ref[...] = split(right_ref[...])
    z_ref[...] = jnp.zeros_like(z_ref)
    lt_ref[...] = jnp.zeros_like(lt_ref)
    rt_ref[...] = jnp.zeros_like(rt_ref)

    def step(i, carry):
        start = pl.multiple_of(i * tile, tile)
        image = split(parts_dot(split(window_ref[pl.ds(start, tile), :]), (top_ref[...], rest_ref[...]), 1, 1))
        left = split(left_ref[:, pl.ds(start, tile)])
        z_ref[...] += parts_dot(left, image)
        rt_ref[...] += parts_dot(split(co_ref[:, pl.ds(start, tile)]), image)
        lt_ref[...] += parts_dot(left, split(range_ref[pl.ds(start, tile), :]))
        return carry

    lax.fori_loop(0, TILES, step, 0)
    for first_ref, second_ref, core in ((kept_ref, sent_ref, 0), (sent_ref, kept_ref, 1)):
        @pl.when(core_ref[0] == core)
        def _():
            first_ref[:, :k] = lt_ref[...]
            first_ref[:, k:] = z_ref[:, :half]
            second_ref[:, :k] = rt_ref[...].T
            second_ref[:, k:] = z_ref[:, half:]


def core_terms(core, window, core_right, core_left, co_test, range_term):
    rows, cols = window.shape
    s_core, count, k = core_right.shape[0], co_test.shape[0], range_term.shape[1]
    return call(
        core_kernel, (float_shape(s_core, k + s_core // 2),) * 2, [SCALAR] + [WHOLE] * 5, (WHOLE, WHOLE),
        [pltpu.VMEM((s_core, cols), jnp.bfloat16)] * 2
        + [pltpu.VMEM((s_core, s_core), jnp.float32), pltpu.VMEM((s_core, k), jnp.float32), pltpu.VMEM((count, s_core), jnp.float32)],
        flops=18 * rows * cols * s_core,
    )(core, window, core_right, core_left, co_test, range_term)


def gram_kernel(scales, core_ref, range_ref, co_ref, sent_ref, kept_ref):
    gram_y = highest(range_ref[...], range_ref[...], 0, 0) / scales[0]
    gram_w = highest(co_ref[...], co_ref[...], 1, 1) / scales[1]
    first = core_ref[0] == 0
    kept_ref[...] = jnp.where(first, gram_y, gram_w)
    sent_ref[...] = jnp.where(first, gram_w, gram_y)


def gram_terms(core, range_piece, co_piece, scales):
    k = range_piece.shape[1]
    kernel = functools.partial(gram_kernel, scales)
    return call(kernel, (float_shape(k, k),) * 2, [SCALAR, WHOLE, WHOLE], (WHOLE, WHOLE), flops=12 * k * k * k * 2)(core, range_piece, co_piece)


def middle_kernel(core_ref, own_ref, other_ref, middle_ref, gram_ref):
    k = middle_ref.shape[0]
    first = core_ref[0] == 0
    own, other = own_ref[...], other_ref[...]
    left, right = jnp.where(first, own, other), jnp.where(first, other, own)
    gram_ref[...] = highest(own[:, :k], own[:, :k], 0, 0)
    halves = [highest(left[:, :k], side[:, k:], 0, 0) for side in (left, right)]
    middle_ref[...] = highest(jnp.concatenate(halves, axis=1), right[:, :k])


def middle_terms(core, own, other, k):
    return call(middle_kernel, (float_shape(k, k),) * 2, [SCALAR, WHOLE, WHOLE], (WHOLE, WHOLE), flops=12 * k * k * k * 8)(core, own, other)


def spread_lane(values, lane):
    return jnp.broadcast_to(values[:, lane:lane + 1], values.shape)


def spread_row(values, row):
    return jnp.broadcast_to(values[row:row + 1, :], values.shape)


def factor_blocks(blocks):
    count = len(blocks)
    groups = BASE // SUBLANES
    rows = [[x[SUBLANES * g:SUBLANES * (g + 1)] for g in range(groups)] for x in blocks]
    sub = lax.broadcasted_iota(jnp.int32, (SUBLANES, LANES), 0)
    pivots = [[] for _ in blocks]
    for p in range(groups):
        cols = [{g: [spread_lane(rows[b][g], SUBLANES * p + k) for k in range(SUBLANES)] for g in range(p, groups)} for b in range(count)]
        found = [jnp.zeros((SUBLANES, LANES), jnp.float32)] * count
        for k in range(SUBLANES):
            for b in range(count):
                held = cols[b]
                pivot = spread_row(held[p][k], k)
                found[b] = jnp.where(sub == k, pivot, found[b])
                scale = 1.0 / pivot
                pivot_row = spread_row(rows[b][p], k)
                heads = [spread_row(held[p][j], k) for j in range(k + 1, SUBLANES)]
                for g in range(p, groups):
                    weight = held[g][k] * scale
                    if g == p:
                        weight = jnp.where(sub > k, weight, 0.0)
                    rows[b][g] = rows[b][g] - weight * pivot_row
                    for j in range(k + 1, SUBLANES):
                        held[g][j] = held[g][j] - weight * heads[j - k - 1]
        for b in range(count):
            pivots[b].append(found[b])
    return [jnp.concatenate([rows[b][g] * lax.rsqrt(pivots[b][g]) for g in range(groups)], axis=0) for b in range(count)]


def factor_kernel(gram_ref, image_ref, out_ref, inverse_ref, upper_ref):
    count, n = inverse_ref.shape[0], inverse_ref.shape[1]
    every = range(count)
    inverse_ref[0] = gram_ref[...]
    inverse_ref[1] = image_ref[...]
    row_id = lax.broadcasted_iota(jnp.int32, (n, n), 0)
    col_id = lax.broadcasted_iota(jnp.int32, (n, n), 1)
    panel_col = lax.broadcasted_iota(jnp.int32, (BASE, n), 1)
    lane = lax.broadcasted_iota(jnp.int32, (BASE, LANES), 1)
    low = lax.broadcasted_iota(jnp.int32, (BASE, LANES), 0)

    def place(half, start):
        rest = [jnp.zeros((BASE, LANES), jnp.float32)] * (n // LANES - 1)
        return pltpu.roll(jnp.concatenate([jnp.where(lane < BASE, half, 0.0)] + rest, axis=1), start, 1)

    def step(t, carry):
        start = pl.multiple_of(t * BASE, BASE)
        back = jnp.where(t == 0, 0, n - start)
        panel = [inverse_ref[b, pl.ds(start, BASE), :] for b in every]
        whole = [inverse_ref[b] for b in every]
        block = [pltpu.roll(panel[b], back, 1)[:, :LANES] for b in every]
        block = [jnp.where(lane < BASE, block[b], jnp.where(lane - BASE == low, 1.0, 0.0)) for b in every]
        done = factor_blocks(block)
        inv = [pltpu.roll(done[b], LANES - BASE, 1) for b in every]
        inv_placed = [place(inv[b], start) for b in every]
        up_placed = place(done[0], start)
        inside = (panel_col >= start) & (panel_col < start + BASE)
        rows = [jnp.where(inside, inv_placed[b], highest(inv[b][:, :BASE], panel[b])) for b in every]
        below = [jnp.where(row_id[:, :BASE] >= start + BASE, highest(whole[b], inv_placed[b], 1, 1), 0.0) for b in every]
        spent = (row_id >= start + BASE) & (col_id >= start) & (col_id < start + BASE)
        left = [jnp.where(spent, 0.0, whole[b]) - highest(below[b], rows[b]) for b in every]
        for b in every:
            inverse_ref[b] = left[b]
        for b in every:
            inverse_ref[b, pl.ds(start, BASE), :] = rows[b]
        upper_ref[pl.ds(start, BASE), :] = jnp.where(inside, up_placed, jnp.where(panel_col >= start + BASE, rows[0], 0.0))
        return carry

    lax.fori_loop(0, n // BASE, step, 0)
    out_ref[0] = jnp.where(row_id >= col_id, inverse_ref[0], 0.0)
    upper = jnp.where(row_id <= col_id, upper_ref[...], 0.0)
    image = jnp.where(row_id >= col_id, inverse_ref[1], 0.0)
    out_ref[1] = highest(highest(upper, image, 1, 1), image)


def factor_grams(gram, image_gram):
    n = gram.shape[0]
    return call(
        factor_kernel, float_shape(2, n, n), [WHOLE, WHOLE], WHOLE,
        [pltpu.VMEM((2, n, n), jnp.float32), pltpu.VMEM((n, n), jnp.float32)],
        flops=n * n * n * 400,
    )(gram, image_gram)


def basis_kernel(spot, core_ref, own_ref, other_ref, middle_ref, range_ref, co_ref, range_out_ref, co_out_ref, core_out_ref, parts_ref, *, scale):
    first = core_ref[0] == 0

    @pl.when(pl.program_id(0) == 0)
    def _():
        for i in range(2):
            here = jnp.where((first if i == 0 else jnp.logical_not(first)), own_ref[0], other_ref[0])
            parts_ref[2 * i], parts_ref[2 * i + 1] = split(here)
        left = jnp.where(first, own_ref[1], other_ref[1])
        right = jnp.where(first, other_ref[1], own_ref[1])
        core_out_ref[...] = highest(highest(left, middle_ref[...]), right, 1, 1) * scale

    range_out_ref[...] = parts_dot(split(range_ref[...]), (parts_ref[0], parts_ref[1]), 1, 1)
    co_out_ref[...] = parts_dot((parts_ref[2], parts_ref[3]), split(co_ref[0]))


def bases(core, own, other, middle, range_full, co_all, spot, scale):
    rows, k = range_full.shape
    blocks, count, width = co_all.shape
    tile = rows // blocks
    fixed = pl.BlockSpec((2, k, k), lambda i: (0, 0, 0))
    square = pl.BlockSpec((k, k), lambda i: (0, 0))
    return pl.pallas_call(
        functools.partial(basis_kernel, spot, scale=scale),
        out_shape=(float_shape(rows, k), float_shape(count, blocks * width), float_shape(k, k)),
        grid=(blocks,),
        in_specs=[SCALAR, fixed, fixed, square, pl.BlockSpec((tile, k), lambda i: (i, 0)), pl.BlockSpec((1, count, width), lambda i: (i, 0, 0))],
        out_specs=(pl.BlockSpec((tile, k), lambda i: (i, 0)), pl.BlockSpec((count, width), lambda i: (0, spot(i))), square),
        scratch_shapes=[pltpu.VMEM((4, k, k), jnp.bfloat16)],
        compiler_params=pltpu.CompilerParams(vmem_limit_bytes=24 * 1024 * 1024),
        cost_estimate=pl.CostEstimate(flops=18 * rows * k * k, bytes_accessed=6 * 1024 * 1024, transcendentals=0),
    )(core, own, other, middle, range_full, co_all)


def per_device(window, range_test, co_test, core_left, core_right):
    rows_total = window.shape[0] * lax.axis_size("cell")
    cols_total = window.shape[1] * lax.axis_size("tm")
    k = range_test.shape[1]
    core = side_of("cell", 0).astype(jnp.int32).reshape(1)
    cell_groups = groups_of("cell", 1, 2)

    range_term = range_terms(window, range_test)
    range_piece = lax.psum_scatter(range_term, "tm", scatter_dimension=0, tiled=True)
    co_sent, co_kept = co_terms(core, window, co_test)
    co_piece = co_kept + swap(co_sent, "cell", 1)
    for group in cell_groups:
        co_piece = scatter_sum(co_piece, group, 1)
    fold_sent, fold_kept = core_terms(core, window, core_right, core_left, co_test, range_term)

    range_full = lax.all_gather(range_piece, "tm", axis=0, tiled=True)
    co_all = lax.all_gather(co_piece, "cell", axis=0)

    gram_sent, gram_kept = gram_terms(core, range_piece, co_piece, (rows_total, cols_total))
    gram = total_over_chips(gram_kept + swap(gram_sent, "cell", 1))

    fold = total_over_chips(fold_kept + swap(fold_sent, "cell", 1))
    middle, image_gram = middle_terms(core, fold, swap(fold, "cell", 1), k)

    own = factor_grams(gram, image_gram)

    def spot(device):
        block = device & 1
        for _, bits in cell_groups:
            block = block * (1 << len(bits)) + ((device >> bits[0]) & ((1 << len(bits)) - 1))
        return block

    return bases(core, own, swap(own, "cell", 1), middle, range_full, co_all, spot, math.sqrt(rows_total * cols_total))


def solution(mesh):
    return jax.shard_map(
        per_device,
        mesh=mesh,
        in_specs=(P("cell", "tm"), P("tm", None), P(None, "cell"), P(None, "cell"), P(None, "tm")),
        out_specs=(P("cell", None), P(None, "tm"), P()),
        check_vma=False,
    )
```

```python
import functools
import math

import jax
import jax.numpy as jnp
from jax import lax
from jax.experimental import pallas as pl
from jax.experimental.pallas import tpu as pltpu
from jax.sharding import PartitionSpec as P

BASE = 64
LANES = 128
SUBLANES = 8
TILES = 4
WHOLE = pl.BlockSpec(memory_space=pltpu.VMEM)
SCALAR = pl.BlockSpec(memory_space=pltpu.SMEM)
OUTSIDE = pl.BlockSpec(memory_space=pl.ANY)


def highest(left, right, left_dim=1, right_dim=0):
    dims = (((left_dim,), (right_dim,)), ((), ()))
    return lax.dot_general(left, right, dims, precision=lax.Precision.HIGHEST, preferred_element_type=jnp.float32)


def split(values):
    top = values.astype(jnp.bfloat16)
    return top, (values - top.astype(jnp.float32)).astype(jnp.bfloat16)


def parts_dot(left, right, left_dim=1, right_dim=0):
    dims = (((left_dim,), (right_dim,)), ((), ()))
    pairs = ((left[0], right[0]), (left[0], right[1]), (left[1], right[0]))
    return sum(lax.dot_general(a, b, dims, preferred_element_type=jnp.float32) for a, b in pairs)


def float_shape(*shape):
    return jax.ShapeDtypeStruct(shape, jnp.float32)


def call(kernel, out_shape, in_specs, out_specs, scratch=(), flops=0, limit=24):
    return pl.pallas_call(
        kernel,
        out_shape=out_shape,
        in_specs=in_specs,
        out_specs=out_specs,
        scratch_shapes=list(scratch),
        compiler_params=pltpu.CompilerParams(vmem_limit_bytes=limit * 1024 * 1024),
        cost_estimate=pl.CostEstimate(flops=flops, bytes_accessed=4 * 1024 * 1024, transcendentals=0),
    )


def bits_of(axis):
    return int(math.log2(lax.axis_size(axis)))


def groups_of(axis, first, width):
    bits = list(range(first, bits_of(axis)))
    return [(axis, tuple(bits[i:i + width])) for i in range(0, len(bits), width)]


def place_of(groups, index):
    place = 0
    for _, bits in groups:
        place = (place << len(bits)) + sum(((index >> bit) & 1) << i for i, bit in enumerate(bits))
    return place


def swap(values, axis, mask):
    return lax.ppermute(values, axis, [(i, i ^ mask) for i in range(lax.axis_size(axis))])


def masks_of(bits):
    return [sum(((peer >> i) & 1) << bit for i, bit in enumerate(bits)) for peer in range(1 << len(bits))]


def pair_sum(parts):
    while len(parts) > 1:
        parts = [parts[i] + parts[i + 1] for i in range(0, len(parts), 2)]
    return parts[0]


def scatter_sum(blocks, groups):
    for axis, bits in groups:
        count = blocks.shape[0] >> len(bits)
        parts = [blocks[peer * count:(peer + 1) * count] for peer in range(1 << len(bits))]
        blocks = pair_sum([parts[0]] + [swap(part, axis, mask) for part, mask in zip(parts[1:], masks_of(bits)[1:])])
    return blocks


def gather(blocks, groups):
    parts = [blocks]
    for axis, bits in reversed(groups):
        blocks = jnp.concatenate(parts) if len(parts) > 1 else parts[0]
        parts = [blocks] + [swap(blocks, axis, mask) for mask in masks_of(bits)[1:]]
    return parts


def whole_sum(values, axis):
    for bit in range(bits_of(axis)):
        values = values + swap(values, axis, 1 << bit)
    return values


def after(values, *earlier):
    return lax.optimization_barrier((values,) + earlier)[0]


def block_start(place, block, extent):
    return pl.multiple_of((place ^ block) * extent, extent)


def put_blocks(refs, out_ref, place):
    count, extent = refs[0].shape[0], refs[0].shape[1]
    for i, ref in enumerate(refs):
        for j in range(count):
            out_ref[pl.ds(block_start(place, i * count + j, extent), extent), :] = ref[j]


def take_blocks(ref, out_ref, place, base=0):
    count, extent = out_ref.shape[0], out_ref.shape[1]
    for i in range(count):
        out_ref[i] = ref[pl.ds(pl.multiple_of(base + (place ^ i) * extent, extent), extent), :]


def pack_width(count, width, k):
    return count * width // k


def sketch_kernel(spot_ref, window_ref, test_ref, co_ref, left_ref, right_ref, r3_ref, r2_ref, r1_ref, r0_ref, sent_ref, kept_ref, held_ref, test_held_ref, co_held_ref, left_held_ref, right_held_ref, top_ref, rest_ref, co_done_ref, lt_ref, rt_ref, window_sem, sem):
    core, place, line = spot_ref[0], spot_ref[1], spot_ref[2]
    tile = held_ref.shape[1]
    chips, _, k = kept_ref.shape
    count, cols = co_done_ref.shape
    width = cols // (2 * chips)
    packed = pack_width(count, width, k)
    small = [(test_ref, test_held_ref), (co_ref, co_held_ref), (left_ref, left_held_ref), (right_ref, right_held_ref)]
    small = [pltpu.make_async_copy(a, b, sem.at[i]) for i, (a, b) in enumerate(small)]

    def window_copy(i):
        return pltpu.make_async_copy(window_ref.at[pl.ds(block_start(line, TILES - 1 - i, tile), tile)], held_ref.at[i], window_sem.at[i])

    small[0].start()
    window_copy(0).start()
    small[1].start()
    small[2].start()
    for i in range(1, TILES):
        window_copy(i).start()
    small[3].start()
    co_done_ref[...] = jnp.zeros_like(co_done_ref)
    lt_ref[...] = jnp.zeros_like(lt_ref)
    small[0].wait()
    top_ref[...], rest_ref[...] = split(test_held_ref[...])
    small[1].wait()
    small[2].wait()

    def step(i, carry):
        window_copy(i).wait()
        rows = split(held_ref[i])
        spot = pl.ds(block_start(line, TILES - 1 - i, tile), tile)
        done = parts_dot(rows, (top_ref[...], rest_ref[...]))
        co_done_ref[...] += parts_dot(split(co_held_ref[:, spot]), rows)
        lt_ref[...] += parts_dot(split(left_held_ref[:, spot]), split(done))
        for block, ref in enumerate((r3_ref, r2_ref, r1_ref, r0_ref)):
            @pl.when(i == block)
            def _():
                ref[...] = done

        return carry

    lax.fori_loop(0, TILES, step, 0)
    small[3].wait()
    rt_ref[...] = parts_dot(split(right_held_ref[...]), split(co_done_ref[...]), 1, 1)
    for ref, side in ((sent_ref, 1 - core), (kept_ref, core)):
        for i in range(chips):
            start = pl.multiple_of((side * chips + (place ^ i)) * width, width)
            for j in range(count // packed):
                ref[i, :packed, j * width:(j + 1) * width] = co_done_ref[j * packed:(j + 1) * packed, pl.ds(start, width)]
    for owner, left_out, right_out in ((0, kept_ref, sent_ref), (1, sent_ref, kept_ref)):
        @pl.when(core == owner)
        def _():
            take_blocks(lt_ref, left_out.at[:, packed:], place)
            take_blocks(rt_ref, right_out.at[:, packed:], place)


def sketch_terms(spot, chips, window, range_test, co_test, core_left, core_right):
    rows, cols = window.shape
    count, k, s_core = co_test.shape[0], range_test.shape[1], core_left.shape[0]
    block = pack_width(count, cols // (2 * chips), k) + s_core // chips
    return call(
        sketch_kernel, (float_shape(rows // TILES, k),) * 4 + (float_shape(chips, block, k),) * 2,
        [SCALAR] + [OUTSIDE] * 5, (WHOLE,) * 6,
        [
            pltpu.VMEM((TILES, rows // TILES, cols), jnp.float32), pltpu.VMEM((cols, k), jnp.float32), pltpu.VMEM((count, rows), jnp.float32),
            pltpu.VMEM((s_core, rows), jnp.float32), pltpu.VMEM((s_core, cols), jnp.float32),
            pltpu.VMEM((cols, k), jnp.bfloat16), pltpu.VMEM((cols, k), jnp.bfloat16),
            pltpu.VMEM((count, cols), jnp.float32), pltpu.VMEM((s_core, k), jnp.float32), pltpu.VMEM((s_core, k), jnp.float32),
            pltpu.SemaphoreType.DMA((TILES,)), pltpu.SemaphoreType.DMA((4,)),
        ],
        flops=12 * rows * cols * count, limit=56,
    )(spot, window, range_test, co_test, core_left, core_right)


def core_kernel(spot_ref, window_ref, right_ref, left_ref, z_ref, held_ref, right_held_ref, left_held_ref, image_ref, window_sem, right_sem, left_sem):
    width = held_ref.shape[2]
    tile = window_ref.shape[0] // TILES
    left_copy = pltpu.make_async_copy(left_ref, left_held_ref, left_sem)

    def copies(i):
        start = pl.multiple_of(i * width, width)
        return (
            pltpu.make_async_copy(right_ref.at[:, pl.ds(start, width)], right_held_ref.at[i], right_sem.at[i]),
            pltpu.make_async_copy(window_ref.at[:, pl.ds(start, width)], held_ref.at[i], window_sem.at[i]),
        )

    for i in range(TILES):
        for copy in copies(i):
            copy.start()
    left_copy.start()
    image_ref[...] = jnp.zeros_like(image_ref)

    def step(i, carry):
        for copy in copies(i):
            copy.wait()
        image_ref[...] += parts_dot(split(held_ref[i]), split(right_held_ref[i]), 1, 1)
        return carry

    lax.fori_loop(0, TILES, step, 0)
    left_copy.wait()
    z_ref[...] = jnp.zeros_like(z_ref)

    def fold(i, carry):
        start = pl.multiple_of(i * tile, tile)
        z_ref[...] += parts_dot(split(left_held_ref[:, pl.ds(start, tile)]), split(image_ref[pl.ds(start, tile), :]))
        return carry

    lax.fori_loop(0, TILES, fold, 0)


def core_terms(spot, window, core_right, core_left):
    rows, cols = window.shape
    s_core = core_right.shape[0]
    return call(
        core_kernel, float_shape(s_core, s_core), [SCALAR] + [OUTSIDE] * 3, WHOLE,
        [
            pltpu.VMEM((TILES, rows, cols // TILES), jnp.float32), pltpu.VMEM((TILES, s_core, cols // TILES), jnp.float32),
            pltpu.VMEM((s_core, rows), jnp.float32), pltpu.VMEM((rows, s_core), jnp.float32),
            pltpu.SemaphoreType.DMA((TILES,)), pltpu.SemaphoreType.DMA((TILES,)), pltpu.SemaphoreType.DMA,
        ],
        flops=9 * rows * cols * s_core, limit=56,
    )(spot, window, core_right, core_left)


def gram_kernel(scales, spot_ref, range_ref, co_ref, sent_ref, kept_ref, y_ref, w_ref):
    y_ref[...] = highest(range_ref[...], range_ref[...], 0, 0) / scales[0]
    w_ref[...] = highest(co_ref[...], co_ref[...], 1, 1) / scales[1]
    for owner, y_out, w_out in ((0, kept_ref, sent_ref), (1, sent_ref, kept_ref)):
        @pl.when(spot_ref[0] == owner)
        def _():
            take_blocks(y_ref, y_out, spot_ref[1])
            take_blocks(w_ref, w_out, spot_ref[1])


def gram_terms(spot, chips, range_piece, co_piece, scales):
    k = range_piece.shape[1]
    square = pltpu.VMEM((k, k), jnp.float32)
    return call(
        functools.partial(gram_kernel, scales), (float_shape(chips, k // chips, k),) * 2, [SCALAR, WHOLE, WHOLE], (WHOLE, WHOLE),
        [square, square], flops=24 * k * k * k,
    )(spot, range_piece, co_piece)


def middle_kernel(spot_ref, z_ref, own_ref, other_ref, sent_ref, kept_ref, gram_ref, left_ref, right_ref, middle_ref):
    core, place = spot_ref[0], spot_ref[1]
    for owner, left_in, right_in in ((0, own_ref, other_ref), (1, other_ref, own_ref)):
        @pl.when(core == owner)
        def _():
            put_blocks([left_in], left_ref, place)
            put_blocks([right_in], right_ref, place)

    first = core == 0
    own = jnp.where(first, left_ref[...], right_ref[...])
    gram_ref[...] = highest(own, own, 0, 0)
    middle_ref[...] = parts_dot(split(parts_dot(split(left_ref[...]), split(z_ref[...]), 0, 0)), split(right_ref[...]))
    half = middle_ref.shape[0] // 2
    take_blocks(middle_ref, kept_ref, place, core * half)
    take_blocks(middle_ref, sent_ref, place, (1 - core) * half)


def middle_terms(spot, chips, sketch_z, own, other):
    s_core, k = sketch_z.shape[0], own.shape[2]
    return call(
        middle_kernel, (float_shape(chips, k // (2 * chips), k),) * 2 + (float_shape(k, k),), [SCALAR] + [WHOLE] * 3, (WHOLE,) * 3,
        [pltpu.VMEM((s_core, k), jnp.float32), pltpu.VMEM((s_core, k), jnp.float32), pltpu.VMEM((k, k), jnp.float32)],
        flops=6 * k * s_core * s_core,
    )(spot, sketch_z, own, other)


def spread_lane(values, lane):
    return jnp.broadcast_to(values[:, lane:lane + 1], values.shape)


def spread_row(values, row):
    return jnp.broadcast_to(values[row:row + 1, :], values.shape)


def factor_blocks(blocks):
    count = len(blocks)
    groups = BASE // SUBLANES
    rows = [[x[SUBLANES * g:SUBLANES * (g + 1)] for g in range(groups)] for x in blocks]
    sub = lax.broadcasted_iota(jnp.int32, (SUBLANES, LANES), 0)
    pivots = [[] for _ in blocks]
    for p in range(groups):
        cols = [{g: [spread_lane(rows[b][g], SUBLANES * p + k) for k in range(SUBLANES)] for g in range(p, groups)} for b in range(count)]
        found = [jnp.zeros((SUBLANES, LANES), jnp.float32)] * count
        for k in range(SUBLANES):
            for b in range(count):
                held = cols[b]
                pivot = spread_row(held[p][k], k)
                found[b] = jnp.where(sub == k, pivot, found[b])
                scale = 1.0 / pivot
                pivot_row = spread_row(rows[b][p], k)
                heads = [spread_row(held[p][j], k) for j in range(k + 1, SUBLANES)]
                for g in range(p, groups):
                    weight = held[g][k] * scale
                    if g == p:
                        weight = jnp.where(sub > k, weight, 0.0)
                    rows[b][g] = rows[b][g] - weight * pivot_row
                    for j in range(k + 1, SUBLANES):
                        held[g][j] = held[g][j] - weight * heads[j - k - 1]
        for b in range(count):
            pivots[b].append(found[b])
    return [jnp.concatenate([rows[b][g] * lax.rsqrt(pivots[b][g]) for g in range(groups)], axis=0) for b in range(count)]


def factor_kernel(peers, spot_ref, *refs):
    gram_refs, (image_ref, out_ref, inverse_ref, upper_ref) = refs[:peers], refs[peers:]
    count, n = inverse_ref.shape[0], inverse_ref.shape[1]
    every = range(count)
    put_blocks(gram_refs, inverse_ref.at[0], spot_ref[1])
    inverse_ref[1] = image_ref[...]
    row_id = lax.broadcasted_iota(jnp.int32, (n, n), 0)
    col_id = lax.broadcasted_iota(jnp.int32, (n, n), 1)
    panel_col = lax.broadcasted_iota(jnp.int32, (BASE, n), 1)
    lane = lax.broadcasted_iota(jnp.int32, (BASE, LANES), 1)
    low = lax.broadcasted_iota(jnp.int32, (BASE, LANES), 0)

    def place(half, start):
        rest = [jnp.zeros((BASE, LANES), jnp.float32)] * (n // LANES - 1)
        return pltpu.roll(jnp.concatenate([jnp.where(lane < BASE, half, 0.0)] + rest, axis=1), start, 1)

    def step(t, carry):
        start = pl.multiple_of(t * BASE, BASE)
        back = jnp.where(t == 0, 0, n - start)
        panel = [inverse_ref[b, pl.ds(start, BASE), :] for b in every]
        whole = [inverse_ref[b] for b in every]
        block = [pltpu.roll(panel[b], back, 1)[:, :LANES] for b in every]
        block = [jnp.where(lane < BASE, block[b], jnp.where(lane - BASE == low, 1.0, 0.0)) for b in every]
        done = factor_blocks(block)
        inv = [pltpu.roll(done[b], LANES - BASE, 1) for b in every]
        inv_placed = [place(inv[b], start) for b in every]
        up_placed = place(done[0], start)
        inside = (panel_col >= start) & (panel_col < start + BASE)
        rows = [jnp.where(inside, inv_placed[b], highest(inv[b][:, :BASE], panel[b])) for b in every]
        below = [jnp.where(row_id[:, :BASE] >= start + BASE, highest(whole[b], inv_placed[b], 1, 1), 0.0) for b in every]
        spent = (row_id >= start + BASE) & (col_id >= start) & (col_id < start + BASE)
        left = [jnp.where(spent, 0.0, whole[b]) - highest(below[b], rows[b]) for b in every]
        for b in every:
            inverse_ref[b] = left[b]
        for b in every:
            inverse_ref[b, pl.ds(start, BASE), :] = rows[b]
        upper_ref[pl.ds(start, BASE), :] = jnp.where(inside, up_placed, jnp.where(panel_col >= start + BASE, rows[0], 0.0))
        return carry

    lax.fori_loop(0, n // BASE, step, 0)
    out_ref[0] = jnp.where(row_id >= col_id, inverse_ref[0], 0.0)
    upper = jnp.where(row_id <= col_id, upper_ref[...], 0.0)
    image = jnp.where(row_id >= col_id, inverse_ref[1], 0.0)
    out_ref[1] = highest(highest(upper, image, 1, 1), image)


def factor_grams(spot, grams, image_gram):
    n = image_gram.shape[0]
    return call(
        functools.partial(factor_kernel, len(grams)), float_shape(2, n, n), [SCALAR] + [WHOLE] * (len(grams) + 1), WHOLE,
        [pltpu.VMEM((2, n, n), jnp.float32), pltpu.VMEM((n, n), jnp.float32)],
        flops=n * n * n * 400,
    )(spot, *grams, image_gram)


def basis_kernel(columns, lines_at, spot_ref, own_ref, other_ref, range_ref, co_ref, range_out_ref, co_out_ref, range_held_ref, co_held_ref, range_done_ref, co_done_ref, range_sem, co_sem, range_out_sem, co_out_sem):
    lines, rows, _ = range_held_ref.shape
    cells, _, width = co_held_ref.shape
    ranges = [pltpu.make_async_copy(range_ref.at[f], range_held_ref.at[f], range_sem.at[f]) for f in range(lines)]
    ranges_out = [pltpu.make_async_copy(range_done_ref.at[f], range_out_ref.at[pl.ds(lines_at[f] * rows, rows)], range_out_sem.at[f]) for f in range(lines)]
    cos = [pltpu.make_async_copy(co_ref.at[f], co_held_ref.at[f], co_sem.at[f]) for f in range(cells)]
    cos_out = [pltpu.make_async_copy(co_done_ref.at[f], co_out_ref.at[:, pl.ds(columns[f] * width, width)], co_out_sem.at[f]) for f in range(cells)]
    core = spot_ref[0]
    for copy in ranges + cos:
        copy.start()
    first = core == 0
    left = split(jnp.where(first, own_ref[0], other_ref[0]))
    right = split(jnp.where(first, other_ref[0], own_ref[0]))
    for f, copy in enumerate(ranges):
        copy.wait()
        range_done_ref[f] = parts_dot(split(range_held_ref[f]), left, 1, 1)
        ranges_out[f].start()
    for f, copy in enumerate(cos):
        copy.wait()
        co_done_ref[f] = parts_dot(right, split(co_held_ref[f]))
        cos_out[f].start()
    for copy in ranges_out + cos_out:
        copy.wait()


def bases(spot, own, other, range_all, co_all, columns, lines_at):
    lines, rows, k = range_all.shape
    cells, count, width = co_all.shape
    range_held, co_held = pltpu.VMEM(range_all.shape, jnp.float32), pltpu.VMEM(co_all.shape, jnp.float32)
    line_sem, cell_sem = pltpu.SemaphoreType.DMA((lines,)), pltpu.SemaphoreType.DMA((cells,))
    return call(
        functools.partial(basis_kernel, columns, lines_at), (float_shape(lines * rows, k), float_shape(count, cells * width)),
        [SCALAR, WHOLE, WHOLE, OUTSIDE, OUTSIDE], (OUTSIDE, OUTSIDE),
        [range_held, co_held, range_held, co_held, line_sem, cell_sem, line_sem, cell_sem],
        flops=18 * lines * rows * k * k, limit=56,
    )(spot, own, other, range_all, co_all)


def finish_kernel(scale, spot_ref, own_ref, other_ref, middle_own_ref, middle_other_ref, out_ref, middle_ref):
    core, place = spot_ref[0], spot_ref[1]
    half = middle_ref.shape[0] // 2
    chips, extent = middle_own_ref.shape[0], middle_own_ref.shape[1]
    for side, ref in ((core, middle_own_ref), (1 - core, middle_other_ref)):
        for i in range(chips):
            middle_ref[pl.ds(pl.multiple_of(side * half + (place ^ i) * extent, extent), extent), :] = ref[i]
    left = jnp.where(core == 0, own_ref[1], other_ref[1])
    right = jnp.where(core == 0, other_ref[1], own_ref[1])
    out_ref[...] = highest(highest(left, middle_ref[...]), right, 1, 1) * scale


def finish(spot, own, other, middle_own, middle_other, scale):
    k = own.shape[1]
    return call(
        functools.partial(finish_kernel, scale), float_shape(k, k), [SCALAR] + [WHOLE] * 4, WHOLE,
        [pltpu.VMEM((k, k), jnp.float32)], flops=24 * k * k * k,
    )(spot, own, other, middle_own, middle_other)


def per_device(window, range_test, co_test, core_left, core_right):
    rows_total = window.shape[0] * lax.axis_size("cell")
    cols_total = window.shape[1] * lax.axis_size("tm")
    k = range_test.shape[1]
    chips = lax.axis_size("cell") // 2
    groups = groups_of("cell", 1, 2)
    line_groups = groups_of("tm", 0, 2)
    spot = jnp.stack([lax.axis_index("cell") & 1, place_of(groups, lax.axis_index("cell")), place_of(line_groups[:1], lax.axis_index("tm"))]).astype(jnp.int32)
    columns = [(cell & 1) * chips + place_of(groups, cell) for cell in range(2 * chips)]

    lines_at = [place_of(line_groups, line) for line in range(lax.axis_size("tm"))]

    def core_swap(values):
        return swap(values, "cell", 1)

    r3, r2, r1, r0, sent, kept = sketch_terms(spot, chips, window, range_test, co_test, core_left, core_right)
    far = swap(r3, "tm", 1)
    near = swap(r1, "tm", 1)
    pack = kept + core_swap(sent)
    handed = r2 + far
    sketch_z = core_terms(after(spot, pack, handed), window, core_right, core_left)
    pack = scatter_sum(pack, groups)[0]
    handed, near, pack, sketch_z = lax.optimization_barrier((swap(handed, "tm", 2), near, pack, sketch_z))
    range_piece = (r0 + near + handed).reshape(lax.axis_size("tm") // 4, -1, r0.shape[1])
    if line_groups[1:]:
        rest = place_of(line_groups[1:], lax.axis_index("tm"))
        range_piece = jnp.stack([lax.dynamic_index_in_dim(range_piece, rest ^ f, 0, False) for f in range(range_piece.shape[0])])
    range_piece = scatter_sum(range_piece, line_groups[1:])[0]
    width = window.shape[1] // (2 * chips)
    packed = pack_width(co_test.shape[0], width, k)
    co_piece = pack[:packed].reshape(packed, -1, width).swapaxes(0, 1).reshape(-1, width)
    fold = pack[None, packed:]
    range_all = lax.all_gather(range_piece, "tm", axis=0)
    co_all = lax.all_gather(co_piece, "cell", axis=0)

    gram_sent, gram_kept = gram_terms(spot, chips, range_piece, co_piece, (rows_total, cols_total))
    gram = scatter_sum(gram_kept + core_swap(gram_sent), groups)
    gram = whole_sum(gram, "tm")
    grams = gather(gram, groups)

    fold = jnp.concatenate(gather(whole_sum(fold, "tm"), groups))
    middle_sent, middle_kept, image_gram = middle_terms(spot, chips, sketch_z, fold, core_swap(fold))
    middle = whole_sum(scatter_sum(middle_kept + core_swap(middle_sent), groups), "tm")
    middle = jnp.concatenate(gather(middle, groups))
    middle_other = core_swap(middle)

    own = factor_grams(spot, grams, image_gram)
    other = core_swap(own)
    range_basis, co_basis = bases(spot, own, other, range_all, co_all, columns, lines_at)
    core_out = finish(spot, own, other, middle, middle_other, math.sqrt(rows_total * cols_total))
    return (range_basis, co_basis, core_out)


def solution(mesh):
    return jax.shard_map(
        per_device,
        mesh=mesh,
        in_specs=(P("cell", "tm"), P("tm", None), P(None, "cell"), P(None, "cell"), P(None, "tm")),
        out_specs=(P("cell", None), P(None, "tm"), P()),
        check_vma=False,
    )
```

```python
import functools
import math

import jax
import jax.numpy as jnp
from jax import lax
from jax.experimental import pallas as pl
from jax.experimental.pallas import tpu as pltpu
from jax.sharding import PartitionSpec as P

BASE = 64
LANES = 128
SUBLANES = 8
TILES = 4
WHOLE = pl.BlockSpec(memory_space=pltpu.VMEM)
SCALAR = pl.BlockSpec(memory_space=pltpu.SMEM)
OUTSIDE = pl.BlockSpec(memory_space=pl.ANY)


def highest(left, right, left_dim=1, right_dim=0):
    dims = (((left_dim,), (right_dim,)), ((), ()))
    return lax.dot_general(left, right, dims, precision=lax.Precision.HIGHEST, preferred_element_type=jnp.float32)


def split(values):
    top = values.astype(jnp.bfloat16)
    return top, (values - top.astype(jnp.float32)).astype(jnp.bfloat16)


def parts_dot(left, right, left_dim=1, right_dim=0):
    dims = (((left_dim,), (right_dim,)), ((), ()))
    pairs = ((left[0], right[0]), (left[0], right[1]), (left[1], right[0]))
    return sum(lax.dot_general(a, b, dims, preferred_element_type=jnp.float32) for a, b in pairs)


def float_shape(*shape):
    return jax.ShapeDtypeStruct(shape, jnp.float32)


def call(kernel, out_shape, in_specs, out_specs, scratch=(), flops=0, limit=24):
    return pl.pallas_call(
        kernel,
        out_shape=out_shape,
        in_specs=in_specs,
        out_specs=out_specs,
        scratch_shapes=list(scratch),
        compiler_params=pltpu.CompilerParams(vmem_limit_bytes=limit * 1024 * 1024),
        cost_estimate=pl.CostEstimate(flops=flops, bytes_accessed=4 * 1024 * 1024, transcendentals=0),
    )


def bits_of(axis):
    return int(math.log2(lax.axis_size(axis)))


def groups_of(axis, first, width):
    bits = list(range(first, bits_of(axis)))
    return [(axis, tuple(bits[i:i + width])) for i in range(0, len(bits), width)]


def place_of(groups, index):
    place = 0
    for _, bits in groups:
        place = (place << len(bits)) + sum(((index >> bit) & 1) << i for i, bit in enumerate(bits))
    return place


def swap(values, axis, mask):
    return lax.ppermute(values, axis, [(i, i ^ mask) for i in range(lax.axis_size(axis))])


def masks_of(bits):
    return [sum(((peer >> i) & 1) << bit for i, bit in enumerate(bits)) for peer in range(1 << len(bits))]


def pair_sum(parts):
    while len(parts) > 1:
        parts = [parts[i] + parts[i + 1] for i in range(0, len(parts), 2)]
    return parts[0]


def scatter_sum(blocks, groups):
    for axis, bits in groups:
        count = blocks.shape[0] >> len(bits)
        parts = [blocks[peer * count:(peer + 1) * count] for peer in range(1 << len(bits))]
        blocks = pair_sum([parts[0]] + [swap(part, axis, mask) for part, mask in zip(parts[1:], masks_of(bits)[1:])])
    return blocks


def gather(blocks, groups):
    parts = [blocks]
    for axis, bits in reversed(groups):
        blocks = jnp.concatenate(parts) if len(parts) > 1 else parts[0]
        parts = [blocks] + [swap(blocks, axis, mask) for mask in masks_of(bits)[1:]]
    return parts


def whole_sum(values, axis):
    for bit in range(bits_of(axis)):
        values = values + swap(values, axis, 1 << bit)
    return values


def after(values, *earlier):
    return lax.optimization_barrier((values,) + earlier)[0]


def block_start(place, block, extent):
    return pl.multiple_of((place ^ block) * extent, extent)


def put_blocks(refs, out_ref, place):
    count, extent = refs[0].shape[0], refs[0].shape[1]
    for i, ref in enumerate(refs):
        for j in range(count):
            out_ref[pl.ds(block_start(place, i * count + j, extent), extent), :] = ref[j]


def take_blocks(ref, out_ref, place, base=0):
    count, extent = out_ref.shape[0], out_ref.shape[1]
    for i in range(count):
        out_ref[i] = ref[pl.ds(pl.multiple_of(base + (place ^ i) * extent, extent), extent), :]


def pack_width(count, width, k):
    return count * width // k


def sketch_kernel(spot_ref, window_ref, test_ref, co_ref, left_ref, right_ref, r3_ref, r2_ref, r1_ref, r0_ref, sent_ref, kept_ref, held_ref, test_held_ref, co_held_ref, left_held_ref, right_held_ref, top_ref, rest_ref, co_done_ref, lt_ref, rt_ref, window_sem, sem):
    core, place, line = spot_ref[0], spot_ref[1], spot_ref[2]
    tile = held_ref.shape[1]
    chips, _, k = kept_ref.shape
    count, cols = co_done_ref.shape
    width = cols // (2 * chips)
    packed = pack_width(count, width, k)
    small = [(test_ref, test_held_ref), (co_ref, co_held_ref), (left_ref, left_held_ref), (right_ref, right_held_ref)]
    small = [pltpu.make_async_copy(a, b, sem.at[i]) for i, (a, b) in enumerate(small)]

    def window_copy(i):
        return pltpu.make_async_copy(window_ref.at[pl.ds(block_start(line, TILES - 1 - i, tile), tile)], held_ref.at[i], window_sem.at[i])

    small[0].start()
    window_copy(0).start()
    small[1].start()
    small[2].start()
    for i in range(1, TILES):
        window_copy(i).start()
    small[3].start()
    co_done_ref[...] = jnp.zeros_like(co_done_ref)
    lt_ref[...] = jnp.zeros_like(lt_ref)
    small[0].wait()
    top_ref[...], rest_ref[...] = split(test_held_ref[...])
    small[1].wait()
    small[2].wait()

    def step(i, carry):
        window_copy(i).wait()
        rows = split(held_ref[i])
        spot = pl.ds(block_start(line, TILES - 1 - i, tile), tile)
        done = parts_dot(rows, (top_ref[...], rest_ref[...]))
        co_done_ref[...] += parts_dot(split(co_held_ref[:, spot]), rows)
        lt_ref[...] += parts_dot(split(left_held_ref[:, spot]), split(done))
        for block, ref in enumerate((r3_ref, r2_ref, r1_ref, r0_ref)):
            @pl.when(i == block)
            def _():
                ref[...] = done

        return carry

    lax.fori_loop(0, TILES, step, 0)
    small[3].wait()
    rt_ref[...] = parts_dot(split(right_held_ref[...]), split(co_done_ref[...]), 1, 1)
    for ref, side in ((sent_ref, 1 - core), (kept_ref, core)):
        for i in range(chips):
            start = pl.multiple_of((side * chips + (place ^ i)) * width, width)
            for j in range(count // packed):
                ref[i, :packed, j * width:(j + 1) * width] = co_done_ref[j * packed:(j + 1) * packed, pl.ds(start, width)]
    for owner, left_out, right_out in ((0, kept_ref, sent_ref), (1, sent_ref, kept_ref)):
        @pl.when(core == owner)
        def _():
            take_blocks(lt_ref, left_out.at[:, packed:], place)
            take_blocks(rt_ref, right_out.at[:, packed:], place)


def sketch_terms(spot, chips, window, range_test, co_test, core_left, core_right):
    rows, cols = window.shape
    count, k, s_core = co_test.shape[0], range_test.shape[1], core_left.shape[0]
    block = pack_width(count, cols // (2 * chips), k) + s_core // chips
    return call(
        sketch_kernel, (float_shape(rows // TILES, k),) * 4 + (float_shape(chips, block, k),) * 2,
        [SCALAR] + [OUTSIDE] * 5, (WHOLE,) * 6,
        [
            pltpu.VMEM((TILES, rows // TILES, cols), jnp.float32), pltpu.VMEM((cols, k), jnp.float32), pltpu.VMEM((count, rows), jnp.float32),
            pltpu.VMEM((s_core, rows), jnp.float32), pltpu.VMEM((s_core, cols), jnp.float32),
            pltpu.VMEM((cols, k), jnp.bfloat16), pltpu.VMEM((cols, k), jnp.bfloat16),
            pltpu.VMEM((count, cols), jnp.float32), pltpu.VMEM((s_core, k), jnp.float32), pltpu.VMEM((s_core, k), jnp.float32),
            pltpu.SemaphoreType.DMA((TILES,)), pltpu.SemaphoreType.DMA((4,)),
        ],
        flops=12 * rows * cols * count, limit=56,
    )(spot, window, range_test, co_test, core_left, core_right)


def core_kernel(spot_ref, window_ref, right_ref, left_ref, z_ref, held_ref, right_held_ref, left_held_ref, image_ref, window_sem, right_sem, left_sem):
    width = held_ref.shape[2]
    tile = window_ref.shape[0] // TILES
    left_copy = pltpu.make_async_copy(left_ref, left_held_ref, left_sem)

    def copies(i):
        start = pl.multiple_of(i * width, width)
        return (
            pltpu.make_async_copy(right_ref.at[:, pl.ds(start, width)], right_held_ref.at[i], right_sem.at[i]),
            pltpu.make_async_copy(window_ref.at[:, pl.ds(start, width)], held_ref.at[i], window_sem.at[i]),
        )

    for i in range(TILES):
        for copy in copies(i):
            copy.start()
    left_copy.start()
    image_ref[...] = jnp.zeros_like(image_ref)

    def step(i, carry):
        for copy in copies(i):
            copy.wait()
        image_ref[...] += parts_dot(split(held_ref[i]), split(right_held_ref[i]), 1, 1)
        return carry

    lax.fori_loop(0, TILES, step, 0)
    left_copy.wait()
    z_ref[...] = jnp.zeros_like(z_ref)

    def fold(i, carry):
        start = pl.multiple_of(i * tile, tile)
        z_ref[...] += parts_dot(split(left_held_ref[:, pl.ds(start, tile)]), split(image_ref[pl.ds(start, tile), :]))
        return carry

    lax.fori_loop(0, TILES, fold, 0)


def core_terms(spot, window, core_right, core_left):
    rows, cols = window.shape
    s_core = core_right.shape[0]
    return call(
        core_kernel, float_shape(s_core, s_core), [SCALAR] + [OUTSIDE] * 3, WHOLE,
        [
            pltpu.VMEM((TILES, rows, cols // TILES), jnp.float32), pltpu.VMEM((TILES, s_core, cols // TILES), jnp.float32),
            pltpu.VMEM((s_core, rows), jnp.float32), pltpu.VMEM((rows, s_core), jnp.float32),
            pltpu.SemaphoreType.DMA((TILES,)), pltpu.SemaphoreType.DMA((TILES,)), pltpu.SemaphoreType.DMA,
        ],
        flops=9 * rows * cols * s_core, limit=56,
    )(spot, window, core_right, core_left)


def gram_kernel(scales, spot_ref, range_ref, co_ref, sent_ref, kept_ref, y_ref, w_ref):
    y_ref[...] = highest(range_ref[...], range_ref[...], 0, 0) / scales[0]
    w_ref[...] = highest(co_ref[...], co_ref[...], 1, 1) / scales[1]
    for owner, y_out, w_out in ((0, kept_ref, sent_ref), (1, sent_ref, kept_ref)):
        @pl.when(spot_ref[0] == owner)
        def _():
            take_blocks(y_ref, y_out, spot_ref[1])
            take_blocks(w_ref, w_out, spot_ref[1])


def gram_terms(spot, chips, range_piece, co_piece, scales):
    k = range_piece.shape[1]
    square = pltpu.VMEM((k, k), jnp.float32)
    return call(
        functools.partial(gram_kernel, scales), (float_shape(chips, k // chips, k),) * 2, [SCALAR, WHOLE, WHOLE], (WHOLE, WHOLE),
        [square, square], flops=24 * k * k * k,
    )(spot, range_piece, co_piece)


def middle_kernel(spot_ref, z_ref, own_ref, other_ref, sent_ref, kept_ref, gram_ref, left_ref, right_ref, middle_ref):
    core, place = spot_ref[0], spot_ref[1]
    for owner, left_in, right_in in ((0, own_ref, other_ref), (1, other_ref, own_ref)):
        @pl.when(core == owner)
        def _():
            put_blocks([left_in], left_ref, place)
            put_blocks([right_in], right_ref, place)

    first = core == 0
    own = jnp.where(first, left_ref[...], right_ref[...])
    gram_ref[...] = highest(own, own, 0, 0)
    middle_ref[...] = parts_dot(split(parts_dot(split(left_ref[...]), split(z_ref[...]), 0, 0)), split(right_ref[...]))
    half = middle_ref.shape[0] // 2
    take_blocks(middle_ref, kept_ref, place, core * half)
    take_blocks(middle_ref, sent_ref, place, (1 - core) * half)


def middle_terms(spot, chips, sketch_z, own, other):
    s_core, k = sketch_z.shape[0], own.shape[2]
    return call(
        middle_kernel, (float_shape(chips, k // (2 * chips), k),) * 2 + (float_shape(k, k),), [SCALAR] + [WHOLE] * 3, (WHOLE,) * 3,
        [pltpu.VMEM((s_core, k), jnp.float32), pltpu.VMEM((s_core, k), jnp.float32), pltpu.VMEM((k, k), jnp.float32)],
        flops=6 * k * s_core * s_core,
    )(spot, sketch_z, own, other)


def spread_lane(values, lane):
    return jnp.broadcast_to(values[:, lane:lane + 1], values.shape)


def spread_row(values, row):
    return jnp.broadcast_to(values[row:row + 1, :], values.shape)


def factor_blocks(blocks):
    count = len(blocks)
    groups = BASE // SUBLANES
    rows = [[x[SUBLANES * g:SUBLANES * (g + 1)] for g in range(groups)] for x in blocks]
    sub = lax.broadcasted_iota(jnp.int32, (SUBLANES, LANES), 0)
    pivots = [[] for _ in blocks]
    for p in range(groups):
        cols = [{g: [spread_lane(rows[b][g], SUBLANES * p + k) for k in range(SUBLANES)] for g in range(p, groups)} for b in range(count)]
        found = [jnp.zeros((SUBLANES, LANES), jnp.float32)] * count
        for k in range(SUBLANES):
            for b in range(count):
                held = cols[b]
                pivot = spread_row(held[p][k], k)
                found[b] = jnp.where(sub == k, pivot, found[b])
                scale = 1.0 / pivot
                pivot_row = spread_row(rows[b][p], k)
                heads = [spread_row(held[p][j], k) for j in range(k + 1, SUBLANES)]
                for g in range(p, groups):
                    weight = held[g][k] * scale
                    if g == p:
                        weight = jnp.where(sub > k, weight, 0.0)
                    rows[b][g] = rows[b][g] - weight * pivot_row
                    for j in range(k + 1, SUBLANES):
                        held[g][j] = held[g][j] - weight * heads[j - k - 1]
        for b in range(count):
            pivots[b].append(found[b])
    return [jnp.concatenate([rows[b][g] * lax.rsqrt(pivots[b][g]) for g in range(groups)], axis=0) for b in range(count)]


def factor_steps(steps, inverse_ref, upper_ref):
    count, n = inverse_ref.shape[0], inverse_ref.shape[1]
    every = range(count)
    row_id = lax.broadcasted_iota(jnp.int32, (n, n), 0)
    col_id = lax.broadcasted_iota(jnp.int32, (n, n), 1)
    panel_col = lax.broadcasted_iota(jnp.int32, (BASE, n), 1)
    lane = lax.broadcasted_iota(jnp.int32, (BASE, LANES), 1)
    low = lax.broadcasted_iota(jnp.int32, (BASE, LANES), 0)

    def place(half, start):
        rest = [jnp.zeros((BASE, LANES), jnp.float32)] * (n // LANES - 1)
        return pltpu.roll(jnp.concatenate([jnp.where(lane < BASE, half, 0.0)] + rest, axis=1), start, 1)

    def step(t, carry):
        start = pl.multiple_of(t * BASE, BASE)
        back = jnp.where(t == 0, 0, n - start)
        panel = [inverse_ref[b, pl.ds(start, BASE), :] for b in every]
        whole = [inverse_ref[b] for b in every]
        block = [pltpu.roll(panel[b], back, 1)[:, :LANES] for b in every]
        block = [jnp.where(lane < BASE, block[b], jnp.where(lane - BASE == low, 1.0, 0.0)) for b in every]
        done = factor_blocks(block)
        inv = [pltpu.roll(done[b], LANES - BASE, 1) for b in every]
        inv_placed = [place(inv[b], start) for b in every]
        up_placed = place(done[0], start)
        inside = (panel_col >= start) & (panel_col < start + BASE)
        rows = [jnp.where(inside, inv_placed[b], highest(inv[b][:, :BASE], panel[b])) for b in every]
        below = [jnp.where(row_id[:, :BASE] >= start + BASE, highest(whole[b], inv_placed[b], 1, 1), 0.0) for b in every]
        spent = (row_id >= start + BASE) & (col_id >= start) & (col_id < start + BASE)
        left = [jnp.where(spent, 0.0, whole[b]) - highest(below[b], rows[b]) for b in every]
        for b in every:
            inverse_ref[b] = left[b]
        for b in every:
            inverse_ref[b, pl.ds(start, BASE), :] = rows[b]
        upper_ref[pl.ds(start, BASE), :] = jnp.where(inside, up_placed, jnp.where(panel_col >= start + BASE, rows[0], 0.0))
        return carry

    lax.fori_loop(steps[0], steps[1], step, 0)


def factor_start_kernel(steps, peers, spot_ref, *refs):
    gram_refs, (image_ref, inverse_ref, upper_ref) = refs[:peers], refs[peers:]
    put_blocks(gram_refs, inverse_ref.at[0], spot_ref[1])
    inverse_ref[1] = image_ref[...]
    upper_ref[...] = jnp.zeros_like(upper_ref)
    factor_steps(steps, inverse_ref, upper_ref)


def factor_end_kernel(steps, begun_ref, begun_upper_ref, out_ref, inverse_ref, upper_ref):
    n = upper_ref.shape[0]
    inverse_ref[...] = begun_ref[...]
    upper_ref[...] = begun_upper_ref[...]
    factor_steps(steps, inverse_ref, upper_ref)
    row_id = lax.broadcasted_iota(jnp.int32, (n, n), 0)
    col_id = lax.broadcasted_iota(jnp.int32, (n, n), 1)
    out_ref[0] = jnp.where(row_id >= col_id, inverse_ref[0], 0.0)
    upper = jnp.where(row_id <= col_id, upper_ref[...], 0.0)
    image = jnp.where(row_id >= col_id, inverse_ref[1], 0.0)
    out_ref[1] = highest(highest(upper, image, 1, 1), image)


def factor_start(spot, grams, image_gram):
    n = image_gram.shape[0]
    return call(
        functools.partial(factor_start_kernel, (0, n // BASE // 2), len(grams)), (float_shape(2, n, n), float_shape(n, n)),
        [SCALAR] + [WHOLE] * (len(grams) + 1), (WHOLE, WHOLE), flops=n * n * n * 200,
    )(spot, *grams, image_gram)


def factor_end(begun, upper):
    n = upper.shape[0]
    return call(
        functools.partial(factor_end_kernel, (n // BASE // 2, n // BASE)), float_shape(2, n, n), [WHOLE, WHOLE], WHOLE,
        [pltpu.VMEM((2, n, n), jnp.float32), pltpu.VMEM((n, n), jnp.float32)], flops=n * n * n * 200,
    )(begun, upper)


def basis_kernel(spot_ref, at_ref, own_ref, other_ref, range_ref, co_ref, range_out_ref, co_out_ref, range_held_ref, co_held_ref, range_done_ref, co_done_ref, side_ref, range_sem, co_sem, range_out_sem, co_out_sem):
    lines, rows, _ = range_held_ref.shape
    cells, _, width = co_held_ref.shape

    def range_copy(f):
        return pltpu.make_async_copy(range_ref.at[f], range_held_ref.at[f], range_sem.at[f])

    def co_copy(f):
        return pltpu.make_async_copy(co_ref.at[f], co_held_ref.at[f], co_sem.at[f])

    def range_out(f):
        start = pl.multiple_of(at_ref[f] * rows, rows)
        return pltpu.make_async_copy(range_done_ref.at[f], range_out_ref.at[pl.ds(start, rows)], range_out_sem.at[f])

    def co_out(f):
        start = pl.multiple_of(at_ref[lines + f] * width, width)
        return pltpu.make_async_copy(co_done_ref.at[f], co_out_ref.at[:, pl.ds(start, width)], co_out_sem.at[f])

    for f in range(lines):
        range_copy(f).start()
    for f in range(cells):
        co_copy(f).start()
    first = spot_ref[0] == 0
    side_ref[0], side_ref[1] = split(jnp.where(first, own_ref[0], other_ref[0]))
    side_ref[2], side_ref[3] = split(jnp.where(first, other_ref[0], own_ref[0]))

    def range_step(f, carry):
        range_copy(f).wait()
        range_done_ref[f] = parts_dot(split(range_held_ref[f]), (side_ref[0], side_ref[1]), 1, 1)
        range_out(f).start()
        return carry

    def co_step(f, carry):
        co_copy(f).wait()
        co_done_ref[f] = parts_dot((side_ref[2], side_ref[3]), split(co_held_ref[f]))
        co_out(f).start()
        return carry

    lax.fori_loop(0, lines, range_step, 0)
    lax.fori_loop(0, cells, co_step, 0)
    for f in range(lines):
        range_out(f).wait()
    for f in range(cells):
        co_out(f).wait()


def bases(spot, at, own, other, range_all, co_all):
    lines, rows, k = range_all.shape
    cells, count, width = co_all.shape
    range_held, co_held = pltpu.VMEM(range_all.shape, jnp.float32), pltpu.VMEM(co_all.shape, jnp.float32)
    line_sem, cell_sem = pltpu.SemaphoreType.DMA((lines,)), pltpu.SemaphoreType.DMA((cells,))
    return call(
        basis_kernel, (float_shape(lines * rows, k), float_shape(count, cells * width)),
        [SCALAR, SCALAR, WHOLE, WHOLE, OUTSIDE, OUTSIDE], (OUTSIDE, OUTSIDE),
        [range_held, co_held, range_held, co_held, pltpu.VMEM((4, k, k), jnp.bfloat16), line_sem, cell_sem, line_sem, cell_sem],
        flops=18 * lines * rows * k * k, limit=56,
    )(spot, at, own, other, range_all, co_all)


def finish_kernel(scale, spot_ref, own_ref, other_ref, middle_own_ref, middle_other_ref, out_ref, middle_ref):
    core, place = spot_ref[0], spot_ref[1]
    half = middle_ref.shape[0] // 2
    chips, extent = middle_own_ref.shape[0], middle_own_ref.shape[1]
    for side, ref in ((core, middle_own_ref), (1 - core, middle_other_ref)):
        for i in range(chips):
            middle_ref[pl.ds(pl.multiple_of(side * half + (place ^ i) * extent, extent), extent), :] = ref[i]
    left = jnp.where(core == 0, own_ref[1], other_ref[1])
    right = jnp.where(core == 0, other_ref[1], own_ref[1])
    out_ref[...] = highest(highest(left, middle_ref[...]), right, 1, 1) * scale


def finish(spot, own, other, middle_own, middle_other, scale):
    k = own.shape[1]
    return call(
        functools.partial(finish_kernel, scale), float_shape(k, k), [SCALAR] + [WHOLE] * 4, WHOLE,
        [pltpu.VMEM((k, k), jnp.float32)], flops=24 * k * k * k,
    )(spot, own, other, middle_own, middle_other)


def per_device(window, range_test, co_test, core_left, core_right):
    rows_total = window.shape[0] * lax.axis_size("cell")
    cols_total = window.shape[1] * lax.axis_size("tm")
    k = range_test.shape[1]
    chips = lax.axis_size("cell") // 2
    groups = groups_of("cell", 1, 2)
    line_groups = groups_of("tm", 0, 2)
    spot = jnp.stack([lax.axis_index("cell") & 1, place_of(groups, lax.axis_index("cell")), place_of(line_groups[:1], lax.axis_index("tm"))]).astype(jnp.int32)
    at = [place_of(line_groups, line) for line in range(lax.axis_size("tm"))]
    at = jnp.array(at + [(cell & 1) * chips + place_of(groups, cell) for cell in range(2 * chips)], jnp.int32)

    def core_swap(values):
        return swap(values, "cell", 1)

    r3, r2, r1, r0, sent, kept = sketch_terms(spot, chips, window, range_test, co_test, core_left, core_right)
    far = swap(r3, "tm", 1)
    near = swap(r1, "tm", 1)
    pack = kept + core_swap(sent)
    handed = r2 + after(far, pack)
    sketch_z = core_terms(after(spot, pack, handed), window, core_right, core_left)
    pack = scatter_sum(pack, groups)[0]
    handed, near, pack, sketch_z = lax.optimization_barrier((swap(handed, "tm", 2), near, pack, sketch_z))
    range_piece = (r0 + near + handed).reshape(lax.axis_size("tm") // 4, -1, r0.shape[1])
    if line_groups[1:]:
        rest = place_of(line_groups[1:], lax.axis_index("tm"))
        range_piece = jnp.stack([lax.dynamic_index_in_dim(range_piece, rest ^ f, 0, False) for f in range(range_piece.shape[0])])
    range_piece = scatter_sum(range_piece, line_groups[1:])[0]
    width = window.shape[1] // (2 * chips)
    packed = pack_width(co_test.shape[0], width, k)
    co_piece = pack[:packed].reshape(packed, -1, width).swapaxes(0, 1).reshape(-1, width)
    fold = pack[None, packed:]
    co_all = lax.all_gather(co_piece, "cell", axis=0)

    gram_sent, gram_kept = gram_terms(spot, chips, range_piece, co_piece, (rows_total, cols_total))
    gram = whole_sum(scatter_sum(gram_kept + core_swap(gram_sent), groups), "tm")
    fold = whole_sum(fold, "tm")
    range_all = lax.all_gather(after(range_piece, gram, fold), "tm", axis=0)
    grams = gather(gram, groups)
    fold = jnp.concatenate(gather(fold, groups))
    middle_sent, middle_kept, image_gram = middle_terms(spot, chips, sketch_z, fold, core_swap(fold))
    middle = scatter_sum(middle_kept + core_swap(middle_sent), groups)

    image_gram, middle = lax.optimization_barrier((image_gram, middle))
    begun, upper = factor_start(spot, grams, image_gram)
    for bit in range(bits_of("tm")):
        middle = middle + swap(middle, "tm", 1 << bit)
        if bit == 0:
            middle, begun, upper = lax.optimization_barrier((middle, begun, upper))
    own = factor_end(begun, upper)
    middle, own = lax.optimization_barrier((middle, own))
    middle = jnp.concatenate(gather(middle, groups))
    middle_other = core_swap(middle)
    other = core_swap(own)
    range_basis, co_basis = bases(spot, at, own, other, range_all, co_all)
    core_out = finish(spot, own, other, middle, middle_other, math.sqrt(rows_total * cols_total))
    return (range_basis, co_basis, core_out)


def solution(mesh):
    return jax.shard_map(
        per_device,
        mesh=mesh,
        in_specs=(P("cell", "tm"), P("tm", None), P(None, "cell"), P(None, "cell"), P(None, "tm")),
        out_specs=(P("cell", None), P(None, "tm"), P()),
        check_vma=False,
    )
```

```python
import functools
import math

import jax
import jax.numpy as jnp
from jax import lax
from jax.experimental import pallas as pl
from jax.experimental.pallas import tpu as pltpu
from jax.sharding import PartitionSpec as P

BASE = 64
LANES = 128
SUBLANES = 8
TILES = 4
WHOLE = pl.BlockSpec(memory_space=pltpu.VMEM)
SCALAR = pl.BlockSpec(memory_space=pltpu.SMEM)
OUTSIDE = pl.BlockSpec(memory_space=pl.ANY)


def highest(left, right, left_dim=1, right_dim=0):
    dims = (((left_dim,), (right_dim,)), ((), ()))
    return lax.dot_general(left, right, dims, precision=lax.Precision.HIGHEST, preferred_element_type=jnp.float32)


def split(values):
    top = values.astype(jnp.bfloat16)
    return top, (values - top.astype(jnp.float32)).astype(jnp.bfloat16)


def parts_dot(left, right, left_dim=1, right_dim=0):
    dims = (((left_dim,), (right_dim,)), ((), ()))
    pairs = ((left[0], right[0]), (left[0], right[1]), (left[1], right[0]))
    return sum(lax.dot_general(a, b, dims, preferred_element_type=jnp.float32) for a, b in pairs)


def float_shape(*shape):
    return jax.ShapeDtypeStruct(shape, jnp.float32)


def call(kernel, out_shape, in_specs, out_specs, scratch=(), flops=0, limit=24):
    return pl.pallas_call(
        kernel,
        out_shape=out_shape,
        in_specs=in_specs,
        out_specs=out_specs,
        scratch_shapes=list(scratch),
        compiler_params=pltpu.CompilerParams(vmem_limit_bytes=limit * 1024 * 1024),
        cost_estimate=pl.CostEstimate(flops=flops, bytes_accessed=4 * 1024 * 1024, transcendentals=0),
    )


def bits_of(axis):
    return int(math.log2(lax.axis_size(axis)))


def groups_of(axis, first, width):
    bits = list(range(first, bits_of(axis)))
    return [(axis, tuple(bits[i:i + width])) for i in range(0, len(bits), width)]


def place_of(groups, index):
    place = 0
    for _, bits in groups:
        place = (place << len(bits)) + sum(((index >> bit) & 1) << i for i, bit in enumerate(bits))
    return place


def swap(values, axis, mask):
    return lax.ppermute(values, axis, [(i, i ^ mask) for i in range(lax.axis_size(axis))])


def masks_of(bits):
    return [sum(((peer >> i) & 1) << bit for i, bit in enumerate(bits)) for peer in range(1 << len(bits))]


def pair_sum(parts):
    while len(parts) > 1:
        parts = [parts[i] + parts[i + 1] for i in range(0, len(parts), 2)]
    return parts[0]


def scatter_sum(blocks, groups):
    for axis, bits in groups:
        count = blocks.shape[0] >> len(bits)
        parts = [blocks[peer * count:(peer + 1) * count] for peer in range(1 << len(bits))]
        blocks = pair_sum([parts[0]] + [swap(part, axis, mask) for part, mask in zip(parts[1:], masks_of(bits)[1:])])
    return blocks


def gather(blocks, groups):
    parts = [blocks]
    for axis, bits in reversed(groups):
        blocks = jnp.concatenate(parts) if len(parts) > 1 else parts[0]
        parts = [blocks] + [swap(blocks, axis, mask) for mask in masks_of(bits)[1:]]
    return parts


def whole_sum(values, axis):
    for bit in range(bits_of(axis)):
        values = values + swap(values, axis, 1 << bit)
    return values


def after(values, *earlier):
    return lax.optimization_barrier((values,) + earlier)[0]


def block_start(place, block, extent):
    return pl.multiple_of((place ^ block) * extent, extent)


def put_blocks(refs, out_ref, place):
    count, extent = refs[0].shape[0], refs[0].shape[1]
    for i, ref in enumerate(refs):
        for j in range(count):
            out_ref[pl.ds(block_start(place, i * count + j, extent), extent), :] = ref[j]


def take_blocks(ref, out_ref, place, base=0):
    count, extent = out_ref.shape[0], out_ref.shape[1]
    for i in range(count):
        out_ref[i] = ref[pl.ds(pl.multiple_of(base + (place ^ i) * extent, extent), extent), :]


def pack_width(count, width, k):
    return count * width // k


def sketch_kernel(spot_ref, window_ref, test_ref, co_ref, left_ref, right_ref, r3_ref, r2_ref, r1_ref, r0_ref, sent_ref, kept_ref, held_ref, test_held_ref, co_held_ref, left_held_ref, right_held_ref, top_ref, rest_ref, co_done_ref, lt_ref, rt_ref, window_sem, sem):
    core, place, line = spot_ref[0], spot_ref[1], spot_ref[2]
    tile = held_ref.shape[1]
    chips, _, k = kept_ref.shape
    count, cols = co_done_ref.shape
    width = cols // (2 * chips)
    packed = pack_width(count, width, k)
    small = [(test_ref, test_held_ref), (co_ref, co_held_ref), (left_ref, left_held_ref), (right_ref, right_held_ref)]
    small = [pltpu.make_async_copy(a, b, sem.at[i]) for i, (a, b) in enumerate(small)]

    def window_copy(i):
        return pltpu.make_async_copy(window_ref.at[pl.ds(block_start(line, TILES - 1 - i, tile), tile)], held_ref.at[i], window_sem.at[i])

    small[0].start()
    window_copy(0).start()
    small[1].start()
    small[2].start()
    for i in range(1, TILES):
        window_copy(i).start()
    small[3].start()
    co_done_ref[...] = jnp.zeros_like(co_done_ref)
    lt_ref[...] = jnp.zeros_like(lt_ref)
    small[0].wait()
    top_ref[...], rest_ref[...] = split(test_held_ref[...])
    small[1].wait()
    small[2].wait()

    def step(i, carry):
        window_copy(i).wait()
        rows = split(held_ref[i])
        spot = pl.ds(block_start(line, TILES - 1 - i, tile), tile)
        done = parts_dot(rows, (top_ref[...], rest_ref[...]))
        co_done_ref[...] += parts_dot(split(co_held_ref[:, spot]), rows)
        lt_ref[...] += parts_dot(split(left_held_ref[:, spot]), split(done))
        for block, ref in enumerate((r3_ref, r2_ref, r1_ref, r0_ref)):
            @pl.when(i == block)
            def _():
                ref[...] = done

        return carry

    lax.fori_loop(0, TILES, step, 0)
    small[3].wait()
    rt_ref[...] = parts_dot(split(right_held_ref[...]), split(co_done_ref[...]), 1, 1)
    for ref, side in ((sent_ref, 1 - core), (kept_ref, core)):
        for i in range(chips):
            start = pl.multiple_of((side * chips + (place ^ i)) * width, width)
            for j in range(count // packed):
                ref[i, :packed, j * width:(j + 1) * width] = co_done_ref[j * packed:(j + 1) * packed, pl.ds(start, width)]
    for owner, left_out, right_out in ((0, kept_ref, sent_ref), (1, sent_ref, kept_ref)):
        @pl.when(core == owner)
        def _():
            take_blocks(lt_ref, left_out.at[:, packed:], place)
            take_blocks(rt_ref, right_out.at[:, packed:], place)


def sketch_terms(spot, chips, window, range_test, co_test, core_left, core_right):
    rows, cols = window.shape
    count, k, s_core = co_test.shape[0], range_test.shape[1], core_left.shape[0]
    block = pack_width(count, cols // (2 * chips), k) + s_core // chips
    return call(
        sketch_kernel, (float_shape(rows // TILES, k),) * 4 + (float_shape(chips, block, k),) * 2,
        [SCALAR] + [OUTSIDE] * 5, (WHOLE,) * 6,
        [
            pltpu.VMEM((TILES, rows // TILES, cols), jnp.float32), pltpu.VMEM((cols, k), jnp.float32), pltpu.VMEM((count, rows), jnp.float32),
            pltpu.VMEM((s_core, rows), jnp.float32), pltpu.VMEM((s_core, cols), jnp.float32),
            pltpu.VMEM((cols, k), jnp.bfloat16), pltpu.VMEM((cols, k), jnp.bfloat16),
            pltpu.VMEM((count, cols), jnp.float32), pltpu.VMEM((s_core, k), jnp.float32), pltpu.VMEM((s_core, k), jnp.float32),
            pltpu.SemaphoreType.DMA((TILES,)), pltpu.SemaphoreType.DMA((4,)),
        ],
        flops=12 * rows * cols * count, limit=56,
    )(spot, window, range_test, co_test, core_left, core_right)


def core_kernel(spot_ref, window_ref, right_ref, left_ref, z_ref, held_ref, right_held_ref, left_held_ref, image_ref, window_sem, right_sem, left_sem):
    width = held_ref.shape[2]
    tile = window_ref.shape[0] // TILES
    left_copy = pltpu.make_async_copy(left_ref, left_held_ref, left_sem)

    def copies(i):
        start = pl.multiple_of(i * width, width)
        return (
            pltpu.make_async_copy(right_ref.at[:, pl.ds(start, width)], right_held_ref.at[i], right_sem.at[i]),
            pltpu.make_async_copy(window_ref.at[:, pl.ds(start, width)], held_ref.at[i], window_sem.at[i]),
        )

    for i in range(TILES):
        for copy in copies(i):
            copy.start()
    left_copy.start()
    image_ref[...] = jnp.zeros_like(image_ref)

    def step(i, carry):
        for copy in copies(i):
            copy.wait()
        image_ref[...] += parts_dot(split(held_ref[i]), split(right_held_ref[i]), 1, 1)
        return carry

    lax.fori_loop(0, TILES, step, 0)
    left_copy.wait()
    z_ref[...] = jnp.zeros_like(z_ref)

    def fold(i, carry):
        start = pl.multiple_of(i * tile, tile)
        z_ref[...] += parts_dot(split(left_held_ref[:, pl.ds(start, tile)]), split(image_ref[pl.ds(start, tile), :]))
        return carry

    lax.fori_loop(0, TILES, fold, 0)


def core_terms(spot, window, core_right, core_left):
    rows, cols = window.shape
    s_core = core_right.shape[0]
    return call(
        core_kernel, float_shape(s_core, s_core), [SCALAR] + [OUTSIDE] * 3, WHOLE,
        [
            pltpu.VMEM((TILES, rows, cols // TILES), jnp.float32), pltpu.VMEM((TILES, s_core, cols // TILES), jnp.float32),
            pltpu.VMEM((s_core, rows), jnp.float32), pltpu.VMEM((rows, s_core), jnp.float32),
            pltpu.SemaphoreType.DMA((TILES,)), pltpu.SemaphoreType.DMA((TILES,)), pltpu.SemaphoreType.DMA,
        ],
        flops=9 * rows * cols * s_core, limit=56,
    )(spot, window, core_right, core_left)


def gram_kernel(scales, spot_ref, range_ref, co_ref, sent_ref, kept_ref, y_ref, w_ref):
    y_ref[...] = highest(range_ref[...], range_ref[...], 0, 0) / scales[0]
    w_ref[...] = highest(co_ref[...], co_ref[...], 1, 1) / scales[1]
    for owner, y_out, w_out in ((0, kept_ref, sent_ref), (1, sent_ref, kept_ref)):
        @pl.when(spot_ref[0] == owner)
        def _():
            take_blocks(y_ref, y_out, spot_ref[1])
            take_blocks(w_ref, w_out, spot_ref[1])


def gram_terms(spot, chips, range_piece, co_piece, scales):
    k = range_piece.shape[1]
    square = pltpu.VMEM((k, k), jnp.float32)
    return call(
        functools.partial(gram_kernel, scales), (float_shape(chips, k // chips, k),) * 2, [SCALAR, WHOLE, WHOLE], (WHOLE, WHOLE),
        [square, square], flops=24 * k * k * k,
    )(spot, range_piece, co_piece)


def middle_kernel(spot_ref, z_ref, own_ref, other_ref, blocks_ref, left_ref, right_ref, middle_ref):
    core, place = spot_ref[0], spot_ref[1]
    for owner, left_in, right_in in ((0, own_ref, other_ref), (1, other_ref, own_ref)):
        @pl.when(core == owner)
        def _():
            put_blocks([left_in], left_ref, place)
            put_blocks([right_in], right_ref, place)

    middle_ref[...] = parts_dot(split(parts_dot(split(left_ref[...]), split(z_ref[...]), 0, 0)), split(right_ref[...]))
    take_blocks(middle_ref, blocks_ref, place)


def middle_terms(spot, chips, sketch_z, own, other):
    s_core, k = sketch_z.shape[0], own.shape[2]
    return call(
        middle_kernel, float_shape(chips, k // chips, k), [SCALAR] + [WHOLE] * 3, WHOLE,
        [pltpu.VMEM((s_core, k), jnp.float32), pltpu.VMEM((s_core, k), jnp.float32), pltpu.VMEM((k, k), jnp.float32)],
        flops=6 * k * s_core * s_core,
    )(spot, sketch_z, own, other)


def spread_lane(values, lane):
    return jnp.broadcast_to(values[:, lane:lane + 1], values.shape)


def spread_row(values, row):
    return jnp.broadcast_to(values[row:row + 1, :], values.shape)


def factor_blocks(blocks):
    count = len(blocks)
    groups = BASE // SUBLANES
    rows = [[x[SUBLANES * g:SUBLANES * (g + 1)] for g in range(groups)] for x in blocks]
    sub = lax.broadcasted_iota(jnp.int32, (SUBLANES, LANES), 0)
    pivots = [[] for _ in blocks]
    for p in range(groups):
        cols = [{g: [spread_lane(rows[b][g], SUBLANES * p + k) for k in range(SUBLANES)] for g in range(p, groups)} for b in range(count)]
        found = [jnp.zeros((SUBLANES, LANES), jnp.float32)] * count
        for k in range(SUBLANES):
            for b in range(count):
                held = cols[b]
                pivot = spread_row(held[p][k], k)
                found[b] = jnp.where(sub == k, pivot, found[b])
                scale = 1.0 / pivot
                pivot_row = spread_row(rows[b][p], k)
                heads = [spread_row(held[p][j], k) for j in range(k + 1, SUBLANES)]
                for g in range(p, groups):
                    weight = held[g][k] * scale
                    if g == p:
                        weight = jnp.where(sub > k, weight, 0.0)
                    rows[b][g] = rows[b][g] - weight * pivot_row
                    for j in range(k + 1, SUBLANES):
                        held[g][j] = held[g][j] - weight * heads[j - k - 1]
        for b in range(count):
            pivots[b].append(found[b])
    return [jnp.concatenate([rows[b][g] * lax.rsqrt(pivots[b][g]) for g in range(groups)], axis=0) for b in range(count)]


def factor_steps(steps, inverse_ref, upper_ref):
    count, n = inverse_ref.shape[0], inverse_ref.shape[1]
    every = range(count)
    row_id = lax.broadcasted_iota(jnp.int32, (n, n), 0)
    col_id = lax.broadcasted_iota(jnp.int32, (n, n), 1)
    panel_col = lax.broadcasted_iota(jnp.int32, (BASE, n), 1)
    lane = lax.broadcasted_iota(jnp.int32, (BASE, LANES), 1)
    low = lax.broadcasted_iota(jnp.int32, (BASE, LANES), 0)

    def place(half, start):
        rest = [jnp.zeros((BASE, LANES), jnp.float32)] * (n // LANES - 1)
        return pltpu.roll(jnp.concatenate([jnp.where(lane < BASE, half, 0.0)] + rest, axis=1), start, 1)

    def step(t, carry):
        start = pl.multiple_of(t * BASE, BASE)
        back = jnp.where(t == 0, 0, n - start)
        panel = [inverse_ref[b, pl.ds(start, BASE), :] for b in every]
        whole = [inverse_ref[b] for b in every]
        block = [pltpu.roll(panel[b], back, 1)[:, :LANES] for b in every]
        block = [jnp.where(lane < BASE, block[b], jnp.where(lane - BASE == low, 1.0, 0.0)) for b in every]
        done = factor_blocks(block)
        inv = [pltpu.roll(done[b], LANES - BASE, 1) for b in every]
        inv_placed = [place(inv[b], start) for b in every]
        up_placed = place(done[0], start)
        inside = (panel_col >= start) & (panel_col < start + BASE)
        rows = [jnp.where(inside, inv_placed[b], highest(inv[b][:, :BASE], panel[b])) for b in every]
        below = [jnp.where(row_id[:, :BASE] >= start + BASE, highest(whole[b], inv_placed[b], 1, 1), 0.0) for b in every]
        spent = (row_id >= start + BASE) & (col_id >= start) & (col_id < start + BASE)
        left = [jnp.where(spent, 0.0, whole[b]) - highest(below[b], rows[b]) for b in every]
        for b in every:
            inverse_ref[b] = left[b]
        for b in every:
            inverse_ref[b, pl.ds(start, BASE), :] = rows[b]
        upper_ref[pl.ds(start, BASE), :] = jnp.where(inside, up_placed, jnp.where(panel_col >= start + BASE, rows[0], 0.0))
        return carry

    lax.fori_loop(steps[0], steps[1], step, 0)


def factor_start_kernel(steps, peers, spot_ref, *refs):
    part_refs, (inverse_ref, upper_ref, fold_ref) = refs[:peers], refs[peers:]
    n = upper_ref.shape[0]
    inner = part_refs[0].shape[0]
    rows = n // (peers * inner)
    fold_rows = fold_ref.shape[0] // (peers * inner)
    for i, ref in enumerate(part_refs):
        for j in range(inner):
            block = i * inner + j
            inverse_ref[0, pl.ds(block_start(spot_ref[1], block, rows), rows), :] = ref[j, :rows]
            fold_ref[block * fold_rows:(block + 1) * fold_rows, :] = ref[j, rows:]
    inverse_ref[1] = highest(fold_ref[...], fold_ref[...], 0, 0)
    upper_ref[...] = jnp.zeros_like(upper_ref)
    factor_steps(steps, inverse_ref, upper_ref)


def factor_next_kernel(steps, begun_ref, begun_upper_ref, inverse_ref, upper_ref):
    inverse_ref[...] = begun_ref[...]
    upper_ref[...] = begun_upper_ref[...]
    factor_steps(steps, inverse_ref, upper_ref)


def factor_end_kernel(steps, begun_ref, begun_upper_ref, out_ref, inverse_ref, upper_ref):
    n = upper_ref.shape[0]
    inverse_ref[...] = begun_ref[...]
    upper_ref[...] = begun_upper_ref[...]
    factor_steps(steps, inverse_ref, upper_ref)
    row_id = lax.broadcasted_iota(jnp.int32, (n, n), 0)
    col_id = lax.broadcasted_iota(jnp.int32, (n, n), 1)
    out_ref[0] = jnp.where(row_id >= col_id, inverse_ref[0], 0.0)
    upper = jnp.where(row_id <= col_id, upper_ref[...], 0.0)
    image = jnp.where(row_id >= col_id, inverse_ref[1], 0.0)
    out_ref[1] = highest(highest(upper, image, 1, 1), image)


def factor_start(spot, parts):
    n = parts[0].shape[2]
    blocks = len(parts) * parts[0].shape[0]
    return call(
        functools.partial(factor_start_kernel, (0, 1), len(parts)), (float_shape(2, n, n), float_shape(n, n)),
        [SCALAR] + [WHOLE] * len(parts), (WHOLE, WHOLE), [pltpu.VMEM((blocks * parts[0].shape[1] - n, n), jnp.float32)], flops=n * n * n * 100,
    )(spot, *parts)


def factor_next(steps, begun, upper):
    n = upper.shape[0]
    return call(
        functools.partial(factor_next_kernel, steps), (float_shape(2, n, n), float_shape(n, n)), [WHOLE, WHOLE], (WHOLE, WHOLE), flops=n * n * n * 100,
    )(begun, upper)


def factor_end(begun, upper):
    n = upper.shape[0]
    return call(
        functools.partial(factor_end_kernel, (n // BASE - 1, n // BASE)), float_shape(2, n, n), [WHOLE, WHOLE], WHOLE,
        [pltpu.VMEM((2, n, n), jnp.float32), pltpu.VMEM((n, n), jnp.float32)], flops=n * n * n * 100,
    )(begun, upper)


def basis_kernel(peers, spot_ref, own_ref, other_ref, *refs):
    range_refs, (co_own_ref, co_other_ref, range_out_ref, co_out_ref, range_held_ref, co_held_ref, range_done_ref, co_done_ref, side_ref, range_sem, co_sem, range_out_sem, co_out_sem) = refs[:peers], refs[peers:]
    core, place, line = spot_ref[0], spot_ref[1], spot_ref[3]
    lines, rows, _ = range_held_ref.shape
    cells, _, width = co_held_ref.shape
    chips = cells // 2

    def range_copy(f):
        return pltpu.make_async_copy(range_refs[f // (lines // peers)].at[f % (lines // peers)], range_held_ref.at[f], range_sem.at[f])

    def co_copy(f):
        return pltpu.make_async_copy((co_own_ref, co_other_ref)[f // chips].at[f % chips], co_held_ref.at[f], co_sem.at[f])

    def range_wait(f):
        pltpu.make_async_copy(range_refs[0].at[0], range_held_ref.at[f], range_sem.at[f]).wait()

    def co_wait(f):
        pltpu.make_async_copy(co_own_ref.at[0], co_held_ref.at[f], co_sem.at[f]).wait()

    def range_out(f):
        return pltpu.make_async_copy(range_done_ref.at[f], range_out_ref.at[pl.ds(block_start(line, f, rows), rows)], range_out_sem.at[f])

    def co_out(f):
        column = jnp.where(f < chips, core, 1 - core) * chips + (place ^ (f % chips))
        return pltpu.make_async_copy(co_done_ref.at[f], co_out_ref.at[:, pl.ds(pl.multiple_of(column * width, width), width)], co_out_sem.at[f])

    for f in range(lines):
        range_copy(f).start()
    for f in range(cells):
        co_copy(f).start()
    first = spot_ref[0] == 0
    side_ref[0], side_ref[1] = split(jnp.where(first, own_ref[0], other_ref[0]))
    side_ref[2], side_ref[3] = split(jnp.where(first, other_ref[0], own_ref[0]))

    def range_step(f, carry):
        range_wait(f)
        range_done_ref[f] = parts_dot(split(range_held_ref[f]), (side_ref[0], side_ref[1]), 1, 1)
        range_out(f).start()
        return carry

    def co_step(f, carry):
        co_wait(f)
        co_done_ref[f] = parts_dot((side_ref[2], side_ref[3]), split(co_held_ref[f]))
        co_out(f).start()
        return carry

    lax.fori_loop(0, lines, range_step, 0)
    lax.fori_loop(0, cells, co_step, 0)
    for f in range(lines):
        range_out(f).wait()
    for f in range(cells):
        co_out(f).wait()


def bases(spot, own, other, ranges, co_own, co_other):
    inner, rows, k = ranges[0].shape
    chips, count, width = co_own.shape
    lines, cells = inner * len(ranges), 2 * chips
    range_held, co_held = pltpu.VMEM((lines, rows, k), jnp.float32), pltpu.VMEM((cells, count, width), jnp.float32)
    line_sem, cell_sem = pltpu.SemaphoreType.DMA((lines,)), pltpu.SemaphoreType.DMA((cells,))
    return call(
        functools.partial(basis_kernel, len(ranges)), (float_shape(lines * rows, k), float_shape(count, cells * width)),
        [SCALAR, WHOLE, WHOLE] + [OUTSIDE] * (len(ranges) + 2), (OUTSIDE, OUTSIDE),
        [range_held, co_held, range_held, co_held, pltpu.VMEM((4, k, k), jnp.bfloat16), line_sem, cell_sem, line_sem, cell_sem],
        flops=18 * lines * rows * k * k, limit=56,
    )(spot, own, other, *ranges, co_own, co_other)


def finish_kernel(scale, spot_ref, own_ref, other_ref, middle_own_ref, middle_other_ref, out_ref, middle_ref):
    core, place = spot_ref[0], spot_ref[1]
    chips, extent = middle_own_ref.shape[0], middle_own_ref.shape[1]
    for i in range(chips):
        middle_ref[pl.ds(block_start(place, i, extent), extent), :] = middle_own_ref[i] + middle_other_ref[i]
    left = jnp.where(core == 0, own_ref[1], other_ref[1])
    right = jnp.where(core == 0, other_ref[1], own_ref[1])
    out_ref[...] = highest(highest(left, middle_ref[...]), right, 1, 1) * scale


def finish(spot, own, other, middle_own, middle_other, scale):
    k = own.shape[1]
    return call(
        functools.partial(finish_kernel, scale), float_shape(k, k), [SCALAR] + [WHOLE] * 4, WHOLE,
        [pltpu.VMEM((k, k), jnp.float32)], flops=24 * k * k * k,
    )(spot, own, other, middle_own, middle_other)


def per_device(window, range_test, co_test, core_left, core_right):
    rows_total = window.shape[0] * lax.axis_size("cell")
    cols_total = window.shape[1] * lax.axis_size("tm")
    k = range_test.shape[1]
    chips = lax.axis_size("cell") // 2
    groups = groups_of("cell", 1, 2)
    lines = [("tm", (bit,)) for bit in range(bits_of("tm"))]
    cell, line = lax.axis_index("cell"), lax.axis_index("tm")
    spot = jnp.stack([cell & 1, place_of(groups, cell), place_of(lines[:2], line), place_of(lines, line)]).astype(jnp.int32)

    def core_swap(values):
        return swap(values, "cell", 1)

    r3, r2, r1, r0, sent, kept = sketch_terms(spot, chips, window, range_test, co_test, core_left, core_right)
    far = swap(r3, "tm", 1)
    pack = kept + core_swap(sent)
    handed = r1 + after(far, pack)
    near = swap(after(r2, handed), "tm", 1)
    sketch_z = core_terms(after(spot, pack, handed), window, core_right, core_left)
    pack = scatter_sum(pack, groups)[0]
    handed, near, pack, sketch_z = lax.optimization_barrier((swap(handed, "tm", 2), near, pack, sketch_z))
    range_piece = (r0 + near + handed).reshape(lax.axis_size("tm") // 4, -1, r0.shape[1])
    if lines[2:]:
        rest = place_of(lines[2:], line)
        range_piece = jnp.stack([lax.dynamic_index_in_dim(range_piece, rest ^ f, 0, False) for f in range(range_piece.shape[0])])
    range_piece = scatter_sum(range_piece, lines[2:])
    width = window.shape[1] // (2 * chips)
    packed = pack_width(co_test.shape[0], width, k)
    co_piece = pack[:packed].reshape(packed, -1, width).swapaxes(0, 1).reshape(-1, width)
    fold = pack[None, packed:]

    gram_sent, gram_kept = gram_terms(spot, chips, range_piece[0], co_piece, (rows_total, cols_total))
    fold = whole_sum(fold, "tm")
    gram = scatter_sum(gram_kept + core_swap(gram_sent), groups)
    co_parts = gather(after(co_piece[None], gram), groups)
    gram, co_parts = lax.optimization_barrier((whole_sum(gram, "tm"), co_parts))
    rows = gram.shape[1]
    parts = gather(jnp.concatenate([gram, fold], axis=1), groups)
    co_own = jnp.concatenate(co_parts)
    fold = jnp.concatenate([part[:, rows:] for part in parts])

    range_parts = gather(after(range_piece, gram, fold), lines[1:])
    co_other, fold_other = core_swap(co_own), core_swap(fold)
    state = factor_start(spot, parts)
    state, fold_other = lax.optimization_barrier((state, fold_other))
    middle = middle_terms(spot, chips, sketch_z, fold, fold_other)
    middle = scatter_sum(middle, groups)
    state = factor_next((1, 2), *state)
    state, middle, range_parts = lax.optimization_barrier((state, middle, range_parts))
    range_all = gather(jnp.concatenate(range_parts), lines[:1])
    for bit in range(bits_of("tm")):
        middle = middle + swap(middle, "tm", 1 << bit)
        if bit == 0:
            state = factor_next((2, state[1].shape[0] // BASE - 1), *state)
            state, middle = lax.optimization_barrier((state, middle))
    own = factor_end(*state)
    own, middle = lax.optimization_barrier((own, middle))
    other = core_swap(own)
    middle = jnp.concatenate(gather(middle, groups))
    range_basis, co_basis = bases(spot, own, other, range_all, co_own, co_other)
    core_out = finish(spot, own, other, middle, core_swap(middle), math.sqrt(rows_total * cols_total))
    return (range_basis, co_basis, core_out)


def solution(mesh):
    return jax.shard_map(
        per_device,
        mesh=mesh,
        in_specs=(P("cell", "tm"), P("tm", None), P(None, "cell"), P(None, "cell"), P(None, "tm")),
        out_specs=(P("cell", None), P(None, "tm"), P()),
        check_vma=False,
    )
```

```python
import functools
import math

import jax
import jax.numpy as jnp
from jax import lax
from jax.experimental import pallas as pl
from jax.experimental.pallas import tpu as pltpu
from jax.sharding import PartitionSpec as P

BASE = 64
LANES = 128
SUBLANES = 8
TILES = 4
WHOLE = pl.BlockSpec(memory_space=pltpu.VMEM)
SCALAR = pl.BlockSpec(memory_space=pltpu.SMEM)
OUTSIDE = pl.BlockSpec(memory_space=pl.ANY)


def highest(left, right, left_dim=1, right_dim=0):
    dims = (((left_dim,), (right_dim,)), ((), ()))
    return lax.dot_general(left, right, dims, precision=lax.Precision.HIGHEST, preferred_element_type=jnp.float32)


def split(values):
    top = values.astype(jnp.bfloat16)
    return top, (values - top.astype(jnp.float32)).astype(jnp.bfloat16)


def parts_dot(left, right, left_dim=1, right_dim=0):
    dims = (((left_dim,), (right_dim,)), ((), ()))
    pairs = ((left[0], right[0]), (left[0], right[1]), (left[1], right[0]))
    return sum(lax.dot_general(a, b, dims, preferred_element_type=jnp.float32) for a, b in pairs)


def float_shape(*shape):
    return jax.ShapeDtypeStruct(shape, jnp.float32)


def call(kernel, out_shape, in_specs, out_specs, scratch=(), flops=0, limit=24):
    return pl.pallas_call(
        kernel,
        out_shape=out_shape,
        in_specs=in_specs,
        out_specs=out_specs,
        scratch_shapes=list(scratch),
        compiler_params=pltpu.CompilerParams(vmem_limit_bytes=limit * 1024 * 1024),
        cost_estimate=pl.CostEstimate(flops=flops, bytes_accessed=4 * 1024 * 1024, transcendentals=0),
    )


def bits_of(axis):
    return int(math.log2(lax.axis_size(axis)))


def groups_of(axis, first, width):
    bits = list(range(first, bits_of(axis)))
    return [(axis, tuple(bits[i:i + width])) for i in range(0, len(bits), width)]


def place_of(groups, index):
    place = 0
    for _, bits in groups:
        place = (place << len(bits)) + sum(((index >> bit) & 1) << i for i, bit in enumerate(bits))
    return place


def swap(values, axis, mask):
    return lax.ppermute(values, axis, [(i, i ^ mask) for i in range(lax.axis_size(axis))])


def masks_of(bits):
    return [sum(((peer >> i) & 1) << bit for i, bit in enumerate(bits)) for peer in range(1 << len(bits))]


def pair_sum(parts):
    while len(parts) > 1:
        parts = [parts[i] + parts[i + 1] for i in range(0, len(parts), 2)]
    return parts[0]


def scatter_sum(blocks, groups):
    for axis, bits in groups:
        count = blocks.shape[0] >> len(bits)
        parts = [blocks[peer * count:(peer + 1) * count] for peer in range(1 << len(bits))]
        blocks = pair_sum([parts[0]] + [swap(part, axis, mask) for part, mask in zip(parts[1:], masks_of(bits)[1:])])
    return blocks


def gather(blocks, groups):
    parts = [blocks]
    for axis, bits in reversed(groups):
        blocks = jnp.concatenate(parts) if len(parts) > 1 else parts[0]
        parts = [blocks] + [swap(blocks, axis, mask) for mask in masks_of(bits)[1:]]
    return parts


def whole_sum(values, axis):
    for bit in range(bits_of(axis)):
        values = values + swap(values, axis, 1 << bit)
    return values


def after(values, *earlier):
    return lax.optimization_barrier((values,) + earlier)[0]


def block_start(place, block, extent):
    return pl.multiple_of((place ^ block) * extent, extent)


def put_blocks(refs, out_ref, place):
    count, extent = refs[0].shape[0], refs[0].shape[1]
    for i, ref in enumerate(refs):
        for j in range(count):
            out_ref[pl.ds(block_start(place, i * count + j, extent), extent), :] = ref[j]


def take_blocks(ref, out_ref, place, base=0):
    count, extent = out_ref.shape[0], out_ref.shape[1]
    for i in range(count):
        out_ref[i] = ref[pl.ds(pl.multiple_of(base + (place ^ i) * extent, extent), extent), :]


def pack_width(count, width, k):
    return count * width // k


def sketch_kernel(spot_ref, window_ref, test_ref, co_ref, left_ref, right_ref, r3_ref, r2_ref, r1_ref, r0_ref, sent_ref, kept_ref, held_ref, test_held_ref, co_held_ref, left_held_ref, right_held_ref, top_ref, rest_ref, range_done_ref, co_done_ref, lt_ref, rt_ref, fold_ref, window_sem, sem, range_sem, co_sem, fold_sem):
    core, place, line = spot_ref[0], spot_ref[1], spot_ref[2]
    tile = held_ref.shape[1]
    chips, _, k = kept_ref.shape
    count, cols = co_done_ref.shape
    width = cols // (2 * chips)
    packed = pack_width(count, width, k)
    extent = lt_ref.shape[0] // chips
    small = [(test_ref, test_held_ref), (co_ref, co_held_ref), (left_ref, left_held_ref), (right_ref, right_held_ref)]
    small = [pltpu.make_async_copy(a, b, sem.at[i]) for i, (a, b) in enumerate(small)]

    def window_copy(i):
        return pltpu.make_async_copy(window_ref.at[pl.ds(block_start(line, TILES - 1 - i, tile), tile)], held_ref.at[i], window_sem.at[i])

    small[0].start()
    window_copy(0).start()
    small[1].start()
    co_done_ref[...] = jnp.zeros_like(co_done_ref)
    lt_ref[...] = jnp.zeros_like(lt_ref)
    small[0].wait()
    window_copy(1).start()
    small[2].start()
    for i in range(2, TILES):
        window_copy(i).start()
    small[3].start()
    top_ref[...], rest_ref[...] = split(test_held_ref[...])
    range_outs = [pltpu.make_async_copy(range_done_ref.at[i], ref, range_sem.at[i]) for i, ref in enumerate((r3_ref, r2_ref, r1_ref, r0_ref))]
    small[1].wait()

    def step(i, carry):
        window_copy(i).wait()
        rows = split(held_ref[i])
        spot = pl.ds(block_start(line, TILES - 1 - i, tile), tile)
        done = parts_dot(rows, (top_ref[...], rest_ref[...]))
        range_done_ref[i] = done
        for block, copy in enumerate(range_outs):
            @pl.when(i == block)
            def _():
                copy.start()

        co_done_ref[...] += parts_dot(split(co_held_ref[:, spot]), rows)

        @pl.when(i == 0)
        def _():
            small[2].wait()

        lt_ref[...] += parts_dot(split(left_held_ref[:, spot]), split(done))
        return carry

    lax.fori_loop(0, TILES, step, 0)
    co_outs = []
    for out_ref, side in ((sent_ref, 1 - core), (kept_ref, core)):
        for i in range(chips):
            for j in range(count // packed):
                start = pl.multiple_of((side * chips + (place ^ i)) * width, width)
                part = co_done_ref.at[j * packed:(j + 1) * packed, pl.ds(start, width)]
                co_outs.append(pltpu.make_async_copy(part, out_ref.at[i, :packed, j * width:(j + 1) * width], co_sem.at[len(co_outs)]))
    for copy in co_outs:
        copy.start()
    small[3].wait()
    rt_ref[...] = parts_dot(split(right_held_ref[...]), split(co_done_ref[...]), 1, 1)
    first = core == 0
    fold_ref[0] = jnp.where(first, rt_ref[...], lt_ref[...])
    fold_ref[1] = jnp.where(first, lt_ref[...], rt_ref[...])
    fold_outs = []
    for side, out_ref in enumerate((sent_ref, kept_ref)):
        for i in range(chips):
            part = fold_ref.at[side, pl.ds(block_start(place, i, extent), extent)]
            fold_outs.append(pltpu.make_async_copy(part, out_ref.at[i, packed:], fold_sem.at[len(fold_outs)]))
    for copy in fold_outs:
        copy.start()
    for copy in range_outs + co_outs + fold_outs:
        copy.wait()


def sketch_terms(spot, chips, window, range_test, co_test, core_left, core_right):
    rows, cols = window.shape
    count, k, s_core = co_test.shape[0], range_test.shape[1], core_left.shape[0]
    width = cols // (2 * chips)
    block = pack_width(count, width, k) + s_core // chips
    return call(
        sketch_kernel, (float_shape(rows // TILES, k),) * 4 + (float_shape(chips, block, k),) * 2,
        [SCALAR] + [OUTSIDE] * 5, (OUTSIDE,) * 6,
        [
            pltpu.VMEM((TILES, rows // TILES, cols), jnp.float32), pltpu.VMEM((cols, k), jnp.float32), pltpu.VMEM((count, rows), jnp.float32),
            pltpu.VMEM((s_core, rows), jnp.float32), pltpu.VMEM((s_core, cols), jnp.float32),
            pltpu.VMEM((cols, k), jnp.bfloat16), pltpu.VMEM((cols, k), jnp.bfloat16),
            pltpu.VMEM((TILES, rows // TILES, k), jnp.float32), pltpu.VMEM((count, cols), jnp.float32),
            pltpu.VMEM((s_core, k), jnp.float32), pltpu.VMEM((s_core, k), jnp.float32), pltpu.VMEM((2, s_core, k), jnp.float32),
            pltpu.SemaphoreType.DMA((TILES,)), pltpu.SemaphoreType.DMA((4,)), pltpu.SemaphoreType.DMA((TILES,)),
            pltpu.SemaphoreType.DMA((2 * cols // width,)), pltpu.SemaphoreType.DMA((2 * chips,)),
        ],
        flops=12 * rows * cols * count, limit=56,
    )(spot, window, range_test, co_test, core_left, core_right)


def core_kernel(spot_ref, window_ref, right_ref, left_ref, z_ref, held_ref, right_held_ref, left_held_ref, image_ref, window_sem, right_sem, left_sem):
    width = held_ref.shape[2]
    tile = window_ref.shape[0] // TILES
    left_copy = pltpu.make_async_copy(left_ref, left_held_ref, left_sem)

    def copies(i):
        start = pl.multiple_of(i * width, width)
        return (
            pltpu.make_async_copy(right_ref.at[:, pl.ds(start, width)], right_held_ref.at[i], right_sem.at[i]),
            pltpu.make_async_copy(window_ref.at[:, pl.ds(start, width)], held_ref.at[i], window_sem.at[i]),
        )

    for i in range(TILES):
        for copy in copies(i):
            copy.start()
    left_copy.start()
    image_ref[...] = jnp.zeros_like(image_ref)

    def step(i, carry):
        for copy in copies(i):
            copy.wait()
        image_ref[...] += parts_dot(split(held_ref[i]), split(right_held_ref[i]), 1, 1)
        return carry

    lax.fori_loop(0, TILES, step, 0)
    left_copy.wait()
    z_ref[...] = jnp.zeros_like(z_ref)

    def fold(i, carry):
        start = pl.multiple_of(i * tile, tile)
        z_ref[...] += parts_dot(split(left_held_ref[:, pl.ds(start, tile)]), split(image_ref[pl.ds(start, tile), :]))
        return carry

    lax.fori_loop(0, TILES, fold, 0)


def core_terms(spot, window, core_right, core_left):
    rows, cols = window.shape
    s_core = core_right.shape[0]
    return call(
        core_kernel, float_shape(s_core, s_core), [SCALAR] + [OUTSIDE] * 3, WHOLE,
        [
            pltpu.VMEM((TILES, rows, cols // TILES), jnp.float32), pltpu.VMEM((TILES, s_core, cols // TILES), jnp.float32),
            pltpu.VMEM((s_core, rows), jnp.float32), pltpu.VMEM((rows, s_core), jnp.float32),
            pltpu.SemaphoreType.DMA((TILES,)), pltpu.SemaphoreType.DMA((TILES,)), pltpu.SemaphoreType.DMA,
        ],
        flops=9 * rows * cols * s_core, limit=56,
    )(spot, window, core_right, core_left)


def gram_kernel(scales, spot_ref, range_ref, co_ref, sent_ref, kept_ref, y_ref, w_ref):
    y_ref[...] = highest(range_ref[...], range_ref[...], 0, 0) / scales[0]
    w_ref[...] = highest(co_ref[...], co_ref[...], 1, 1) / scales[1]
    for owner, y_out, w_out in ((0, kept_ref, sent_ref), (1, sent_ref, kept_ref)):
        @pl.when(spot_ref[0] == owner)
        def _():
            take_blocks(y_ref, y_out, spot_ref[1])
            take_blocks(w_ref, w_out, spot_ref[1])


def gram_terms(spot, chips, range_piece, co_piece, scales):
    k = range_piece.shape[1]
    square = pltpu.VMEM((k, k), jnp.float32)
    return call(
        functools.partial(gram_kernel, scales), (float_shape(chips, k // chips, k),) * 2, [SCALAR, WHOLE, WHOLE], (WHOLE, WHOLE),
        [square, square], flops=24 * k * k * k,
    )(spot, range_piece, co_piece)


def middle_kernel(spot_ref, z_ref, own_ref, other_ref, blocks_ref, left_ref, right_ref, middle_ref):
    core, place = spot_ref[0], spot_ref[1]
    for owner, left_in, right_in in ((0, own_ref, other_ref), (1, other_ref, own_ref)):
        @pl.when(core == owner)
        def _():
            put_blocks([left_in], left_ref, place)
            put_blocks([right_in], right_ref, place)

    middle_ref[...] = parts_dot(split(parts_dot(split(left_ref[...]), split(z_ref[...]), 0, 0)), split(right_ref[...]))
    take_blocks(middle_ref, blocks_ref, place)


def middle_terms(spot, chips, sketch_z, own, other):
    s_core, k = sketch_z.shape[0], own.shape[2]
    return call(
        middle_kernel, float_shape(chips, k // chips, k), [SCALAR] + [WHOLE] * 3, WHOLE,
        [pltpu.VMEM((s_core, k), jnp.float32), pltpu.VMEM((s_core, k), jnp.float32), pltpu.VMEM((k, k), jnp.float32)],
        flops=6 * k * s_core * s_core,
    )(spot, sketch_z, own, other)


def spread_lane(values, lane):
    return jnp.broadcast_to(values[:, lane:lane + 1], values.shape)


def spread_row(values, row):
    return jnp.broadcast_to(values[row:row + 1, :], values.shape)


def factor_blocks(blocks):
    count = len(blocks)
    groups = BASE // SUBLANES
    rows = [[x[SUBLANES * g:SUBLANES * (g + 1)] for g in range(groups)] for x in blocks]
    sub = lax.broadcasted_iota(jnp.int32, (SUBLANES, LANES), 0)
    pivots = [[] for _ in blocks]
    for p in range(groups):
        cols = [{g: [spread_lane(rows[b][g], SUBLANES * p + k) for k in range(SUBLANES)] for g in range(p, groups)} for b in range(count)]
        found = [jnp.zeros((SUBLANES, LANES), jnp.float32)] * count
        for k in range(SUBLANES):
            for b in range(count):
                held = cols[b]
                pivot = spread_row(held[p][k], k)
                found[b] = jnp.where(sub == k, pivot, found[b])
                scale = 1.0 / pivot
                pivot_row = spread_row(rows[b][p], k)
                heads = [spread_row(held[p][j], k) for j in range(k + 1, SUBLANES)]
                for g in range(p, groups):
                    weight = held[g][k] * scale
                    if g == p:
                        weight = jnp.where(sub > k, weight, 0.0)
                    rows[b][g] = rows[b][g] - weight * pivot_row
                    for j in range(k + 1, SUBLANES):
                        held[g][j] = held[g][j] - weight * heads[j - k - 1]
        for b in range(count):
            pivots[b].append(found[b])
    return [jnp.concatenate([rows[b][g] * lax.rsqrt(pivots[b][g]) for g in range(groups)], axis=0) for b in range(count)]


def factor_steps(steps, inverse_ref, upper_ref):
    count, n = inverse_ref.shape[0], inverse_ref.shape[1]
    every = range(count)
    row_id = lax.broadcasted_iota(jnp.int32, (n, n), 0)
    col_id = lax.broadcasted_iota(jnp.int32, (n, n), 1)
    panel_col = lax.broadcasted_iota(jnp.int32, (BASE, n), 1)
    lane = lax.broadcasted_iota(jnp.int32, (BASE, LANES), 1)
    low = lax.broadcasted_iota(jnp.int32, (BASE, LANES), 0)

    def place(half, start):
        rest = [jnp.zeros((BASE, LANES), jnp.float32)] * (n // LANES - 1)
        return pltpu.roll(jnp.concatenate([jnp.where(lane < BASE, half, 0.0)] + rest, axis=1), start, 1)

    def step(t, carry):
        start = pl.multiple_of(t * BASE, BASE)
        back = jnp.where(t == 0, 0, n - start)
        panel = [inverse_ref[b, pl.ds(start, BASE), :] for b in every]
        whole = [inverse_ref[b] for b in every]
        block = [pltpu.roll(panel[b], back, 1)[:, :LANES] for b in every]
        block = [jnp.where(lane < BASE, block[b], jnp.where(lane - BASE == low, 1.0, 0.0)) for b in every]
        done = factor_blocks(block)
        inv = [pltpu.roll(done[b], LANES - BASE, 1) for b in every]
        inv_placed = [place(inv[b], start) for b in every]
        up_placed = place(done[0], start)
        inside = (panel_col >= start) & (panel_col < start + BASE)
        rows = [jnp.where(inside, inv_placed[b], highest(inv[b][:, :BASE], panel[b])) for b in every]
        below = [jnp.where(row_id[:, :BASE] >= start + BASE, highest(whole[b], inv_placed[b], 1, 1), 0.0) for b in every]
        spent = (row_id >= start + BASE) & (col_id >= start) & (col_id < start + BASE)
        left = [jnp.where(spent, 0.0, whole[b]) - highest(below[b], rows[b]) for b in every]
        for b in every:
            inverse_ref[b] = left[b]
        for b in every:
            inverse_ref[b, pl.ds(start, BASE), :] = rows[b]
        upper_ref[pl.ds(start, BASE), :] = jnp.where(inside, up_placed, jnp.where(panel_col >= start + BASE, rows[0], 0.0))
        return carry

    lax.fori_loop(steps[0], steps[1], step, 0)


def factor_start_kernel(steps, peers, spot_ref, *refs):
    part_refs, (inverse_ref, upper_ref, fold_ref) = refs[:peers], refs[peers:]
    n = upper_ref.shape[0]
    inner = part_refs[0].shape[0]
    rows = n // (peers * inner)
    fold_rows = fold_ref.shape[0] // (peers * inner)
    for i, ref in enumerate(part_refs):
        for j in range(inner):
            block = i * inner + j
            inverse_ref[0, pl.ds(block_start(spot_ref[1], block, rows), rows), :] = ref[j, :rows]
            fold_ref[block * fold_rows:(block + 1) * fold_rows, :] = ref[j, rows:]
    inverse_ref[1] = highest(fold_ref[...], fold_ref[...], 0, 0)
    upper_ref[...] = jnp.zeros_like(upper_ref)
    factor_steps(steps, inverse_ref, upper_ref)


def factor_next_kernel(steps, begun_ref, begun_upper_ref, inverse_ref, upper_ref):
    inverse_ref[...] = begun_ref[...]
    upper_ref[...] = begun_upper_ref[...]
    factor_steps(steps, inverse_ref, upper_ref)


def factor_end_kernel(steps, begun_ref, begun_upper_ref, out_ref, inverse_ref, upper_ref):
    n = upper_ref.shape[0]
    inverse_ref[...] = begun_ref[...]
    upper_ref[...] = begun_upper_ref[...]
    factor_steps(steps, inverse_ref, upper_ref)
    row_id = lax.broadcasted_iota(jnp.int32, (n, n), 0)
    col_id = lax.broadcasted_iota(jnp.int32, (n, n), 1)
    out_ref[0] = jnp.where(row_id >= col_id, inverse_ref[0], 0.0)
    upper = jnp.where(row_id <= col_id, upper_ref[...], 0.0)
    image = jnp.where(row_id >= col_id, inverse_ref[1], 0.0)
    out_ref[1] = highest(highest(upper, image, 1, 1), image)


def factor_start(spot, parts):
    n = parts[0].shape[2]
    blocks = len(parts) * parts[0].shape[0]
    return call(
        functools.partial(factor_start_kernel, (0, 1), len(parts)), (float_shape(2, n, n), float_shape(n, n)),
        [SCALAR] + [WHOLE] * len(parts), (WHOLE, WHOLE), [pltpu.VMEM((blocks * parts[0].shape[1] - n, n), jnp.float32)], flops=n * n * n * 100,
    )(spot, *parts)


def factor_next(steps, begun, upper):
    n = upper.shape[0]
    return call(
        functools.partial(factor_next_kernel, steps), (float_shape(2, n, n), float_shape(n, n)), [WHOLE, WHOLE], (WHOLE, WHOLE), flops=n * n * n * 100,
    )(begun, upper)


def factor_end(begun, upper):
    n = upper.shape[0]
    return call(
        functools.partial(factor_end_kernel, (n // BASE - 1, n // BASE)), float_shape(2, n, n), [WHOLE, WHOLE], WHOLE,
        [pltpu.VMEM((2, n, n), jnp.float32), pltpu.VMEM((n, n), jnp.float32)], flops=n * n * n * 100,
    )(begun, upper)


def basis_kernel(peers, spot_ref, own_ref, other_ref, *refs):
    range_refs, (co_own_ref, co_other_ref, range_out_ref, co_out_ref, range_done_ref, co_done_ref, side_ref, range_sem, co_sem) = refs[:peers], refs[peers:]
    core, place, line = spot_ref[0], spot_ref[1], spot_ref[3]
    inner, rows, _ = range_refs[0].shape
    chips, _, width = co_own_ref.shape
    first = core == 0
    side_ref[0], side_ref[1] = split(jnp.where(first, own_ref[0], other_ref[0]))
    side_ref[2], side_ref[3] = split(jnp.where(first, other_ref[0], own_ref[0]))

    def range_out(f):
        return pltpu.make_async_copy(range_done_ref.at[f], range_out_ref.at[pl.ds(block_start(line, f, rows), rows)], range_sem.at[f])

    def co_out(f):
        column = jnp.where(f < chips, core, 1 - core) * chips + (place ^ (f % chips))
        return pltpu.make_async_copy(co_done_ref.at[f], co_out_ref.at[:, pl.ds(pl.multiple_of(column * width, width), width)], co_sem.at[f])

    for i, ref in enumerate(range_refs):
        def range_step(j, carry, i=i, ref=ref):
            f = i * inner + j
            range_done_ref[f] = parts_dot(split(ref[j]), (side_ref[0], side_ref[1]), 1, 1)
            range_out(f).start()
            return carry

        lax.fori_loop(0, inner, range_step, 0)
    for i, ref in enumerate((co_own_ref, co_other_ref)):
        def co_step(j, carry, i=i, ref=ref):
            f = i * chips + j
            co_done_ref[f] = parts_dot((side_ref[2], side_ref[3]), split(ref[j]))
            co_out(f).start()
            return carry

        lax.fori_loop(0, chips, co_step, 0)
    for f in range(peers * inner):
        range_out(f).wait()
    for f in range(2 * chips):
        co_out(f).wait()


def bases(spot, own, other, ranges, co_own, co_other):
    inner, rows, k = ranges[0].shape
    chips, count, width = co_own.shape
    lines, cells = inner * len(ranges), 2 * chips
    return call(
        functools.partial(basis_kernel, len(ranges)), (float_shape(lines * rows, k), float_shape(count, cells * width)),
        [SCALAR] + [WHOLE] * (len(ranges) + 4), (OUTSIDE, OUTSIDE),
        [
            pltpu.VMEM((lines, rows, k), jnp.float32), pltpu.VMEM((cells, count, width), jnp.float32), pltpu.VMEM((4, k, k), jnp.bfloat16),
            pltpu.SemaphoreType.DMA((lines,)), pltpu.SemaphoreType.DMA((cells,)),
        ],
        flops=18 * lines * rows * k * k, limit=24,
    )(spot, own, other, *ranges, co_own, co_other)


def finish_kernel(scale, spot_ref, own_ref, other_ref, middle_own_ref, middle_other_ref, out_ref, middle_ref):
    core, place = spot_ref[0], spot_ref[1]
    chips, extent = middle_own_ref.shape[0], middle_own_ref.shape[1]
    for i in range(chips):
        middle_ref[pl.ds(block_start(place, i, extent), extent), :] = middle_own_ref[i] + middle_other_ref[i]
    left = jnp.where(core == 0, own_ref[1], other_ref[1])
    right = jnp.where(core == 0, other_ref[1], own_ref[1])
    out_ref[...] = highest(highest(left, middle_ref[...]), right, 1, 1) * scale


def finish(spot, own, other, middle_own, middle_other, scale):
    k = own.shape[1]
    return call(
        functools.partial(finish_kernel, scale), float_shape(k, k), [SCALAR] + [WHOLE] * 4, WHOLE,
        [pltpu.VMEM((k, k), jnp.float32)], flops=24 * k * k * k,
    )(spot, own, other, middle_own, middle_other)


def per_device(window, range_test, co_test, core_left, core_right):
    rows_total = window.shape[0] * lax.axis_size("cell")
    cols_total = window.shape[1] * lax.axis_size("tm")
    k = range_test.shape[1]
    chips = lax.axis_size("cell") // 2
    groups = groups_of("cell", 1, 2)
    lines = [("tm", (bit,)) for bit in range(bits_of("tm"))]
    cell, line = lax.axis_index("cell"), lax.axis_index("tm")
    spot = jnp.stack([cell & 1, place_of(groups, cell), place_of(lines[:2], line), place_of(lines, line)]).astype(jnp.int32)

    def core_swap(values):
        return swap(values, "cell", 1)

    r3, r2, r1, r0, sent, kept = sketch_terms(spot, chips, window, range_test, co_test, core_left, core_right)
    far = swap(r3, "tm", 1)
    near = swap(r2, "tm", 1)
    pack = kept + core_swap(sent)
    sketch_z = core_terms(after(spot, pack), window, core_right, core_left)
    handed = swap(r1 + after(far, pack), "tm", 2)
    pack = scatter_sum(pack, groups)[0]
    handed, near, pack, sketch_z = lax.optimization_barrier((handed, near, pack, sketch_z))
    range_piece = (r0 + near + handed).reshape(lax.axis_size("tm") // 4, -1, r0.shape[1])
    if lines[2:]:
        rest = place_of(lines[2:], line)
        range_piece = jnp.stack([lax.dynamic_index_in_dim(range_piece, rest ^ f, 0, False) for f in range(range_piece.shape[0])])
    range_piece = scatter_sum(range_piece, lines[2:])
    width = window.shape[1] // (2 * chips)
    packed = pack_width(co_test.shape[0], width, k)
    co_piece = pack[:packed].reshape(packed, -1, width).swapaxes(0, 1).reshape(-1, width)
    fold = pack[None, packed:]

    gram_sent, gram_kept = gram_terms(spot, chips, range_piece[0], co_piece, (rows_total, cols_total))
    fold = whole_sum(fold, "tm")
    gram = scatter_sum(gram_kept + core_swap(gram_sent), groups)
    co_parts = gather(after(co_piece[None], gram), groups)
    gram, co_parts = lax.optimization_barrier((whole_sum(gram, "tm"), co_parts))
    rows = gram.shape[1]
    parts = gather(jnp.concatenate([gram, fold], axis=1), groups)
    co_own = jnp.concatenate(co_parts)
    fold = jnp.concatenate([part[:, rows:] for part in parts])

    range_parts = gather(after(range_piece, gram, fold), lines[1:])
    co_other, fold_other = core_swap(co_own), core_swap(fold)
    state = factor_start(spot, parts)
    state, fold_other = lax.optimization_barrier((state, fold_other))
    middle = middle_terms(spot, chips, sketch_z, fold, fold_other)
    middle = scatter_sum(middle, groups)
    state = factor_next((1, 2), *state)
    state, middle, range_parts = lax.optimization_barrier((state, middle, range_parts))
    range_all = jnp.concatenate(range_parts)
    for bit in range(bits_of("tm")):
        middle = middle + swap(middle, "tm", 1 << bit)
        if bit == 0:
            state = factor_next((2, state[1].shape[0] // BASE - 1), *state)
            state, middle, range_all = lax.optimization_barrier((state, middle, range_all))
    range_all = gather(range_all, lines[:1])
    own = factor_end(*state)
    own, middle = lax.optimization_barrier((own, middle))
    other = core_swap(own)
    range_basis, co_basis = bases(spot, own, other, range_all, co_own, co_other)
    middle, range_basis, co_basis = lax.optimization_barrier((gather(middle, groups), range_basis, co_basis))
    middle = jnp.concatenate(middle)
    core_out = finish(spot, own, other, middle, core_swap(middle), math.sqrt(rows_total * cols_total))
    return (range_basis, co_basis, core_out)


def solution(mesh):
    return jax.shard_map(
        per_device,
        mesh=mesh,
        in_specs=(P("cell", "tm"), P("tm", None), P(None, "cell"), P(None, "cell"), P(None, "tm")),
        out_specs=(P("cell", None), P(None, "tm"), P()),
        check_vma=False,
    )
```

```python
import functools
import math

import jax
import jax.numpy as jnp
from jax import lax
from jax.experimental import pallas as pl
from jax.experimental.pallas import tpu as pltpu
from jax.sharding import PartitionSpec as P

BASE = 64
LANES = 128
SUBLANES = 8
TILES = 4
WHOLE = pl.BlockSpec(memory_space=pltpu.VMEM)
SCALAR = pl.BlockSpec(memory_space=pltpu.SMEM)
OUTSIDE = pl.BlockSpec(memory_space=pl.ANY)


def highest(left, right, left_dim=1, right_dim=0):
    dims = (((left_dim,), (right_dim,)), ((), ()))
    return lax.dot_general(left, right, dims, precision=lax.Precision.HIGHEST, preferred_element_type=jnp.float32)


def split(values):
    top = values.astype(jnp.bfloat16)
    return top, (values - top.astype(jnp.float32)).astype(jnp.bfloat16)


def parts_dot(left, right, left_dim=1, right_dim=0):
    dims = (((left_dim,), (right_dim,)), ((), ()))
    pairs = ((left[0], right[0]), (left[0], right[1]), (left[1], right[0]))
    return sum(lax.dot_general(a, b, dims, preferred_element_type=jnp.float32) for a, b in pairs)


def float_shape(*shape):
    return jax.ShapeDtypeStruct(shape, jnp.float32)


def call(kernel, out_shape, in_specs, out_specs, scratch=(), flops=0, limit=24):
    return pl.pallas_call(
        kernel,
        out_shape=out_shape,
        in_specs=in_specs,
        out_specs=out_specs,
        scratch_shapes=list(scratch),
        compiler_params=pltpu.CompilerParams(vmem_limit_bytes=limit * 1024 * 1024),
        cost_estimate=pl.CostEstimate(flops=flops, bytes_accessed=4 * 1024 * 1024, transcendentals=0),
    )


def bits_of(axis):
    return int(math.log2(lax.axis_size(axis)))


def groups_of(axis, first, width):
    bits = list(range(first, bits_of(axis)))
    return [(axis, tuple(bits[i:i + width])) for i in range(0, len(bits), width)]


def place_of(groups, index):
    place = 0
    for _, bits in groups:
        place = (place << len(bits)) + sum(((index >> bit) & 1) << i for i, bit in enumerate(bits))
    return place


def swap(values, axis, mask):
    return lax.ppermute(values, axis, [(i, i ^ mask) for i in range(lax.axis_size(axis))])


def masks_of(bits):
    return [sum(((peer >> i) & 1) << bit for i, bit in enumerate(bits)) for peer in range(1 << len(bits))]


def pair_sum(parts):
    while len(parts) > 1:
        parts = [parts[i] + parts[i + 1] for i in range(0, len(parts), 2)]
    return parts[0]


def scatter_sum(blocks, groups):
    for axis, bits in groups:
        count = blocks.shape[0] >> len(bits)
        parts = [blocks[peer * count:(peer + 1) * count] for peer in range(1 << len(bits))]
        blocks = pair_sum([parts[0]] + [swap(part, axis, mask) for part, mask in zip(parts[1:], masks_of(bits)[1:])])
    return blocks


def gather(blocks, groups):
    parts = [blocks]
    for axis, bits in reversed(groups):
        blocks = jnp.concatenate(parts) if len(parts) > 1 else parts[0]
        parts = [blocks] + [swap(blocks, axis, mask) for mask in masks_of(bits)[1:]]
    return parts


def whole_sum(values, axis):
    for bit in range(bits_of(axis)):
        values = values + swap(values, axis, 1 << bit)
    return values


def after(values, *earlier):
    return lax.optimization_barrier((values,) + earlier)[0]


def block_start(place, block, extent):
    return pl.multiple_of((place ^ block) * extent, extent)


def put_blocks(refs, out_ref, place):
    count, extent = refs[0].shape[0], refs[0].shape[1]
    for i, ref in enumerate(refs):
        for j in range(count):
            out_ref[pl.ds(block_start(place, i * count + j, extent), extent), :] = ref[j]


def take_blocks(ref, out_ref, place, base=0):
    count, extent = out_ref.shape[0], out_ref.shape[1]
    for i in range(count):
        out_ref[i] = ref[pl.ds(pl.multiple_of(base + (place ^ i) * extent, extent), extent), :]


def pack_width(count, width, k):
    return count * width // k


def sketch_kernel(spot_ref, window_ref, test_ref, co_ref, left_ref, right_ref, r3_ref, r2_ref, r1_ref, r0_ref, sent_ref, kept_ref, held_ref, test_held_ref, co_held_ref, left_held_ref, right_held_ref, top_ref, rest_ref, range_done_ref, co_done_ref, lt_ref, rt_ref, fold_ref, window_sem, sem, range_sem, co_sem, fold_sem):
    core, place, line = spot_ref[0], spot_ref[1], spot_ref[2]
    tile = held_ref.shape[1]
    chips, _, k = kept_ref.shape
    count, cols = co_done_ref.shape
    width = cols // (2 * chips)
    packed = pack_width(count, width, k)
    extent = lt_ref.shape[0] // chips
    small = [(test_ref, test_held_ref), (co_ref, co_held_ref), (left_ref, left_held_ref), (right_ref, right_held_ref)]
    small = [pltpu.make_async_copy(a, b, sem.at[i]) for i, (a, b) in enumerate(small)]

    def window_copy(i):
        return pltpu.make_async_copy(window_ref.at[pl.ds(block_start(line, TILES - 1 - i, tile), tile)], held_ref.at[i], window_sem.at[i])

    small[0].start()
    window_copy(0).start()
    small[1].start()
    co_done_ref[...] = jnp.zeros_like(co_done_ref)
    lt_ref[...] = jnp.zeros_like(lt_ref)
    small[0].wait()
    window_copy(1).start()
    small[2].start()
    for i in range(2, TILES):
        window_copy(i).start()
    small[3].start()
    top_ref[...], rest_ref[...] = split(test_held_ref[...])
    range_outs = [pltpu.make_async_copy(range_done_ref.at[i], ref, range_sem.at[i]) for i, ref in enumerate((r3_ref, r2_ref, r1_ref, r0_ref))]
    small[1].wait()

    def step(i, carry):
        window_copy(i).wait()
        rows = split(held_ref[i])
        spot = pl.ds(block_start(line, TILES - 1 - i, tile), tile)
        done = parts_dot(rows, (top_ref[...], rest_ref[...]))
        range_done_ref[i] = done
        for block, copy in enumerate(range_outs):
            @pl.when(i == block)
            def _():
                copy.start()

        co_done_ref[...] += parts_dot(split(co_held_ref[:, spot]), rows)

        @pl.when(i == 0)
        def _():
            small[2].wait()

        lt_ref[...] += parts_dot(split(left_held_ref[:, spot]), split(done))
        return carry

    lax.fori_loop(0, TILES, step, 0)
    co_outs = []
    for out_ref, side in ((sent_ref, 1 - core), (kept_ref, core)):
        for i in range(chips):
            for j in range(count // packed):
                start = pl.multiple_of((side * chips + (place ^ i)) * width, width)
                part = co_done_ref.at[j * packed:(j + 1) * packed, pl.ds(start, width)]
                co_outs.append(pltpu.make_async_copy(part, out_ref.at[i, :packed, j * width:(j + 1) * width], co_sem.at[len(co_outs)]))
    for copy in co_outs:
        copy.start()
    small[3].wait()
    rt_ref[...] = parts_dot(split(right_held_ref[...]), split(co_done_ref[...]), 1, 1)
    first = core == 0
    fold_ref[0] = jnp.where(first, rt_ref[...], lt_ref[...])
    fold_ref[1] = jnp.where(first, lt_ref[...], rt_ref[...])
    fold_outs = []
    for side, out_ref in enumerate((sent_ref, kept_ref)):
        for i in range(chips):
            part = fold_ref.at[side, pl.ds(block_start(place, i, extent), extent)]
            fold_outs.append(pltpu.make_async_copy(part, out_ref.at[i, packed:], fold_sem.at[len(fold_outs)]))
    for copy in fold_outs:
        copy.start()
    for copy in range_outs + co_outs + fold_outs:
        copy.wait()


def sketch_terms(spot, chips, window, range_test, co_test, core_left, core_right):
    rows, cols = window.shape
    count, k, s_core = co_test.shape[0], range_test.shape[1], core_left.shape[0]
    width = cols // (2 * chips)
    block = pack_width(count, width, k) + s_core // chips
    return call(
        sketch_kernel, (float_shape(rows // TILES, k),) * 4 + (float_shape(chips, block, k),) * 2,
        [SCALAR] + [OUTSIDE] * 5, (OUTSIDE,) * 6,
        [
            pltpu.VMEM((TILES, rows // TILES, cols), jnp.float32), pltpu.VMEM((cols, k), jnp.float32), pltpu.VMEM((count, rows), jnp.float32),
            pltpu.VMEM((s_core, rows), jnp.float32), pltpu.VMEM((s_core, cols), jnp.float32),
            pltpu.VMEM((cols, k), jnp.bfloat16), pltpu.VMEM((cols, k), jnp.bfloat16),
            pltpu.VMEM((TILES, rows // TILES, k), jnp.float32), pltpu.VMEM((count, cols), jnp.float32),
            pltpu.VMEM((s_core, k), jnp.float32), pltpu.VMEM((s_core, k), jnp.float32), pltpu.VMEM((2, s_core, k), jnp.float32),
            pltpu.SemaphoreType.DMA((TILES,)), pltpu.SemaphoreType.DMA((4,)), pltpu.SemaphoreType.DMA((TILES,)),
            pltpu.SemaphoreType.DMA((2 * cols // width,)), pltpu.SemaphoreType.DMA((2 * chips,)),
        ],
        flops=12 * rows * cols * count, limit=56,
    )(spot, window, range_test, co_test, core_left, core_right)


def core_kernel(spot_ref, window_ref, right_ref, left_ref, z_ref, held_ref, right_held_ref, left_held_ref, image_ref, window_sem, right_sem, left_sem):
    width = held_ref.shape[2]
    tile = window_ref.shape[0] // TILES
    left_copy = pltpu.make_async_copy(left_ref, left_held_ref, left_sem)

    def copies(i):
        start = pl.multiple_of(i * width, width)
        return (
            pltpu.make_async_copy(right_ref.at[:, pl.ds(start, width)], right_held_ref.at[i], right_sem.at[i]),
            pltpu.make_async_copy(window_ref.at[:, pl.ds(start, width)], held_ref.at[i], window_sem.at[i]),
        )

    for i in range(TILES):
        for copy in copies(i):
            copy.start()
    left_copy.start()
    image_ref[...] = jnp.zeros_like(image_ref)

    def step(i, carry):
        for copy in copies(i):
            copy.wait()
        image_ref[...] += parts_dot(split(held_ref[i]), split(right_held_ref[i]), 1, 1)
        return carry

    lax.fori_loop(0, TILES, step, 0)
    left_copy.wait()
    z_ref[...] = jnp.zeros_like(z_ref)

    def fold(i, carry):
        start = pl.multiple_of(i * tile, tile)
        z_ref[...] += parts_dot(split(left_held_ref[:, pl.ds(start, tile)]), split(image_ref[pl.ds(start, tile), :]))
        return carry

    lax.fori_loop(0, TILES, fold, 0)


def core_terms(spot, window, core_right, core_left):
    rows, cols = window.shape
    s_core = core_right.shape[0]
    return call(
        core_kernel, float_shape(s_core, s_core), [SCALAR] + [OUTSIDE] * 3, WHOLE,
        [
            pltpu.VMEM((TILES, rows, cols // TILES), jnp.float32), pltpu.VMEM((TILES, s_core, cols // TILES), jnp.float32),
            pltpu.VMEM((s_core, rows), jnp.float32), pltpu.VMEM((rows, s_core), jnp.float32),
            pltpu.SemaphoreType.DMA((TILES,)), pltpu.SemaphoreType.DMA((TILES,)), pltpu.SemaphoreType.DMA,
        ],
        flops=9 * rows * cols * s_core, limit=56,
    )(spot, window, core_right, core_left)


def gram_kernel(scales, spot_ref, range_ref, co_ref, sent_ref, kept_ref, y_ref, w_ref):
    y_ref[...] = highest(range_ref[...], range_ref[...], 0, 0) / scales[0]
    w_ref[...] = highest(co_ref[...], co_ref[...], 1, 1) / scales[1]
    for owner, y_out, w_out in ((0, kept_ref, sent_ref), (1, sent_ref, kept_ref)):
        @pl.when(spot_ref[0] == owner)
        def _():
            take_blocks(y_ref, y_out, spot_ref[1])
            take_blocks(w_ref, w_out, spot_ref[1])


def gram_terms(spot, chips, range_piece, co_piece, scales):
    k = range_piece.shape[1]
    square = pltpu.VMEM((k, k), jnp.float32)
    return call(
        functools.partial(gram_kernel, scales), (float_shape(chips, k // chips, k),) * 2, [SCALAR, WHOLE, WHOLE], (WHOLE, WHOLE),
        [square, square], flops=24 * k * k * k,
    )(spot, range_piece, co_piece)


def middle_kernel(spot_ref, z_ref, own_ref, other_ref, blocks_ref, left_ref, right_ref, middle_ref):
    core, place = spot_ref[0], spot_ref[1]
    for owner, left_in, right_in in ((0, own_ref, other_ref), (1, other_ref, own_ref)):
        @pl.when(core == owner)
        def _():
            put_blocks([left_in], left_ref, place)
            put_blocks([right_in], right_ref, place)

    middle_ref[...] = parts_dot(split(parts_dot(split(left_ref[...]), split(z_ref[...]), 0, 0)), split(right_ref[...]))
    take_blocks(middle_ref, blocks_ref, place)


def middle_terms(spot, chips, sketch_z, own, other):
    s_core, k = sketch_z.shape[0], own.shape[2]
    return call(
        middle_kernel, float_shape(chips, k // chips, k), [SCALAR] + [WHOLE] * 3, WHOLE,
        [pltpu.VMEM((s_core, k), jnp.float32), pltpu.VMEM((s_core, k), jnp.float32), pltpu.VMEM((k, k), jnp.float32)],
        flops=6 * k * s_core * s_core,
    )(spot, sketch_z, own, other)


def spread_lane(values, lane):
    return jnp.broadcast_to(values[:, lane:lane + 1], values.shape)


def spread_row(values, row):
    return jnp.broadcast_to(values[row:row + 1, :], values.shape)


def factor_blocks(blocks):
    count = len(blocks)
    groups = BASE // SUBLANES
    rows = [[x[SUBLANES * g:SUBLANES * (g + 1)] for g in range(groups)] for x in blocks]
    sub = lax.broadcasted_iota(jnp.int32, (SUBLANES, LANES), 0)
    pivots = [[] for _ in blocks]
    for p in range(groups):
        cols = [{g: [spread_lane(rows[b][g], SUBLANES * p + k) for k in range(SUBLANES)] for g in range(p, groups)} for b in range(count)]
        found = [jnp.zeros((SUBLANES, LANES), jnp.float32)] * count
        for k in range(SUBLANES):
            for b in range(count):
                held = cols[b]
                pivot = spread_row(held[p][k], k)
                found[b] = jnp.where(sub == k, pivot, found[b])
                scale = 1.0 / pivot
                pivot_row = spread_row(rows[b][p], k)
                heads = [spread_row(held[p][j], k) for j in range(k + 1, SUBLANES)]
                for g in range(p, groups):
                    weight = held[g][k] * scale
                    if g == p:
                        weight = jnp.where(sub > k, weight, 0.0)
                    rows[b][g] = rows[b][g] - weight * pivot_row
                    for j in range(k + 1, SUBLANES):
                        held[g][j] = held[g][j] - weight * heads[j - k - 1]
        for b in range(count):
            pivots[b].append(found[b])
    return [jnp.concatenate([rows[b][g] * lax.rsqrt(pivots[b][g]) for g in range(groups)], axis=0) for b in range(count)]


def factor_steps(steps, inverse_ref, upper_ref):
    count, n = inverse_ref.shape[0], inverse_ref.shape[1]
    every = range(count)
    row_id = lax.broadcasted_iota(jnp.int32, (n, n), 0)
    col_id = lax.broadcasted_iota(jnp.int32, (n, n), 1)
    panel_col = lax.broadcasted_iota(jnp.int32, (BASE, n), 1)
    lane = lax.broadcasted_iota(jnp.int32, (BASE, LANES), 1)
    low = lax.broadcasted_iota(jnp.int32, (BASE, LANES), 0)

    def place(half, start):
        rest = [jnp.zeros((BASE, LANES), jnp.float32)] * (n // LANES - 1)
        return pltpu.roll(jnp.concatenate([jnp.where(lane < BASE, half, 0.0)] + rest, axis=1), start, 1)

    def step(t, carry):
        start = pl.multiple_of(t * BASE, BASE)
        back = jnp.where(t == 0, 0, n - start)
        panel = [inverse_ref[b, pl.ds(start, BASE), :] for b in every]
        whole = [inverse_ref[b] for b in every]
        block = [pltpu.roll(panel[b], back, 1)[:, :LANES] for b in every]
        block = [jnp.where(lane < BASE, block[b], jnp.where(lane - BASE == low, 1.0, 0.0)) for b in every]
        done = factor_blocks(block)
        inv = [pltpu.roll(done[b], LANES - BASE, 1) for b in every]
        inv_placed = [place(inv[b], start) for b in every]
        up_placed = place(done[0], start)
        inside = (panel_col >= start) & (panel_col < start + BASE)
        rows = [jnp.where(inside, inv_placed[b], highest(inv[b][:, :BASE], panel[b])) for b in every]
        right = [jnp.where(panel_col >= start + BASE, rows[b], 0.0) for b in every]
        spent = (row_id >= start + BASE) & (col_id >= start) & (col_id < start + BASE)
        left = [jnp.where(spent, 0.0, whole[b]) - highest(right[b], rows[b], 0, 0) for b in every]
        for b in every:
            inverse_ref[b] = left[b]
        for b in every:
            inverse_ref[b, pl.ds(start, BASE), :] = rows[b]
        upper_ref[pl.ds(start, BASE), :] = jnp.where(inside, up_placed, right[0])
        return carry

    lax.fori_loop(steps[0], steps[1], step, 0)


def factor_start_kernel(steps, peers, spot_ref, *refs):
    part_refs, (inverse_ref, upper_ref, fold_ref) = refs[:peers], refs[peers:]
    n = upper_ref.shape[0]
    inner = part_refs[0].shape[0]
    rows = n // (peers * inner)
    fold_rows = fold_ref.shape[0] // (peers * inner)
    for i, ref in enumerate(part_refs):
        for j in range(inner):
            block = i * inner + j
            inverse_ref[0, pl.ds(block_start(spot_ref[1], block, rows), rows), :] = ref[j, :rows]
            fold_ref[block * fold_rows:(block + 1) * fold_rows, :] = ref[j, rows:]
    inverse_ref[1] = highest(fold_ref[...], fold_ref[...], 0, 0)
    upper_ref[...] = jnp.zeros_like(upper_ref)
    factor_steps(steps, inverse_ref, upper_ref)


def factor_next_kernel(steps, begun_ref, begun_upper_ref, inverse_ref, upper_ref):
    inverse_ref[...] = begun_ref[...]
    upper_ref[...] = begun_upper_ref[...]
    factor_steps(steps, inverse_ref, upper_ref)


def factor_end_kernel(steps, begun_ref, begun_upper_ref, out_ref, inverse_ref, upper_ref):
    n = upper_ref.shape[0]
    inverse_ref[...] = begun_ref[...]
    upper_ref[...] = begun_upper_ref[...]
    factor_steps(steps, inverse_ref, upper_ref)
    row_id = lax.broadcasted_iota(jnp.int32, (n, n), 0)
    col_id = lax.broadcasted_iota(jnp.int32, (n, n), 1)
    out_ref[0] = jnp.where(row_id >= col_id, inverse_ref[0], 0.0)
    upper = jnp.where(row_id <= col_id, upper_ref[...], 0.0)
    image = jnp.where(row_id >= col_id, inverse_ref[1], 0.0)
    out_ref[1] = highest(highest(upper, image, 1, 1), image)


def factor_start(spot, parts):
    n = parts[0].shape[2]
    blocks = len(parts) * parts[0].shape[0]
    return call(
        functools.partial(factor_start_kernel, (0, 1), len(parts)), (float_shape(2, n, n), float_shape(n, n)),
        [SCALAR] + [WHOLE] * len(parts), (WHOLE, WHOLE), [pltpu.VMEM((blocks * parts[0].shape[1] - n, n), jnp.float32)], flops=n * n * n * 100,
    )(spot, *parts)


def factor_next(steps, begun, upper):
    n = upper.shape[0]
    return call(
        functools.partial(factor_next_kernel, steps), (float_shape(2, n, n), float_shape(n, n)), [WHOLE, WHOLE], (WHOLE, WHOLE), flops=n * n * n * 100,
    )(begun, upper)


def factor_end(begun, upper):
    n = upper.shape[0]
    return call(
        functools.partial(factor_end_kernel, (n // BASE - 1, n // BASE)), float_shape(2, n, n), [WHOLE, WHOLE], WHOLE,
        [pltpu.VMEM((2, n, n), jnp.float32), pltpu.VMEM((n, n), jnp.float32)], flops=n * n * n * 100,
    )(begun, upper)


def basis_kernel(peers, spot_ref, own_ref, other_ref, *refs):
    range_refs, (co_own_ref, co_other_ref, range_out_ref, co_out_ref, range_done_ref, co_done_ref, side_ref, range_sem, co_sem) = refs[:peers], refs[peers:]
    core, place, line = spot_ref[0], spot_ref[1], spot_ref[3]
    inner, rows, _ = range_refs[0].shape
    chips, _, width = co_own_ref.shape
    first = core == 0
    side_ref[0], side_ref[1] = split(jnp.where(first, own_ref[0], other_ref[0]))
    side_ref[2], side_ref[3] = split(jnp.where(first, other_ref[0], own_ref[0]))

    def range_out(f):
        return pltpu.make_async_copy(range_done_ref.at[f], range_out_ref.at[pl.ds(block_start(line, f, rows), rows)], range_sem.at[f])

    def co_out(f):
        column = jnp.where(f < chips, core, 1 - core) * chips + (place ^ (f % chips))
        return pltpu.make_async_copy(co_done_ref.at[f], co_out_ref.at[:, pl.ds(pl.multiple_of(column * width, width), width)], co_sem.at[f])

    for i, ref in enumerate(range_refs):
        def range_step(j, carry, i=i, ref=ref):
            f = i * inner + j
            range_done_ref[f] = parts_dot(split(ref[j]), (side_ref[0], side_ref[1]), 1, 1)
            range_out(f).start()
            return carry

        lax.fori_loop(0, inner, range_step, 0)
    for i, ref in enumerate((co_own_ref, co_other_ref)):
        def co_step(j, carry, i=i, ref=ref):
            f = i * chips + j
            co_done_ref[f] = parts_dot((side_ref[2], side_ref[3]), split(ref[j]))
            co_out(f).start()
            return carry

        lax.fori_loop(0, chips, co_step, 0)
    for f in range(peers * inner):
        range_out(f).wait()
    for f in range(2 * chips):
        co_out(f).wait()


def bases(spot, own, other, ranges, co_own, co_other):
    inner, rows, k = ranges[0].shape
    chips, count, width = co_own.shape
    lines, cells = inner * len(ranges), 2 * chips
    return call(
        functools.partial(basis_kernel, len(ranges)), (float_shape(lines * rows, k), float_shape(count, cells * width)),
        [SCALAR] + [WHOLE] * (len(ranges) + 4), (OUTSIDE, OUTSIDE),
        [
            pltpu.VMEM((lines, rows, k), jnp.float32), pltpu.VMEM((cells, count, width), jnp.float32), pltpu.VMEM((4, k, k), jnp.bfloat16),
            pltpu.SemaphoreType.DMA((lines,)), pltpu.SemaphoreType.DMA((cells,)),
        ],
        flops=18 * lines * rows * k * k, limit=24,
    )(spot, own, other, *ranges, co_own, co_other)


def finish_kernel(scale, spot_ref, own_ref, other_ref, middle_own_ref, middle_other_ref, out_ref, middle_ref):
    core, place = spot_ref[0], spot_ref[1]
    chips, extent = middle_own_ref.shape[0], middle_own_ref.shape[1]
    for i in range(chips):
        middle_ref[pl.ds(block_start(place, i, extent), extent), :] = middle_own_ref[i] + middle_other_ref[i]
    left = jnp.where(core == 0, own_ref[1], other_ref[1])
    right = jnp.where(core == 0, other_ref[1], own_ref[1])
    out_ref[...] = highest(highest(left, middle_ref[...]), right, 1, 1) * scale


def finish(spot, own, other, middle_own, middle_other, scale):
    k = own.shape[1]
    return call(
        functools.partial(finish_kernel, scale), float_shape(k, k), [SCALAR] + [WHOLE] * 4, WHOLE,
        [pltpu.VMEM((k, k), jnp.float32)], flops=24 * k * k * k,
    )(spot, own, other, middle_own, middle_other)


def per_device(window, range_test, co_test, core_left, core_right):
    rows_total = window.shape[0] * lax.axis_size("cell")
    cols_total = window.shape[1] * lax.axis_size("tm")
    k = range_test.shape[1]
    chips = lax.axis_size("cell") // 2
    groups = groups_of("cell", 1, 2)
    lines = [("tm", (bit,)) for bit in range(bits_of("tm"))]
    cell, line = lax.axis_index("cell"), lax.axis_index("tm")
    spot = jnp.stack([cell & 1, place_of(groups, cell), place_of(lines[:2], line), place_of(lines, line)]).astype(jnp.int32)

    def core_swap(values):
        return swap(values, "cell", 1)

    r3, r2, r1, r0, sent, kept = sketch_terms(spot, chips, window, range_test, co_test, core_left, core_right)
    far = swap(r3, "tm", 1)
    near = swap(r2, "tm", 1)
    pack = kept + core_swap(sent)
    sketch_z = core_terms(after(spot, pack), window, core_right, core_left)
    handed = swap(r1 + after(far, pack), "tm", 2)
    pack = scatter_sum(pack, groups)[0]
    handed, near, pack, sketch_z = lax.optimization_barrier((handed, near, pack, sketch_z))
    range_piece = (r0 + near + handed).reshape(lax.axis_size("tm") // 4, -1, r0.shape[1])
    if lines[2:]:
        rest = place_of(lines[2:], line)
        range_piece = jnp.stack([lax.dynamic_index_in_dim(range_piece, rest ^ f, 0, False) for f in range(range_piece.shape[0])])
    range_piece = scatter_sum(range_piece, lines[2:])
    width = window.shape[1] // (2 * chips)
    packed = pack_width(co_test.shape[0], width, k)
    co_piece = pack[:packed].reshape(packed, -1, width).swapaxes(0, 1).reshape(-1, width)
    fold = pack[None, packed:]

    gram_sent, gram_kept = gram_terms(spot, chips, range_piece[0], co_piece, (rows_total, cols_total))
    fold = whole_sum(fold, "tm")
    gram = scatter_sum(gram_kept + core_swap(gram_sent), groups)
    co_parts = gather(after(co_piece[None], gram), groups)
    gram, co_parts = lax.optimization_barrier((whole_sum(gram, "tm"), co_parts))
    rows = gram.shape[1]
    parts = gather(jnp.concatenate([gram, fold], axis=1), groups)
    co_own = jnp.concatenate(co_parts)
    fold = jnp.concatenate([part[:, rows:] for part in parts])

    range_parts = gather(after(range_piece, gram, fold), lines[1:])
    range_near = swap(range_parts[0], "tm", 1)
    co_other, fold_other = core_swap(co_own), core_swap(fold)
    state = factor_start(spot, parts)
    state, fold_other = lax.optimization_barrier((state, fold_other))
    middle = middle_terms(spot, chips, sketch_z, fold, fold_other)
    middle = scatter_sum(middle, groups)
    state = factor_next((1, 2), *state)
    state, middle, range_parts, range_near = lax.optimization_barrier((state, middle, range_parts, range_near))
    for bit in range(bits_of("tm")):
        middle = middle + swap(middle, "tm", 1 << bit)
        if bit == 0:
            state = factor_next((2, state[1].shape[0] // BASE - 1), *state)
            state, middle, range_parts = lax.optimization_barrier((state, middle, range_parts))
    corners = [swap(part, "tm", 1) for part in range_parts[1:]]
    own = factor_end(*state)
    own, middle, corners = lax.optimization_barrier((own, middle, corners))
    range_all = range_parts + [range_near] + corners
    other = core_swap(own)
    range_basis, co_basis = bases(spot, own, other, range_all, co_own, co_other)
    middle, range_basis, co_basis = lax.optimization_barrier((gather(middle, groups), range_basis, co_basis))
    middle = jnp.concatenate(middle)
    core_out = finish(spot, own, other, middle, core_swap(middle), math.sqrt(rows_total * cols_total))
    return (range_basis, co_basis, core_out)


def solution(mesh):
    return jax.shard_map(
        per_device,
        mesh=mesh,
        in_specs=(P("cell", "tm"), P("tm", None), P(None, "cell"), P(None, "cell"), P(None, "tm")),
        out_specs=(P("cell", None), P(None, "tm"), P()),
        check_vma=False,
    )
```

```python
import functools
import math

import jax
import jax.numpy as jnp
from jax import lax
from jax.experimental import pallas as pl
from jax.experimental.pallas import tpu as pltpu
from jax.sharding import PartitionSpec as P

BASE = 64
LANES = 128
SUBLANES = 8
TILES = 4
WHOLE = pl.BlockSpec(memory_space=pltpu.VMEM)
SCALAR = pl.BlockSpec(memory_space=pltpu.SMEM)
OUTSIDE = pl.BlockSpec(memory_space=pl.ANY)


def highest(left, right, left_dim=1, right_dim=0):
    dims = (((left_dim,), (right_dim,)), ((), ()))
    return lax.dot_general(left, right, dims, precision=lax.Precision.HIGHEST, preferred_element_type=jnp.float32)


def split(values):
    top = values.astype(jnp.bfloat16)
    return top, (values - top.astype(jnp.float32)).astype(jnp.bfloat16)


def parts_dot(left, right, left_dim=1, right_dim=0):
    dims = (((left_dim,), (right_dim,)), ((), ()))
    pairs = ((left[0], right[0]), (left[0], right[1]), (left[1], right[0]))
    return sum(lax.dot_general(a, b, dims, preferred_element_type=jnp.float32) for a, b in pairs)


def float_shape(*shape):
    return jax.ShapeDtypeStruct(shape, jnp.float32)


def call(kernel, out_shape, in_specs, out_specs, scratch=(), flops=0, limit=24):
    return pl.pallas_call(
        kernel,
        out_shape=out_shape,
        in_specs=in_specs,
        out_specs=out_specs,
        scratch_shapes=list(scratch),
        compiler_params=pltpu.CompilerParams(vmem_limit_bytes=limit * 1024 * 1024),
        cost_estimate=pl.CostEstimate(flops=flops, bytes_accessed=4 * 1024 * 1024, transcendentals=0),
    )


def bits_of(axis):
    return int(math.log2(lax.axis_size(axis)))


def groups_of(axis, first, width):
    bits = list(range(first, bits_of(axis)))
    return [(axis, tuple(bits[i:i + width])) for i in range(0, len(bits), width)]


def place_of(groups, index):
    place = 0
    for _, bits in groups:
        place = (place << len(bits)) + sum(((index >> bit) & 1) << i for i, bit in enumerate(bits))
    return place


def swap(values, axis, mask):
    return lax.ppermute(values, axis, [(i, i ^ mask) for i in range(lax.axis_size(axis))])


def masks_of(bits):
    return [sum(((peer >> i) & 1) << bit for i, bit in enumerate(bits)) for peer in range(1 << len(bits))]


def pair_sum(parts):
    while len(parts) > 1:
        parts = [parts[i] + parts[i + 1] for i in range(0, len(parts), 2)]
    return parts[0]


def scatter_sum(blocks, groups):
    for axis, bits in groups:
        count = blocks.shape[0] >> len(bits)
        parts = [blocks[peer * count:(peer + 1) * count] for peer in range(1 << len(bits))]
        blocks = pair_sum([parts[0]] + [swap(part, axis, mask) for part, mask in zip(parts[1:], masks_of(bits)[1:])])
    return blocks


def gather(blocks, groups):
    parts = [blocks]
    for axis, bits in reversed(groups):
        blocks = jnp.concatenate(parts) if len(parts) > 1 else parts[0]
        parts = [blocks] + [swap(blocks, axis, mask) for mask in masks_of(bits)[1:]]
    return parts


def whole_sum(values, axis):
    for bit in range(bits_of(axis)):
        values = values + swap(values, axis, 1 << bit)
    return values


def after(values, *earlier):
    return lax.optimization_barrier((values,) + earlier)[0]


def block_start(place, block, extent):
    return pl.multiple_of((place ^ block) * extent, extent)


def put_blocks(refs, out_ref, place):
    count, extent = refs[0].shape[0], refs[0].shape[1]
    for i, ref in enumerate(refs):
        for j in range(count):
            out_ref[pl.ds(block_start(place, i * count + j, extent), extent), :] = ref[j]


def take_blocks(ref, out_ref, place, base=0):
    count, extent = out_ref.shape[0], out_ref.shape[1]
    for i in range(count):
        out_ref[i] = ref[pl.ds(pl.multiple_of(base + (place ^ i) * extent, extent), extent), :]


def pack_width(count, width, k):
    return count * width // k


def sketch_kernel(spot_ref, window_ref, test_ref, co_ref, left_ref, right_ref, r3_ref, r2_ref, r1_ref, r0_ref, sent_ref, kept_ref, held_ref, test_held_ref, co_held_ref, left_held_ref, right_held_ref, top_ref, rest_ref, range_done_ref, co_done_ref, lt_ref, rt_ref, fold_ref, window_sem, sem, range_sem, co_sem, fold_sem):
    core, place, line = spot_ref[0], spot_ref[1], spot_ref[2]
    tile = held_ref.shape[1]
    chips, _, k = kept_ref.shape
    count, cols = co_done_ref.shape
    width = cols // (2 * chips)
    packed = pack_width(count, width, k)
    extent = lt_ref.shape[0] // chips
    small = [(test_ref, test_held_ref), (co_ref, co_held_ref), (left_ref, left_held_ref), (right_ref, right_held_ref)]
    small = [pltpu.make_async_copy(a, b, sem.at[i]) for i, (a, b) in enumerate(small)]

    def window_copy(i):
        return pltpu.make_async_copy(window_ref.at[pl.ds(block_start(line, TILES - 1 - i, tile), tile)], held_ref.at[i], window_sem.at[i])

    small[0].start()
    window_copy(0).start()
    small[1].start()
    co_done_ref[...] = jnp.zeros_like(co_done_ref)
    lt_ref[...] = jnp.zeros_like(lt_ref)
    small[0].wait()
    window_copy(1).start()
    small[2].start()
    for i in range(2, TILES):
        window_copy(i).start()
    small[3].start()
    top_ref[...], rest_ref[...] = split(test_held_ref[...])
    range_outs = [pltpu.make_async_copy(range_done_ref.at[i], ref, range_sem.at[i]) for i, ref in enumerate((r3_ref, r2_ref, r1_ref, r0_ref))]
    small[1].wait()

    def step(i, carry):
        window_copy(i).wait()
        rows = split(held_ref[i])
        spot = pl.ds(block_start(line, TILES - 1 - i, tile), tile)
        done = parts_dot(rows, (top_ref[...], rest_ref[...]))
        range_done_ref[i] = done
        for block, copy in enumerate(range_outs):
            @pl.when(i == block)
            def _():
                copy.start()

        co_done_ref[...] += parts_dot(split(co_held_ref[:, spot]), rows)

        @pl.when(i == 0)
        def _():
            small[2].wait()

        lt_ref[...] += parts_dot(split(left_held_ref[:, spot]), split(done))
        return carry

    lax.fori_loop(0, TILES, step, 0)
    co_outs = []
    for out_ref, side in ((sent_ref, 1 - core), (kept_ref, core)):
        for i in range(chips):
            for j in range(count // packed):
                start = pl.multiple_of((side * chips + (place ^ i)) * width, width)
                part = co_done_ref.at[j * packed:(j + 1) * packed, pl.ds(start, width)]
                co_outs.append(pltpu.make_async_copy(part, out_ref.at[i, :packed, j * width:(j + 1) * width], co_sem.at[len(co_outs)]))
    for copy in co_outs:
        copy.start()
    small[3].wait()
    rt_ref[...] = parts_dot(split(right_held_ref[...]), split(co_done_ref[...]), 1, 1)
    first = core == 0
    fold_ref[0] = jnp.where(first, rt_ref[...], lt_ref[...])
    fold_ref[1] = jnp.where(first, lt_ref[...], rt_ref[...])
    fold_outs = []
    for side, out_ref in enumerate((sent_ref, kept_ref)):
        for i in range(chips):
            part = fold_ref.at[side, pl.ds(block_start(place, i, extent), extent)]
            fold_outs.append(pltpu.make_async_copy(part, out_ref.at[i, packed:], fold_sem.at[len(fold_outs)]))
    for copy in fold_outs:
        copy.start()
    for copy in range_outs + co_outs + fold_outs:
        copy.wait()


def sketch_terms(spot, chips, window, range_test, co_test, core_left, core_right):
    rows, cols = window.shape
    count, k, s_core = co_test.shape[0], range_test.shape[1], core_left.shape[0]
    width = cols // (2 * chips)
    block = pack_width(count, width, k) + s_core // chips
    return call(
        sketch_kernel, (float_shape(rows // TILES, k),) * 4 + (float_shape(chips, block, k),) * 2,
        [SCALAR] + [OUTSIDE] * 5, (OUTSIDE,) * 6,
        [
            pltpu.VMEM((TILES, rows // TILES, cols), jnp.float32), pltpu.VMEM((cols, k), jnp.float32), pltpu.VMEM((count, rows), jnp.float32),
            pltpu.VMEM((s_core, rows), jnp.float32), pltpu.VMEM((s_core, cols), jnp.float32),
            pltpu.VMEM((cols, k), jnp.bfloat16), pltpu.VMEM((cols, k), jnp.bfloat16),
            pltpu.VMEM((TILES, rows // TILES, k), jnp.float32), pltpu.VMEM((count, cols), jnp.float32),
            pltpu.VMEM((s_core, k), jnp.float32), pltpu.VMEM((s_core, k), jnp.float32), pltpu.VMEM((2, s_core, k), jnp.float32),
            pltpu.SemaphoreType.DMA((TILES,)), pltpu.SemaphoreType.DMA((4,)), pltpu.SemaphoreType.DMA((TILES,)),
            pltpu.SemaphoreType.DMA((2 * cols // width,)), pltpu.SemaphoreType.DMA((2 * chips,)),
        ],
        flops=12 * rows * cols * count, limit=56,
    )(spot, window, range_test, co_test, core_left, core_right)


def core_kernel(spot_ref, window_ref, right_ref, left_ref, z_ref, held_ref, right_held_ref, left_held_ref, image_ref, window_sem, right_sem, left_sem):
    width = held_ref.shape[2]
    tile = window_ref.shape[0] // TILES
    left_copy = pltpu.make_async_copy(left_ref, left_held_ref, left_sem)

    def copies(i):
        start = pl.multiple_of(i * width, width)
        return (
            pltpu.make_async_copy(right_ref.at[:, pl.ds(start, width)], right_held_ref.at[i], right_sem.at[i]),
            pltpu.make_async_copy(window_ref.at[:, pl.ds(start, width)], held_ref.at[i], window_sem.at[i]),
        )

    for i in range(TILES):
        for copy in copies(i):
            copy.start()
    left_copy.start()
    image_ref[...] = jnp.zeros_like(image_ref)

    def step(i, carry):
        for copy in copies(i):
            copy.wait()
        image_ref[...] += parts_dot(split(held_ref[i]), split(right_held_ref[i]), 1, 1)
        return carry

    lax.fori_loop(0, TILES, step, 0)
    left_copy.wait()
    z_ref[...] = jnp.zeros_like(z_ref)

    def fold(i, carry):
        start = pl.multiple_of(i * tile, tile)
        z_ref[...] += parts_dot(split(left_held_ref[:, pl.ds(start, tile)]), split(image_ref[pl.ds(start, tile), :]))
        return carry

    lax.fori_loop(0, TILES, fold, 0)


def core_terms(spot, window, core_right, core_left):
    rows, cols = window.shape
    s_core = core_right.shape[0]
    return call(
        core_kernel, float_shape(s_core, s_core), [SCALAR] + [OUTSIDE] * 3, WHOLE,
        [
            pltpu.VMEM((TILES, rows, cols // TILES), jnp.float32), pltpu.VMEM((TILES, s_core, cols // TILES), jnp.float32),
            pltpu.VMEM((s_core, rows), jnp.float32), pltpu.VMEM((rows, s_core), jnp.float32),
            pltpu.SemaphoreType.DMA((TILES,)), pltpu.SemaphoreType.DMA((TILES,)), pltpu.SemaphoreType.DMA,
        ],
        flops=9 * rows * cols * s_core, limit=56,
    )(spot, window, core_right, core_left)


def gram_kernel(scales, spot_ref, range_ref, co_ref, sent_ref, kept_ref, y_ref, w_ref):
    y_ref[...] = highest(range_ref[...], range_ref[...], 0, 0) / scales[0]
    w_ref[...] = highest(co_ref[...], co_ref[...], 1, 1) / scales[1]
    for owner, y_out, w_out in ((0, kept_ref, sent_ref), (1, sent_ref, kept_ref)):
        @pl.when(spot_ref[0] == owner)
        def _():
            take_blocks(y_ref, y_out, spot_ref[1])
            take_blocks(w_ref, w_out, spot_ref[1])


def gram_terms(spot, chips, range_piece, co_piece, scales):
    k = range_piece.shape[1]
    square = pltpu.VMEM((k, k), jnp.float32)
    return call(
        functools.partial(gram_kernel, scales), (float_shape(chips, k // chips, k),) * 2, [SCALAR, WHOLE, WHOLE], (WHOLE, WHOLE),
        [square, square], flops=24 * k * k * k,
    )(spot, range_piece, co_piece)


def middle_kernel(spot_ref, z_ref, own_ref, other_ref, blocks_ref, left_ref, right_ref, middle_ref):
    core, place = spot_ref[0], spot_ref[1]
    for owner, left_in, right_in in ((0, own_ref, other_ref), (1, other_ref, own_ref)):
        @pl.when(core == owner)
        def _():
            put_blocks([left_in], left_ref, place)
            put_blocks([right_in], right_ref, place)

    middle_ref[...] = parts_dot(split(parts_dot(split(left_ref[...]), split(z_ref[...]), 0, 0)), split(right_ref[...]))
    take_blocks(middle_ref, blocks_ref, place)


def middle_terms(spot, chips, sketch_z, own, other):
    s_core, k = sketch_z.shape[0], own.shape[2]
    return call(
        middle_kernel, float_shape(chips, k // chips, k), [SCALAR] + [WHOLE] * 3, WHOLE,
        [pltpu.VMEM((s_core, k), jnp.float32), pltpu.VMEM((s_core, k), jnp.float32), pltpu.VMEM((k, k), jnp.float32)],
        flops=6 * k * s_core * s_core,
    )(spot, sketch_z, own, other)


def spread_lane(values, lane):
    return jnp.broadcast_to(values[:, lane:lane + 1], values.shape)


def spread_row(values, row):
    return jnp.broadcast_to(values[row:row + 1, :], values.shape)


def factor_blocks(blocks):
    count = len(blocks)
    groups = BASE // SUBLANES
    rows = [[x[SUBLANES * g:SUBLANES * (g + 1)] for g in range(groups)] for x in blocks]
    sub = lax.broadcasted_iota(jnp.int32, (SUBLANES, LANES), 0)
    pivots = [[] for _ in blocks]
    for p in range(groups):
        cols = [{g: [spread_lane(rows[b][g], SUBLANES * p + k) for k in range(SUBLANES)] for g in range(p, groups)} for b in range(count)]
        found = [jnp.zeros((SUBLANES, LANES), jnp.float32)] * count
        for k in range(SUBLANES):
            for b in range(count):
                held = cols[b]
                pivot = spread_row(held[p][k], k)
                found[b] = jnp.where(sub == k, pivot, found[b])
                scale = 1.0 / pivot
                pivot_row = spread_row(rows[b][p], k)
                heads = [spread_row(held[p][j], k) for j in range(k + 1, SUBLANES)]
                for g in range(p, groups):
                    weight = held[g][k] * scale
                    if g == p:
                        weight = jnp.where(sub > k, weight, 0.0)
                    rows[b][g] = rows[b][g] - weight * pivot_row
                    for j in range(k + 1, SUBLANES):
                        held[g][j] = held[g][j] - weight * heads[j - k - 1]
        for b in range(count):
            pivots[b].append(found[b])
    return [jnp.concatenate([rows[b][g] * lax.rsqrt(pivots[b][g]) for g in range(groups)], axis=0) for b in range(count)]


def factor_steps(steps, inverse_ref, upper_ref):
    count, n = inverse_ref.shape[0], inverse_ref.shape[1]
    every = range(count)
    row_id = lax.broadcasted_iota(jnp.int32, (n, n), 0)
    col_id = lax.broadcasted_iota(jnp.int32, (n, n), 1)
    panel_col = lax.broadcasted_iota(jnp.int32, (BASE, n), 1)
    lane = lax.broadcasted_iota(jnp.int32, (BASE, LANES), 1)
    low = lax.broadcasted_iota(jnp.int32, (BASE, LANES), 0)

    def place(half, start):
        rest = [jnp.zeros((BASE, LANES), jnp.float32)] * (n // LANES - 1)
        return pltpu.roll(jnp.concatenate([jnp.where(lane < BASE, half, 0.0)] + rest, axis=1), start, 1)

    def step(t, carry):
        start = pl.multiple_of(t * BASE, BASE)
        back = jnp.where(t == 0, 0, n - start)
        panel = [inverse_ref[b, pl.ds(start, BASE), :] for b in every]
        whole = [inverse_ref[b] for b in every]
        block = [pltpu.roll(panel[b], back, 1)[:, :LANES] for b in every]
        block = [jnp.where(lane < BASE, block[b], jnp.where(lane - BASE == low, 1.0, 0.0)) for b in every]
        done = factor_blocks(block)
        inv = [pltpu.roll(done[b], LANES - BASE, 1) for b in every]
        inv_placed = [place(inv[b], start) for b in every]
        up_placed = place(done[0], start)
        inside = (panel_col >= start) & (panel_col < start + BASE)
        rows = [jnp.where(inside, inv_placed[b], highest(inv[b][:, :BASE], panel[b])) for b in every]
        right = [jnp.where(panel_col >= start + BASE, rows[b], 0.0) for b in every]
        spent = (row_id >= start + BASE) & (col_id >= start) & (col_id < start + BASE)
        left = [jnp.where(spent, 0.0, whole[b]) - highest(right[b], rows[b], 0, 0) for b in every]
        for b in every:
            inverse_ref[b] = left[b]
        for b in every:
            inverse_ref[b, pl.ds(start, BASE), :] = rows[b]
        upper_ref[pl.ds(start, BASE), :] = jnp.where(inside, up_placed, right[0])
        return carry

    lax.fori_loop(steps[0], steps[1], step, 0)


def factor_start_kernel(steps, peers, spot_ref, *refs):
    part_refs, (inverse_ref, upper_ref, fold_ref) = refs[:peers], refs[peers:]
    n = upper_ref.shape[0]
    inner = part_refs[0].shape[0]
    rows = n // (peers * inner)
    fold_rows = fold_ref.shape[0] // (peers * inner)
    for i, ref in enumerate(part_refs):
        for j in range(inner):
            block = i * inner + j
            inverse_ref[0, pl.ds(block_start(spot_ref[1], block, rows), rows), :] = ref[j, :rows]
            fold_ref[block * fold_rows:(block + 1) * fold_rows, :] = ref[j, rows:]
    inverse_ref[1] = highest(fold_ref[...], fold_ref[...], 0, 0)
    upper_ref[...] = jnp.zeros_like(upper_ref)
    factor_steps(steps, inverse_ref, upper_ref)


def factor_next_kernel(steps, begun_ref, begun_upper_ref, inverse_ref, upper_ref):
    inverse_ref[...] = begun_ref[...]
    upper_ref[...] = begun_upper_ref[...]
    factor_steps(steps, inverse_ref, upper_ref)


def factor_end_kernel(steps, begun_ref, begun_upper_ref, out_ref, inverse_ref, upper_ref):
    n = upper_ref.shape[0]
    inverse_ref[...] = begun_ref[...]
    upper_ref[...] = begun_upper_ref[...]
    factor_steps(steps, inverse_ref, upper_ref)
    row_id = lax.broadcasted_iota(jnp.int32, (n, n), 0)
    col_id = lax.broadcasted_iota(jnp.int32, (n, n), 1)
    out_ref[0] = jnp.where(row_id >= col_id, inverse_ref[0], 0.0)
    upper = jnp.where(row_id <= col_id, upper_ref[...], 0.0)
    image = jnp.where(row_id >= col_id, inverse_ref[1], 0.0)
    out_ref[1] = highest(highest(upper, image, 1, 1), image)


def factor_start(spot, parts):
    n = parts[0].shape[2]
    blocks = len(parts) * parts[0].shape[0]
    return call(
        functools.partial(factor_start_kernel, (0, 1), len(parts)), (float_shape(2, n, n), float_shape(n, n)),
        [SCALAR] + [WHOLE] * len(parts), (WHOLE, WHOLE), [pltpu.VMEM((blocks * parts[0].shape[1] - n, n), jnp.float32)], flops=n * n * n * 100,
    )(spot, *parts)


def factor_next(steps, begun, upper):
    n = upper.shape[0]
    return call(
        functools.partial(factor_next_kernel, steps), (float_shape(2, n, n), float_shape(n, n)), [WHOLE, WHOLE], (WHOLE, WHOLE), flops=n * n * n * 100,
    )(begun, upper)


def factor_end(begun, upper):
    n = upper.shape[0]
    return call(
        functools.partial(factor_end_kernel, (n // BASE - 1, n // BASE)), float_shape(2, n, n), [WHOLE, WHOLE], WHOLE,
        [pltpu.VMEM((2, n, n), jnp.float32), pltpu.VMEM((n, n), jnp.float32)], flops=n * n * n * 100,
    )(begun, upper)


def basis_kernel(peers, spot_ref, own_ref, other_ref, *refs):
    range_refs, (co_own_ref, co_other_ref, range_out_ref, co_out_ref, range_done_ref, co_done_ref, side_ref, range_sem, co_sem) = refs[:peers], refs[peers:]
    core, place, line = spot_ref[0], spot_ref[1], spot_ref[3]
    inner, rows, _ = range_refs[0].shape
    chips, _, width = co_own_ref.shape
    first = core == 0
    side_ref[0], side_ref[1] = split(jnp.where(first, own_ref[0], other_ref[0]))
    side_ref[2], side_ref[3] = split(jnp.where(first, other_ref[0], own_ref[0]))

    def range_out(f):
        return pltpu.make_async_copy(range_done_ref.at[f], range_out_ref.at[pl.ds(block_start(line, f, rows), rows)], range_sem.at[f])

    def co_out(f):
        column = jnp.where(f < chips, core, 1 - core) * chips + (place ^ (f % chips))
        return pltpu.make_async_copy(co_done_ref.at[f], co_out_ref.at[:, pl.ds(pl.multiple_of(column * width, width), width)], co_sem.at[f])

    for i, ref in enumerate(range_refs):
        def range_step(j, carry, i=i, ref=ref):
            f = i * inner + j
            range_done_ref[f] = parts_dot(split(ref[j]), (side_ref[0], side_ref[1]), 1, 1)
            range_out(f).start()
            return carry

        lax.fori_loop(0, inner, range_step, 0)
    for i, ref in enumerate((co_own_ref, co_other_ref)):
        def co_step(j, carry, i=i, ref=ref):
            f = i * chips + j
            co_done_ref[f] = parts_dot((side_ref[2], side_ref[3]), split(ref[j]))
            co_out(f).start()
            return carry

        lax.fori_loop(0, chips, co_step, 0)
    for f in range(peers * inner):
        range_out(f).wait()
    for f in range(2 * chips):
        co_out(f).wait()


def bases(spot, own, other, ranges, co_own, co_other):
    inner, rows, k = ranges[0].shape
    chips, count, width = co_own.shape
    lines, cells = inner * len(ranges), 2 * chips
    return call(
        functools.partial(basis_kernel, len(ranges)), (float_shape(lines * rows, k), float_shape(count, cells * width)),
        [SCALAR] + [WHOLE] * (len(ranges) + 4), (OUTSIDE, OUTSIDE),
        [
            pltpu.VMEM((lines, rows, k), jnp.float32), pltpu.VMEM((cells, count, width), jnp.float32), pltpu.VMEM((4, k, k), jnp.bfloat16),
            pltpu.SemaphoreType.DMA((lines,)), pltpu.SemaphoreType.DMA((cells,)),
        ],
        flops=18 * lines * rows * k * k, limit=24,
    )(spot, own, other, *ranges, co_own, co_other)


def finish_kernel(scale, spot_ref, own_ref, other_ref, middle_own_ref, middle_other_ref, out_ref, middle_ref):
    core, place = spot_ref[0], spot_ref[1]
    chips, extent = middle_own_ref.shape[0], middle_own_ref.shape[1]
    for i in range(chips):
        middle_ref[pl.ds(block_start(place, i, extent), extent), :] = middle_own_ref[i] + middle_other_ref[i]
    left = jnp.where(core == 0, own_ref[1], other_ref[1])
    right = jnp.where(core == 0, other_ref[1], own_ref[1])
    out_ref[...] = parts_dot(split(parts_dot(split(left), split(middle_ref[...]))), split(right), 1, 1) * scale


def finish(spot, own, other, middle_own, middle_other, scale):
    k = own.shape[1]
    return call(
        functools.partial(finish_kernel, scale), float_shape(k, k), [SCALAR] + [WHOLE] * 4, WHOLE,
        [pltpu.VMEM((k, k), jnp.float32)], flops=24 * k * k * k,
    )(spot, own, other, middle_own, middle_other)


def per_device(window, range_test, co_test, core_left, core_right):
    rows_total = window.shape[0] * lax.axis_size("cell")
    cols_total = window.shape[1] * lax.axis_size("tm")
    k = range_test.shape[1]
    chips = lax.axis_size("cell") // 2
    groups = groups_of("cell", 1, 2)
    lines = [("tm", (bit,)) for bit in range(bits_of("tm"))]
    cell, line = lax.axis_index("cell"), lax.axis_index("tm")
    spot = jnp.stack([cell & 1, place_of(groups, cell), place_of(lines[:2], line), place_of(lines, line)]).astype(jnp.int32)

    def core_swap(values):
        return swap(values, "cell", 1)

    r3, r2, r1, r0, sent, kept = sketch_terms(spot, chips, window, range_test, co_test, core_left, core_right)
    far = swap(r3, "tm", 1)
    near = swap(r2, "tm", 1)
    pack = kept + core_swap(sent)
    sketch_z = core_terms(after(spot, pack), window, core_right, core_left)
    handed = swap(r1 + after(far, pack), "tm", 2)
    pack = scatter_sum(pack, groups)[0]
    handed, near, pack, sketch_z = lax.optimization_barrier((handed, near, pack, sketch_z))
    range_piece = (r0 + near + handed).reshape(lax.axis_size("tm") // 4, -1, r0.shape[1])
    if lines[2:]:
        rest = place_of(lines[2:], line)
        range_piece = jnp.stack([lax.dynamic_index_in_dim(range_piece, rest ^ f, 0, False) for f in range(range_piece.shape[0])])
    range_piece = scatter_sum(range_piece, lines[2:])
    width = window.shape[1] // (2 * chips)
    packed = pack_width(co_test.shape[0], width, k)
    co_piece = pack[:packed].reshape(packed, -1, width).swapaxes(0, 1).reshape(-1, width)
    fold = pack[None, packed:]

    gram_sent, gram_kept = gram_terms(spot, chips, range_piece[0], co_piece, (rows_total, cols_total))
    fold = whole_sum(fold, "tm")
    gram = scatter_sum(gram_kept + core_swap(gram_sent), groups)
    co_parts = gather(after(co_piece[None], gram), groups)
    gram, co_parts = lax.optimization_barrier((whole_sum(gram, "tm"), co_parts))
    rows = gram.shape[1]
    parts = gather(jnp.concatenate([gram, fold], axis=1), groups)
    co_own = jnp.concatenate(co_parts)
    fold = jnp.concatenate([part[:, rows:] for part in parts])

    range_parts = gather(after(range_piece, gram, fold), lines[1:])
    range_near = swap(range_parts[0], "tm", 1)
    co_other, fold_other = core_swap(co_own), core_swap(fold)
    state = factor_start(spot, parts)
    state, fold_other = lax.optimization_barrier((state, fold_other))
    middle = middle_terms(spot, chips, sketch_z, fold, fold_other)
    middle = scatter_sum(middle, groups)
    state = factor_next((1, 2), *state)
    state, middle, range_parts, range_near = lax.optimization_barrier((state, middle, range_parts, range_near))
    for bit in range(bits_of("tm")):
        middle = middle + swap(middle, "tm", 1 << bit)
        if bit == 0:
            state = factor_next((2, state[1].shape[0] // BASE - 1), *state)
            state, middle, range_parts = lax.optimization_barrier((state, middle, range_parts))
    corners = [swap(part, "tm", 1) for part in range_parts[1:]]
    own = factor_end(*state)
    own, middle, corners = lax.optimization_barrier((own, middle, corners))
    range_all = range_parts + [range_near] + corners
    other = core_swap(own)
    range_basis, co_basis = bases(spot, own, other, range_all, co_own, co_other)
    middle, range_basis, co_basis = lax.optimization_barrier((gather(middle, groups), range_basis, co_basis))
    middle = jnp.concatenate(middle)
    core_out = finish(spot, own, other, middle, core_swap(middle), math.sqrt(rows_total * cols_total))
    return (range_basis, co_basis, core_out)


def solution(mesh):
    return jax.shard_map(
        per_device,
        mesh=mesh,
        in_specs=(P("cell", "tm"), P("tm", None), P(None, "cell"), P(None, "cell"), P(None, "tm")),
        out_specs=(P("cell", None), P(None, "tm"), P()),
        check_vma=False,
    )
```
